512 devices in a mesh: member: 16 (over y, z_hi), space: 32 (over z_lo, x, core).
Axes of the slice: x: 4, y: 8, z: 8 (z_hi: 2, z_lo: 4; z = z_hi * 4 + z_lo), core: 2. Of those that a mesh axis runs over, the one named last changes fastest.
Arguments:
- ensemble: float32 [16, 26, 131072], P('member', None, 'space'), may hold values from -3 to 3, as said below
- target: float32 [26, 131072], P(None, 'space'), may hold values from -3 to 3, as said below
- chan_weight: float32 [26], replicated, may hold values from 0.2 to 2
- lat_band: int32 [1024], P('space'), may hold values from 0 to 359, as said below
Outputs:
- loss: float32 [], replicated
- grad_scaled: float32 [16, 26, 131072], P('member', None, 'space')
The draws below stay inside these ranges and needn't reach their ends.
Inputs may be any that keep to these rules, and one draw needn't show every extreme that they name: `lat_band`: latitude row, counted from the south pole, of each block of 128 grid points; rows lie in the southern half. `ensemble`: multiples of 1/64. `target`: multiples of 1/64.
All inputs are finite; a program needn't handle non-finite values.
Results may differ from the reference program's by a relative error of at most 0.0003.
Values sent between devices are 32-bit elements; how exact they have to be, the bound alone decides.
A program may use at most 64 MiB of HBM per device.

```python
import math
import jax
import jax.numpy as jnp
from jax import lax

BLOCK = 128
BANDS = 720
CH = 26
MEMBERS = 16
NPOINTS = 131072
NBLK = 1024


def draw_lat_band(key, part):
    key = jax.random.fold_in(key, 1)
    first, second, third, fourth = jax.random.split(key, 4)
    blocks = jnp.arange(NBLK, dtype=jnp.int32)
    half = BANDS // 2
    pivot = jax.random.randint(first, (), NBLK // 4, 3 * NBLK // 4 + 1, dtype=jnp.int32)
    line = pivot * half // NBLK
    offset = jax.random.randint(second, (), 60, 121, dtype=jnp.int32)
    side = jax.random.randint(third, (), 0, 2, dtype=jnp.int32) * 2 - 1
    peak = jnp.clip(line + side * offset, 10, half - 11)
    lower = blocks * peak // pivot
    upper = peak + (blocks - pivot) * (half - 1 - peak) // (NBLK - 1 - pivot)
    band = jnp.where(blocks <= pivot, lower, upper)
    band = band + jax.random.randint(fourth, (NBLK,), 0, 4, dtype=jnp.int32)
    band = jnp.clip(band, 0, half - 1)
    band = jnp.where(blocks == NBLK - 1, half - 1, band)
    band = jnp.where(blocks == 0, 0, band)
    return band.astype(jnp.int32)


def base_field(key):
    shape = (CH, NPOINTS)
    first, second, third = jax.random.split(key, 3)
    whole = jax.random.randint(first, shape, -64, 65, dtype=jnp.int32)
    whole = whole + jax.random.randint(second, shape, -64, 65, dtype=jnp.int32)
    whole = whole + jax.random.randint(third, shape, -64, 65, dtype=jnp.int32)
    return whole


def draw_target(key, part):
    whole = base_field(key)
    return whole.astype(jnp.float32) / 64.0


def draw_ensemble(key, part):
    whole = base_field(key)
    key = jax.random.fold_in(key, 2)
    first, second, third = jax.random.split(key, 3)
    raw = jax.random.randint(first, (MEMBERS, CH, NPOINTS), -128, 129, dtype=jnp.int32)
    steps = jnp.arange(MEMBERS, dtype=jnp.int32)
    member_amp = 16 + steps * 48 // max(MEMBERS - 1, 1)
    member_amp = member_amp + jax.random.randint(second, (MEMBERS,), 0, 9, dtype=jnp.int32)
    block_amp = jax.random.randint(third, (NPOINTS // BLOCK,), 8, 65, dtype=jnp.int32)
    point_amp = jnp.repeat(block_amp, BLOCK)
    spread = raw * member_amp[:, None, None] * point_amp[None, None, :] // 4096
    members = whole[None] + spread
    members = jnp.clip(members, -192, 192)
    return members.astype(jnp.float32) / 64.0


def setup_inputs(seed: int = 0) -> dict:
    arg_keys = jax.random.split(jax.random.key(seed), 5)
    ensemble = draw_ensemble(jax.random.fold_in(arg_keys[4], 71), 0)
    target = draw_target(jax.random.fold_in(arg_keys[4], 71), 0)
    chan_weight = jnp.clip(jnp.exp(jax.random.uniform(arg_keys[2], (CH,), jnp.float32, math.log(0.2), math.log(2.0))), 0.2, 2.0)
    lat_band = draw_lat_band(jax.random.fold_in(arg_keys[4], 71), 0)
    return {"ensemble": ensemble, "target": target, "chan_weight": chan_weight, "lat_band": lat_band}


def reference(ensemble, target, chan_weight, lat_band):
    latitude = ((lat_band.astype(jnp.float32) + 0.5) / BANDS - 0.5) * math.pi
    area = jnp.repeat(jnp.cos(latitude), BLOCK)
    area_total = jnp.sum(area)

    def add_pair(carry, other):
        spread, signs = carry
        diff = ensemble - other[None]
        return (spread + jnp.abs(diff), signs + jnp.sign(diff)), None

    zeros = jnp.zeros_like(ensemble)
    (spread_sum, sign_sum), unused = lax.scan(add_pair, (zeros, zeros), ensemble)
    count = float(MEMBERS)
    skill = ensemble - target[None]
    score = jnp.sum(jnp.abs(skill) / count - spread_sum / (2.0 * count * (count - 1.0)), axis=0)
    weights = area[None, :] * chan_weight[:, None]
    loss = jnp.sum(weights * score) / (area_total * CH)
    scale = NPOINTS * weights / area_total
    grad_scaled = scale[None] * (jnp.sign(skill) / count - sign_sum / (count * (count - 1.0)))
    return loss, grad_scaled
```

```python
import math

import jax
import jax.numpy as jnp
from jax import lax
from jax.experimental import pallas as pl
from jax.experimental.pallas import tpu as pltpu
from jax.sharding import PartitionSpec as P

BLOCK = 128
BANDS = 720
MESH = pl.DeviceIdType.MESH
ROWS = 4
NEAR = 8
PLANES = 2
CHUNKS = ((0, 6), (6, 7))


def kernel(
    members,
    spaces,
    ens,
    tgt,
    cw_hbm,
    lat_hbm,
    grad,
    loss,
    cw,
    lat,
    own,
    tgt_rows,
    sgn,
    scl,
    gat,
    sums,
    back,
    area,
    met_area,
    box_row,
    box_a1,
    box_a2,
    box_l1,
    box_l2,
    box_l3,
    local_sem,
    row_sem,
    send1,
    recv1,
    send2,
    recv2,
    send_a1,
    recv_a1,
    send_a2,
    recv_a2,
    send_l1,
    recv_l1,
    send_l2,
    recv_l2,
    send_l3,
    recv_l3,
):
    m = lax.axis_index("member")
    s = lax.axis_index("space")
    far = spaces // NEAR
    ny = members // PLANES
    nz = far * PLANES
    near_at = lax.rem(s, NEAR)
    far_at = lax.div(s, NEAR)
    y = lax.div(m, PLANES)
    z = lax.rem(m, PLANES) * far + far_at
    units = ens.shape[0]
    per = units // members
    channels = tgt.shape[0]
    groups = units // channels
    blocks = groups * ROWS

    def member_of(yy, zz):
        return lax.rem(yy + ny, ny) * PLANES + lax.div(lax.rem(zz + nz, nz), far)

    def place(yy, zz):
        return (member_of(yy, zz), lax.rem(lax.rem(zz + nz, nz), far) * NEAR + near_at)

    def near_peer(k):
        return (m, s - near_at + lax.rem(near_at + k, NEAR))

    def far_peer(k):
        return (m, lax.rem(far_at + k, far) * NEAR + near_at)

    def z_peer(k):
        return place(y, z + k)

    def y_peer(k):
        return place(y + k, z)

    own_copy = pltpu.make_async_copy(ens, own, local_sem.at[0])
    tgt_copy = pltpu.make_async_copy(tgt, tgt_rows, local_sem.at[1])
    cw_copy = pltpu.make_async_copy(cw_hbm, cw, local_sem.at[2])
    lat_copy = pltpu.make_async_copy(lat_hbm, lat, local_sem.at[3])
    lat_copy.start()
    cw_copy.start()
    own_copy.start()
    tgt_copy.start()

    quarter = nz // 4

    def met(n):
        step = lax.div(lax.div(n, 2) + 1, 2)
        dy = ny // 2 + step * (2 * lax.rem(lax.div(n, 2), 2) - 1)
        return place(y + dy, z + quarter * (1 - 2 * lax.rem(n, 2)))

    barrier = pltpu.get_barrier_semaphore()

    def greet(peer):
        pl.semaphore_signal(barrier, inc=1, device_id=peer, device_id_type=MESH)

    def greet_all(peer, start, count):
        def one(k, carry):
            greet(peer(k))
            return carry

        lax.fori_loop(start, count, one, 0)

    greet_all(met, 0, members)
    greet_all(near_peer, 1, NEAR)
    greet_all(z_peer, 1, nz)
    greet_all(y_peer, 1, ny)
    pl.semaphore_wait(barrier, members + (NEAR - 1) + (nz - 1) + (ny - 1))

    def push(src, dst, send, recv, device):
        pltpu.make_async_remote_copy(
            src_ref=src,
            dst_ref=dst,
            send_sem=send,
            recv_sem=recv,
            device_id=device,
            device_id_type=MESH,
        ).start()

    def exchange(source, landing, send, recv, chunk):
        def one(n, carry):
            device = met(n)
            j = device[0]
            push(source(j), landing(m), send.at[chunk, j], recv.at[chunk, m], device)
            return carry

        lax.fori_loop(0, members, one, 0)

    def arrived(ref, sem):
        pltpu.make_async_copy(ref, ref, sem).wait()

    def share(box, at, send, recv, peer, count):
        def one(k, carry):
            push(box.at[at], box.at[at], send.at[k], recv.at[at], peer(k))
            return carry

        lax.fori_loop(1, count, one, 0)

    def collect(box, at, send, recv, count):
        def one(k, carry):
            j = lax.rem(at + k, count)
            pltpu.make_async_copy(box.at[j], box.at[j], recv.at[j]).wait()
            pltpu.make_async_copy(box.at[at], box.at[at], send.at[k]).wait()
            return carry

        lax.fori_loop(1, count, one, 0)
        total = box[0]
        for j in range(1, count):
            total = total + box[j]
        return total

    for chunk, (first, size) in enumerate(CHUNKS):
        exchange(
            lambda j: ens.at[pl.ds(j * per + first, size)],
            lambda i: gat.at[i, pl.ds(first, size)],
            send1,
            recv1,
            chunk,
        )

    def along_rows(row):
        square = jnp.broadcast_to(row, (blocks, blocks))
        diagonal = lax.broadcasted_iota(jnp.int32, (blocks, blocks), 0) == lax.broadcasted_iota(
            jnp.int32, (blocks, blocks), 1
        )
        column = jnp.sum(jnp.where(diagonal, square, 0.0), axis=1, keepdims=True)
        return jnp.broadcast_to(column, (blocks, BLOCK))

    lat_copy.wait()
    latitude = ((lat[...].astype(jnp.float32) + 0.5) / BANDS - 0.5) * math.pi
    block_area = jnp.cos(latitude)
    box_row[0] = block_area
    push(box_row.at[0], box_row.at[1], row_sem.at[0], row_sem.at[1], place(y, z + quarter))
    wide = along_rows(block_area)
    for g in range(groups):
        area[g] = wide[g * ROWS : (g + 1) * ROWS]
    box_a1[near_at] = jnp.sum(wide, axis=0, keepdims=True)
    share(box_a1, near_at, send_a1, recv_a1, near_peer, NEAR)

    cw_copy.wait()
    own_copy.wait()
    tgt_copy.wait()

    def skill_rows(first, rows, acc):
        for g in range(groups):
            tiles = [
                tgt_rows[pl.ds(first, rows), pl.ds((g * ROWS + i) * BLOCK, BLOCK)] for i in range(ROWS)
            ]
            part = jnp.zeros((ROWS, BLOCK), jnp.float32)
            for r in range(rows):
                u = (first + r) * groups + g
                skill = own[u] - jnp.concatenate([tile[r : r + 1] for tile in tiles], axis=0)
                sgn[u] = jnp.clip(skill * 64.0, -1.0, 1.0) * 0.0625
                part = part + cw[first + r] * jnp.abs(skill)
            acc = acc + area[g] * part
        return acc

    def skill_octet(k, acc):
        return skill_rows(pl.multiple_of(k * 8, 8), 8, acc)

    octets = channels // 8
    skill_sum = lax.fori_loop(0, octets, skill_octet, jnp.zeros((ROWS, BLOCK), jnp.float32))
    if channels % 8:
        skill_sum = skill_rows(octets * 8, channels % 8, skill_sum)

    arrived(box_row.at[1], row_sem.at[1])
    met_wide = along_rows(box_row[1])
    for g in range(groups):
        met_area[g] = met_wide[g * ROWS : (g + 1) * ROWS]
    count = float(members)

    def pairs(places, acc):
        values = [
            jnp.concatenate([gat[j, i] for i in places], axis=0) * 64.0 for j in range(members)
        ]
        signs = [jnp.zeros_like(values[0]) for j in range(members)]
        for a in range(members):
            for b in range(a + 1, members):
                d = jnp.clip(values[a] - values[b], -1.0, 1.0)
                signs[a] = signs[a] + d
                signs[b] = signs[b] - d
        dot = values[0] * signs[0]
        for j in range(1, members):
            dot = dot + values[j] * signs[j]
        for n, i in enumerate(places):
            part = slice(n * ROWS, (n + 1) * ROWS)
            for j in range(members):
                sums[j, i] = signs[j][part]
            u = m * per + i
            acc = acc + (met_area[lax.rem(u, groups)] * cw[lax.div(u, groups)]) * dot[part]
        return acc

    spread_sum = jnp.zeros((ROWS, BLOCK), jnp.float32)
    for chunk, (first, size) in enumerate(CHUNKS):

        def wait_chunk(j, carry):
            arrived(gat.at[j, pl.ds(first, size)], recv1.at[chunk, j])
            return carry

        lax.fori_loop(0, members, wait_chunk, 0)
        spread_sum = lax.fori_loop(
            0,
            size // 2,
            lambda k, acc: pairs((first + 2 * k, first + 2 * k + 1), acc),
            spread_sum,
        )
        if size % 2:
            spread_sum = pairs((first + size - 1,), spread_sum)
        if first + size == per:
            mine = skill_sum * (1.0 / count) - spread_sum * (1.0 / (64.0 * count * (count - 1.0)))
            box_l1[near_at] = jnp.sum(mine, axis=0, keepdims=True)
            share(box_l1, near_at, send_l1, recv_l1, near_peer, NEAR)
        exchange(
            lambda j: sums.at[j, pl.ds(first, size)],
            lambda i: back.at[pl.ds(i * per + first, size)],
            send2,
            recv2,
            chunk,
        )

    area_near = collect(box_a1, near_at, send_a1, recv_a1, NEAR)
    box_a2[far_at] = area_near
    share(box_a2, far_at, send_a2, recv_a2, far_peer, far)
    loss_near = collect(box_l1, near_at, send_l1, recv_l1, NEAR)
    box_l2[z] = loss_near
    share(box_l2, z, send_l2, recv_l2, z_peer, nz)

    area_all = collect(box_a2, far_at, send_a2, recv_a2, far)
    area_total = jnp.sum(area_all, axis=1, keepdims=True)
    points = float(units * ROWS * BLOCK // channels * spaces)
    factor = jnp.broadcast_to(points / area_total, (ROWS, BLOCK))

    def scale_channel(c, carry):
        weight = cw[c]
        for g in range(groups):
            u = c * groups + g
            scale = area[g] * factor * weight
            sgn[u] = sgn[u] * scale
            scl[u] = scale * (1.0 / (count * (count - 1.0)))
        return carry

    lax.fori_loop(0, channels, scale_channel, 0)

    def finish(j, source, first, size):
        part = pl.ds(j * per + first, size)
        grad[part] = sgn[part] - scl[part] * source

    loss_z = collect(box_l2, z, send_l2, recv_l2, nz)
    box_l3[y] = loss_z
    share(box_l3, y, send_l3, recv_l3, y_peer, ny)

    for chunk, (first, size) in enumerate(CHUNKS):

        def take_back(n, carry):
            j = met(n)[0]
            part = back.at[pl.ds(j * per + first, size)]
            arrived(part, recv2.at[chunk, j])
            finish(j, part[...], first, size)
            return carry

        lax.fori_loop(0, members, take_back, 0)

    loss_all = collect(box_l3, y, send_l3, recv_l3, ny)
    loss_total = jnp.sum(loss_all, axis=1, keepdims=True)
    loss[...] = loss_total / (area_total * float(channels))

    for chunk, (first, size) in enumerate(CHUNKS):

        def wait_sent(j, carry):
            arrived(gat.at[j, pl.ds(first, size)], send1.at[chunk, j])
            arrived(sums.at[j, pl.ds(first, size)], send2.at[chunk, j])
            return carry

        lax.fori_loop(0, members, wait_sent, 0)
    arrived(box_row.at[0], row_sem.at[0])


def local(members, spaces, ensemble, target, chan_weight, lat_band):
    channels, points = target.shape
    units = channels * points // (ROWS * BLOCK)
    per = units // members
    far = spaces // NEAR
    ny = members // PLANES
    nz = far * PLANES
    f32 = jnp.float32
    dma = pltpu.SemaphoreType.DMA
    vmem = pl.BlockSpec(memory_space=pltpu.VMEM)
    hbm = pl.BlockSpec(memory_space=pltpu.HBM)
    whole = pltpu.VMEM((units, ROWS, BLOCK), f32)
    slabs = pltpu.VMEM((members, per, ROWS, BLOCK), f32)

    def box(n):
        return pltpu.VMEM((n, 1, BLOCK), f32)

    def in_hbm(x):
        return pltpu.with_memory_space_constraint(x, pltpu.HBM)

    def body(*refs):
        kernel(members, spaces, *refs)

    grad, loss = pl.pallas_call(
        body,
        out_shape=(
            jax.ShapeDtypeStruct((units, ROWS, BLOCK), f32),
            jax.ShapeDtypeStruct((1, 1), f32),
        ),
        in_specs=[hbm] * 4,
        out_specs=(vmem, vmem),
        scratch_shapes=[
            pltpu.SMEM(chan_weight.shape, f32),
            pltpu.VMEM((1, lat_band.shape[0]), lat_band.dtype),
            whole,
            pltpu.VMEM((channels, points), f32),
            whole,
            whole,
            slabs,
            slabs,
            whole,
            pltpu.VMEM((points // (ROWS * BLOCK), ROWS, BLOCK), f32),
            pltpu.VMEM((points // (ROWS * BLOCK), ROWS, BLOCK), f32),
            pltpu.VMEM((2, 1, lat_band.shape[0]), f32),
            box(NEAR),
            box(far),
            box(NEAR),
            box(nz),
            box(ny),
            dma((4,)),
            dma((2,)),
            dma((len(CHUNKS), members)),
            dma((len(CHUNKS), members)),
            dma((len(CHUNKS), members)),
            dma((len(CHUNKS), members)),
            dma((NEAR,)),
            dma((NEAR,)),
            dma((far,)),
            dma((far,)),
            dma((NEAR,)),
            dma((NEAR,)),
            dma((nz,)),
            dma((nz,)),
            dma((ny,)),
            dma((ny,)),
        ],
        compiler_params=pltpu.CompilerParams(
            collective_id=0, has_side_effects=True, vmem_limit_bytes=32 * 1024 * 1024
        ),
    )(
        in_hbm(ensemble.reshape(units, ROWS, BLOCK)),
        in_hbm(target),
        in_hbm(chan_weight),
        in_hbm(lat_band.reshape(1, -1)),
    )
    return loss.reshape(()), grad.reshape(1, channels, points)


def solution(mesh):
    members, spaces = mesh.shape["member"], mesh.shape["space"]

    def step(*args):
        return local(members, spaces, *args)

    in_specs = (P("member", None, "space"), P(None, "space"), P(), P("space"))
    out_specs = (P(), P("member", None, "space"))
    return jax.shard_map(step, mesh=mesh, in_specs=in_specs, out_specs=out_specs, check_vma=False)
```

```python
import math

import jax
import jax.numpy as jnp
from jax import lax
from jax.experimental import pallas as pl
from jax.experimental.pallas import tpu as pltpu
from jax.sharding import PartitionSpec as P

BLOCK = 128
BANDS = 720
MESH = pl.DeviceIdType.MESH
ROWS = 4
NEAR = 8
PLANES = 2
CHUNKS = ((0, 6), (6, 7))


def kernel(
    members,
    spaces,
    ens,
    tgt,
    cw_hbm,
    lat_hbm,
    grad,
    loss,
    cw,
    lat,
    own,
    tgt_rows,
    sgn,
    scl,
    gat,
    sums,
    back,
    relay1,
    relay2,
    area,
    met_area,
    box_row,
    box_a1,
    box_a2,
    box_l1,
    box_l2,
    box_l3,
    local_sem,
    row_sem,
    send1,
    recv1,
    hop1,
    fwd1,
    send2,
    recv2,
    hop2,
    fwd2,
    send_a1,
    recv_a1,
    send_a2,
    recv_a2,
    send_l1,
    recv_l1,
    send_l2,
    recv_l2,
    send_l3,
    recv_l3,
):
    m = lax.axis_index("member")
    s = lax.axis_index("space")
    far = spaces // NEAR
    ny = members // PLANES
    nz = far * PLANES
    near_at = lax.rem(s, NEAR)
    far_at = lax.div(s, NEAR)
    y = lax.div(m, PLANES)
    z = lax.rem(m, PLANES) * far + far_at
    units = ens.shape[0]
    per = units // members
    channels = tgt.shape[0]
    groups = units // channels
    blocks = groups * ROWS

    def member_of(yy, zz):
        return lax.rem(yy + ny, ny) * PLANES + lax.div(lax.rem(zz + nz, nz), far)

    def place(yy, zz):
        return (member_of(yy, zz), lax.rem(lax.rem(zz + nz, nz), far) * NEAR + near_at)

    def near_peer(k):
        return (m, s - near_at + lax.rem(near_at + k, NEAR))

    def far_peer(k):
        return (m, lax.rem(far_at + k, far) * NEAR + near_at)

    def z_peer(k):
        return place(y, z + k)

    def y_peer(k):
        return place(y + k, z)

    own_copy = pltpu.make_async_copy(ens, own, local_sem.at[0])
    tgt_copy = pltpu.make_async_copy(tgt, tgt_rows, local_sem.at[1])
    cw_copy = pltpu.make_async_copy(cw_hbm, cw, local_sem.at[2])
    lat_copy = pltpu.make_async_copy(lat_hbm, lat, local_sem.at[3])
    lat_copy.start()
    cw_copy.start()
    own_copy.start()
    tgt_copy.start()

    quarter = nz // 4

    def met(n):
        step = lax.div(lax.div(n, 2) + 1, 2)
        dy = ny // 2 + step * (2 * lax.rem(lax.div(n, 2), 2) - 1)
        return place(y + dy, z + quarter * (1 - 2 * lax.rem(n, 2)))

    barrier = pltpu.get_barrier_semaphore()

    def greet(peer):
        pl.semaphore_signal(barrier, inc=1, device_id=peer, device_id_type=MESH)

    def greet_all(peer, start, count):
        def one(k, carry):
            greet(peer(k))
            return carry

        lax.fori_loop(start, count, one, 0)

    greet_all(met, 0, members)
    greet_all(near_peer, 1, NEAR)
    greet_all(z_peer, 1, nz)
    greet_all(y_peer, 1, ny)
    pl.semaphore_wait(barrier, members + (NEAR - 1) + (nz - 1) + (ny - 1))

    def push(src, dst, send, recv, device):
        pltpu.make_async_remote_copy(
            src_ref=src,
            dst_ref=dst,
            send_sem=send,
            recv_sem=recv,
            device_id=device,
            device_id_type=MESH,
        ).start()

    twin = y + 1 - 2 * lax.rem(y, 2)
    sides = (quarter, -quarter)

    def exchange(source, landing, relay, send, recv, hop, chunk):
        for side, dz in enumerate(sides):
            j = member_of(y + ny // 2, z + dz)
            push(source(j), relay.at[side], send.at[chunk, j], hop.at[chunk, side], place(twin, z + dz))

        def one(n, carry):
            device = met(n)
            j = device[0]
            push(source(j), landing(m), send.at[chunk, j], recv.at[chunk, m], device)
            return carry

        lax.fori_loop(PLANES, members, one, 0)

    def forward(landing, relay, fwd, recv, hop, chunk):
        for side, dz in enumerate(sides):
            i = member_of(twin, z - dz)
            arrived(relay.at[side], hop.at[chunk, side])
            push(relay.at[side], landing(i), fwd.at[chunk, side], recv.at[chunk, i], place(twin + ny // 2, z))

    def arrived(ref, sem):
        pltpu.make_async_copy(ref, ref, sem).wait()

    def share(box, at, send, recv, peer, count):
        def one(k, carry):
            push(box.at[at], box.at[at], send.at[k], recv.at[at], peer(k))
            return carry

        lax.fori_loop(1, count, one, 0)

    def collect(box, at, send, recv, count):
        def one(k, carry):
            j = lax.rem(at + k, count)
            pltpu.make_async_copy(box.at[j], box.at[j], recv.at[j]).wait()
            pltpu.make_async_copy(box.at[at], box.at[at], send.at[k]).wait()
            return carry

        lax.fori_loop(1, count, one, 0)
        total = box[0]
        for j in range(1, count):
            total = total + box[j]
        return total

    def gather(chunk):
        first, size = CHUNKS[chunk]
        part = pl.ds(first, size)
        landing = lambda i: gat.at[i, part]
        return landing, relay1.at[:, part]

    def scatter(chunk):
        first, size = CHUNKS[chunk]
        landing = lambda i: back.at[pl.ds(i * per + first, size)]
        return landing, relay2.at[:, pl.ds(first, size)]

    for chunk, (first, size) in enumerate(CHUNKS):
        landing, relay = gather(chunk)
        exchange(
            lambda j: ens.at[pl.ds(j * per + first, size)], landing, relay, send1, recv1, hop1, chunk
        )

    def along_rows(row):
        square = jnp.broadcast_to(row, (blocks, blocks))
        diagonal = lax.broadcasted_iota(jnp.int32, (blocks, blocks), 0) == lax.broadcasted_iota(
            jnp.int32, (blocks, blocks), 1
        )
        column = jnp.sum(jnp.where(diagonal, square, 0.0), axis=1, keepdims=True)
        return jnp.broadcast_to(column, (blocks, BLOCK))

    lat_copy.wait()
    latitude = ((lat[...].astype(jnp.float32) + 0.5) / BANDS - 0.5) * math.pi
    block_area = jnp.cos(latitude)
    box_row[0] = block_area
    push(box_row.at[0], box_row.at[1], row_sem.at[0], row_sem.at[1], place(y, z + quarter))
    wide = along_rows(block_area)
    for g in range(groups):
        area[g] = wide[g * ROWS : (g + 1) * ROWS]
    box_a1[near_at] = jnp.sum(wide, axis=0, keepdims=True)
    share(box_a1, near_at, send_a1, recv_a1, near_peer, NEAR)

    landing, relay = gather(0)
    forward(landing, relay, fwd1, recv1, hop1, 0)

    cw_copy.wait()
    own_copy.wait()
    tgt_copy.wait()

    def skill_rows(first, rows, acc):
        for g in range(groups):
            tiles = [
                tgt_rows[pl.ds(first, rows), pl.ds((g * ROWS + i) * BLOCK, BLOCK)] for i in range(ROWS)
            ]
            part = jnp.zeros((ROWS, BLOCK), jnp.float32)
            for r in range(rows):
                u = (first + r) * groups + g
                skill = own[u] - jnp.concatenate([tile[r : r + 1] for tile in tiles], axis=0)
                sgn[u] = jnp.clip(skill * 64.0, -1.0, 1.0) * 0.0625
                part = part + cw[first + r] * jnp.abs(skill)
            acc = acc + area[g] * part
        return acc

    def skill_octet(k, acc):
        return skill_rows(pl.multiple_of(k * 8, 8), 8, acc)

    octets = channels // 8
    skill_sum = lax.fori_loop(0, octets, skill_octet, jnp.zeros((ROWS, BLOCK), jnp.float32))
    if channels % 8:
        skill_sum = skill_rows(octets * 8, channels % 8, skill_sum)

    for chunk in range(1, len(CHUNKS)):
        landing, relay = gather(chunk)
        forward(landing, relay, fwd1, recv1, hop1, chunk)

    arrived(box_row.at[1], row_sem.at[1])
    met_wide = along_rows(box_row[1])
    for g in range(groups):
        met_area[g] = met_wide[g * ROWS : (g + 1) * ROWS]
    count = float(members)

    def pairs(places, acc):
        values = [
            jnp.concatenate([gat[j, i] for i in places], axis=0) * 64.0 for j in range(members)
        ]
        signs = [jnp.zeros_like(values[0]) for j in range(members)]
        for a in range(members):
            for b in range(a + 1, members):
                d = jnp.clip(values[a] - values[b], -1.0, 1.0)
                signs[a] = signs[a] + d
                signs[b] = signs[b] - d
        dot = values[0] * signs[0]
        for j in range(1, members):
            dot = dot + values[j] * signs[j]
        for n, i in enumerate(places):
            part = slice(n * ROWS, (n + 1) * ROWS)
            for j in range(members):
                sums[j, i] = signs[j][part]
            u = m * per + i
            acc = acc + (met_area[lax.rem(u, groups)] * cw[lax.div(u, groups)]) * dot[part]
        return acc

    spread_sum = jnp.zeros((ROWS, BLOCK), jnp.float32)
    for chunk, (first, size) in enumerate(CHUNKS):

        def wait_chunk(j, carry):
            arrived(gat.at[j, pl.ds(first, size)], recv1.at[chunk, j])
            return carry

        lax.fori_loop(0, members, wait_chunk, 0)
        spread_sum = lax.fori_loop(
            0,
            size // 2,
            lambda k, acc: pairs((first + 2 * k, first + 2 * k + 1), acc),
            spread_sum,
        )
        if size % 2:
            spread_sum = pairs((first + size - 1,), spread_sum)
        if first + size == per:
            mine = skill_sum * (1.0 / count) - spread_sum * (1.0 / (64.0 * count * (count - 1.0)))
            box_l1[near_at] = jnp.sum(mine, axis=0, keepdims=True)
            share(box_l1, near_at, send_l1, recv_l1, near_peer, NEAR)
        landing, relay = scatter(chunk)
        exchange(lambda j: sums.at[j, pl.ds(first, size)], landing, relay, send2, recv2, hop2, chunk)
    for chunk in range(len(CHUNKS)):
        landing, relay = scatter(chunk)
        forward(landing, relay, fwd2, recv2, hop2, chunk)

    area_near = collect(box_a1, near_at, send_a1, recv_a1, NEAR)
    box_a2[far_at] = area_near
    share(box_a2, far_at, send_a2, recv_a2, far_peer, far)
    loss_near = collect(box_l1, near_at, send_l1, recv_l1, NEAR)
    box_l2[z] = loss_near
    share(box_l2, z, send_l2, recv_l2, z_peer, nz)

    area_all = collect(box_a2, far_at, send_a2, recv_a2, far)
    area_total = jnp.sum(area_all, axis=1, keepdims=True)
    points = float(units * ROWS * BLOCK // channels * spaces)
    factor = jnp.broadcast_to(points / area_total, (ROWS, BLOCK))

    def scale_channel(c, carry):
        weight = cw[c]
        for g in range(groups):
            u = c * groups + g
            scale = area[g] * factor * weight
            sgn[u] = sgn[u] * scale
            scl[u] = scale * (1.0 / (count * (count - 1.0)))
        return carry

    lax.fori_loop(0, channels, scale_channel, 0)

    def finish(j, source, first, size):
        part = pl.ds(j * per + first, size)
        grad[part] = sgn[part] - scl[part] * source

    loss_z = collect(box_l2, z, send_l2, recv_l2, nz)
    box_l3[y] = loss_z
    share(box_l3, y, send_l3, recv_l3, y_peer, ny)

    for chunk, (first, size) in enumerate(CHUNKS):

        def take_back(n, carry):
            j = met(n)[0]
            part = back.at[pl.ds(j * per + first, size)]
            arrived(part, recv2.at[chunk, j])
            finish(j, part[...], first, size)
            return carry

        lax.fori_loop(0, members, take_back, 0)

    loss_all = collect(box_l3, y, send_l3, recv_l3, ny)
    loss_total = jnp.sum(loss_all, axis=1, keepdims=True)
    loss[...] = loss_total / (area_total * float(channels))

    for chunk, (first, size) in enumerate(CHUNKS):

        def wait_sent(j, carry):
            arrived(gat.at[j, pl.ds(first, size)], send1.at[chunk, j])
            arrived(sums.at[j, pl.ds(first, size)], send2.at[chunk, j])
            return carry

        lax.fori_loop(0, members, wait_sent, 0)
        for side in range(len(sides)):
            arrived(relay1.at[side, pl.ds(first, size)], fwd1.at[chunk, side])
            arrived(relay2.at[side, pl.ds(first, size)], fwd2.at[chunk, side])
    arrived(box_row.at[0], row_sem.at[0])


def local(members, spaces, ensemble, target, chan_weight, lat_band):
    channels, points = target.shape
    units = channels * points // (ROWS * BLOCK)
    per = units // members
    far = spaces // NEAR
    ny = members // PLANES
    nz = far * PLANES
    f32 = jnp.float32
    dma = pltpu.SemaphoreType.DMA
    vmem = pl.BlockSpec(memory_space=pltpu.VMEM)
    hbm = pl.BlockSpec(memory_space=pltpu.HBM)
    whole = pltpu.VMEM((units, ROWS, BLOCK), f32)
    relay = pltpu.VMEM((PLANES, per, ROWS, BLOCK), f32)
    slabs = pltpu.VMEM((members, per, ROWS, BLOCK), f32)

    def box(n):
        return pltpu.VMEM((n, 1, BLOCK), f32)

    def in_hbm(x):
        return pltpu.with_memory_space_constraint(x, pltpu.HBM)

    def body(*refs):
        kernel(members, spaces, *refs)

    grad, loss = pl.pallas_call(
        body,
        out_shape=(
            jax.ShapeDtypeStruct((units, ROWS, BLOCK), f32),
            jax.ShapeDtypeStruct((1, 1), f32),
        ),
        in_specs=[hbm] * 4,
        out_specs=(vmem, vmem),
        scratch_shapes=[
            pltpu.SMEM(chan_weight.shape, f32),
            pltpu.VMEM((1, lat_band.shape[0]), lat_band.dtype),
            whole,
            pltpu.VMEM((channels, points), f32),
            whole,
            whole,
            slabs,
            slabs,
            whole,
            relay,
            relay,
            pltpu.VMEM((points // (ROWS * BLOCK), ROWS, BLOCK), f32),
            pltpu.VMEM((points // (ROWS * BLOCK), ROWS, BLOCK), f32),
            pltpu.VMEM((2, 1, lat_band.shape[0]), f32),
            box(NEAR),
            box(far),
            box(NEAR),
            box(nz),
            box(ny),
            dma((4,)),
            dma((2,)),
            dma((len(CHUNKS), members)),
            dma((len(CHUNKS), members)),
            dma((len(CHUNKS), PLANES)),
            dma((len(CHUNKS), PLANES)),
            dma((len(CHUNKS), members)),
            dma((len(CHUNKS), members)),
            dma((len(CHUNKS), PLANES)),
            dma((len(CHUNKS), PLANES)),
            dma((NEAR,)),
            dma((NEAR,)),
            dma((far,)),
            dma((far,)),
            dma((NEAR,)),
            dma((NEAR,)),
            dma((nz,)),
            dma((nz,)),
            dma((ny,)),
            dma((ny,)),
        ],
        compiler_params=pltpu.CompilerParams(
            collective_id=0, has_side_effects=True, vmem_limit_bytes=32 * 1024 * 1024
        ),
    )(
        in_hbm(ensemble.reshape(units, ROWS, BLOCK)),
        in_hbm(target),
        in_hbm(chan_weight),
        in_hbm(lat_band.reshape(1, -1)),
    )
    return loss.reshape(()), grad.reshape(1, channels, points)


def solution(mesh):
    members, spaces = mesh.shape["member"], mesh.shape["space"]

    def step(*args):
        return local(members, spaces, *args)

    in_specs = (P("member", None, "space"), P(None, "space"), P(), P("space"))
    out_specs = (P(), P("member", None, "space"))
    return jax.shard_map(step, mesh=mesh, in_specs=in_specs, out_specs=out_specs, check_vma=False)
```

```python
import math

import jax
import jax.numpy as jnp
from jax import lax
from jax.experimental import pallas as pl
from jax.experimental.pallas import tpu as pltpu
from jax.sharding import PartitionSpec as P

BLOCK = 128
BANDS = 720
MESH = pl.DeviceIdType.MESH
ROWS = 4
NEAR = 8
PLANES = 2
CHUNKS = ((0, 6), (6, 7))


def kernel(
    members,
    spaces,
    ens,
    tgt,
    cw_hbm,
    lat_hbm,
    grad,
    loss,
    cw,
    lat,
    own,
    tgt_rows,
    sgn,
    scl,
    gat,
    sums,
    back,
    area,
    met_area,
    box_row,
    box_a1,
    box_a2,
    box_l1,
    box_near,
    box_l2,
    box_l3,
    local_sem,
    row_sem,
    send1,
    recv1,
    send2,
    recv2,
    send_a1,
    recv_a1,
    send_a2,
    recv_a2,
    send_l1,
    recv_l1,
    send_l2,
    recv_l2,
    send_l3,
    recv_l3,
):
    m = lax.axis_index("member")
    s = lax.axis_index("space")
    far = spaces // NEAR
    ny = members // PLANES
    nz = far * PLANES
    near_at = lax.rem(s, NEAR)
    far_at = lax.div(s, NEAR)
    y = lax.div(m, PLANES)
    z = lax.rem(m, PLANES) * far + far_at
    units = ens.shape[0]
    per = units // members
    channels = tgt.shape[0]
    groups = units // channels
    blocks = groups * ROWS

    y_at = [lax.rem(y + k, ny) for k in range(ny)]
    z_at = [lax.rem(z + k, nz) for k in range(nz)]

    def place(dy, dz):
        zz = z_at[dz % nz]
        return (y_at[dy % ny] * PLANES + lax.div(zz, far), lax.rem(zz, far) * NEAR + near_at)

    near_base = s - near_at
    near_peers = [(m, near_base + lax.rem(near_at + k, NEAR)) for k in range(1, NEAR)]
    far_peers = [(m, lax.rem(far_at + k, far) * NEAR + near_at) for k in range(1, far)]
    z_peers = [place(0, k) for k in range(1, nz)]

    own_copy = pltpu.make_async_copy(ens, own, local_sem.at[0])
    tgt_copy = pltpu.make_async_copy(tgt, tgt_rows, local_sem.at[1])
    cw_copy = pltpu.make_async_copy(cw_hbm, cw, local_sem.at[2])
    lat_copy = pltpu.make_async_copy(lat_hbm, lat, local_sem.at[3])
    lat_copy.start()
    cw_copy.start()
    own_copy.start()
    tgt_copy.start()

    quarter = nz // 4
    steps = sorted(range(ny), key=lambda k: -min(k, ny - k))
    met = [place(dy, dz) for dy in steps for dz in (quarter, -quarter)]
    upper = [place(dy, quarter) for dy in range(ny)]

    barrier = pltpu.get_barrier_semaphore()
    fresh = [k for k in range(1, nz) if k not in (quarter, nz - quarter)]
    greeted = met + near_peers + [place(0, k) for k in fresh]
    for peer in greeted:
        pl.semaphore_signal(barrier, inc=1, device_id=peer, device_id_type=MESH)
    pl.semaphore_wait(barrier, len(greeted))

    def push(src, dst, send, recv, device):
        pltpu.make_async_remote_copy(
            src_ref=src,
            dst_ref=dst,
            send_sem=send,
            recv_sem=recv,
            device_id=device,
            device_id_type=MESH,
        ).start()

    def exchange(source, landing, send, recv, chunk, peers):
        for device in peers:
            j = device[0]
            push(source(j), landing(m), send.at[chunk, j], recv.at[chunk, m], device)

    def arrived(ref, sem):
        pltpu.make_async_copy(ref, ref, sem).wait()

    def share(box, at, send, recv, peers):
        for k, peer in enumerate(peers):
            push(box.at[at], box.at[at], send.at[k], recv.at[at], peer)

    def sent(box, send, peers):
        for k in range(len(peers)):
            arrived(box.at[0], send.at[k])

    def collect(box, at, recv):
        count = box.shape[0]

        def one(k, carry):
            j = lax.rem(at + k, count)
            arrived(box.at[j], recv.at[j])
            return carry

        lax.fori_loop(1, count, one, 0)
        total = box[0]
        for j in range(1, count):
            total = total + box[j]
        return total

    for chunk, (first, size) in enumerate(CHUNKS):
        exchange(
            lambda j: ens.at[pl.ds(j * per + first, size)],
            lambda i: gat.at[i, pl.ds(first, size)],
            send1,
            recv1,
            chunk,
            met,
        )

    def along_rows(row):
        square = jnp.broadcast_to(row, (blocks, blocks))
        diagonal = lax.broadcasted_iota(jnp.int32, (blocks, blocks), 0) == lax.broadcasted_iota(
            jnp.int32, (blocks, blocks), 1
        )
        column = jnp.sum(jnp.where(diagonal, square, 0.0), axis=1, keepdims=True)
        return jnp.broadcast_to(column, (blocks, BLOCK))

    lat_copy.wait()
    latitude = ((lat[...].astype(jnp.float32) + 0.5) / BANDS - 0.5) * math.pi
    block_area = jnp.cos(latitude)
    box_row[0] = block_area
    push(box_row.at[0], box_row.at[1], row_sem.at[0], row_sem.at[1], place(0, quarter))
    wide = along_rows(block_area)
    for g in range(groups):
        area[g] = wide[g * ROWS : (g + 1) * ROWS]
    box_a1[near_at] = jnp.sum(wide, axis=0, keepdims=True)
    share(box_a1, near_at, send_a1, recv_a1, near_peers)

    cw_copy.wait()
    own_copy.wait()
    tgt_copy.wait()

    def skill_rows(first, rows, acc):
        for g in range(groups):
            tiles = [
                tgt_rows[pl.ds(first, rows), pl.ds((g * ROWS + i) * BLOCK, BLOCK)] for i in range(ROWS)
            ]
            part = jnp.zeros((ROWS, BLOCK), jnp.float32)
            for r in range(rows):
                u = (first + r) * groups + g
                skill = own[u] - jnp.concatenate([tile[r : r + 1] for tile in tiles], axis=0)
                sgn[u] = jnp.clip(skill * 64.0, -1.0, 1.0) * 0.0625
                part = part + cw[first + r] * jnp.abs(skill)
            acc = acc + area[g] * part
        return acc

    def skill_octet(k, acc):
        return skill_rows(pl.multiple_of(k * 8, 8), 8, acc)

    octets = channels // 8
    skill_sum = lax.fori_loop(0, octets, skill_octet, jnp.zeros((ROWS, BLOCK), jnp.float32))
    if channels % 8:
        skill_sum = skill_rows(octets * 8, channels % 8, skill_sum)

    arrived(box_row.at[1], row_sem.at[1])
    met_wide = along_rows(box_row[1])
    for g in range(groups):
        met_area[g] = met_wide[g * ROWS : (g + 1) * ROWS]
    count = float(members)

    def pairs(places, acc):
        values = [
            jnp.concatenate([gat[j, i] for i in places], axis=0) * 64.0 for j in range(members)
        ]
        signs = [jnp.zeros_like(values[0]) for j in range(members)]
        for a in range(members):
            for b in range(a + 1, members):
                d = jnp.clip(values[a] - values[b], -1.0, 1.0)
                signs[a] = signs[a] + d
                signs[b] = signs[b] - d
        dot = values[0] * signs[0]
        for j in range(1, members):
            dot = dot + values[j] * signs[j]
        for n, i in enumerate(places):
            part = slice(n * ROWS, (n + 1) * ROWS)
            for j in range(members):
                sums[j, i] = signs[j][part]
            u = m * per + i
            acc = acc + (met_area[lax.rem(u, groups)] * cw[lax.div(u, groups)]) * dot[part]
        return acc

    spread_sum = jnp.zeros((ROWS, BLOCK), jnp.float32)
    for chunk, (first, size) in enumerate(CHUNKS):

        def wait_chunk(j, carry):
            arrived(gat.at[j, pl.ds(first, size)], recv1.at[chunk, j])
            return carry

        lax.fori_loop(0, members, wait_chunk, 0)
        if chunk == 0:
            area_near = collect(box_a1, near_at, recv_a1)
            box_a2[far_at] = area_near
            share(box_a2, far_at, send_a2, recv_a2, far_peers)
        spread_sum = lax.fori_loop(
            0,
            size // 2,
            lambda k, acc: pairs((first + 2 * k, first + 2 * k + 1), acc),
            spread_sum,
        )
        if size % 2:
            spread_sum = pairs((first + size - 1,), spread_sum)
        def send_back(peers):
            exchange(
                lambda j: sums.at[j, pl.ds(first, size)],
                lambda i: back.at[pl.ds(i * per + first, size)],
                send2,
                recv2,
                chunk,
                peers,
            )

        if first + size < per:
            send_back(met)

    mine = skill_sum * (1.0 / count) - spread_sum * (1.0 / (64.0 * count * (count - 1.0)))
    box_l1[near_at] = jnp.sum(mine, axis=0, keepdims=True)
    share(box_l1, near_at, send_l1, recv_l1, near_peers)
    send_back(met[:5])
    loss_near = collect(box_l1, near_at, recv_l1)
    box_near[0] = loss_near
    for k, peer in enumerate(upper):
        push(box_near.at[0], box_l2.at[y], send_l2.at[k], recv_l2.at[y], peer)
    send_back(met[5:10])
    arrived(box_l2.at[y], recv_l2.at[y])
    loss_y = collect(box_l2, y, recv_l2)
    box_l3[z] = loss_y
    share(box_l3, z, send_l3, recv_l3, z_peers)
    send_back(met[10:])

    area_all = collect(box_a2, far_at, recv_a2)
    area_total = jnp.sum(area_all, axis=1, keepdims=True)
    points = float(units * ROWS * BLOCK // channels * spaces)
    factor = jnp.broadcast_to(points / area_total, (ROWS, BLOCK))

    def scale_channel(c, carry):
        weight = cw[c]
        for g in range(groups):
            u = c * groups + g
            scale = area[g] * factor * weight
            sgn[u] = sgn[u] * scale
            scl[u] = scale * (1.0 / (count * (count - 1.0)))
        return carry

    lax.fori_loop(0, channels, scale_channel, 0)

    def finish(j, source, first, size):
        part = pl.ds(j * per + first, size)
        grad[part] = sgn[part] - scl[part] * source

    for chunk, (first, size) in enumerate(CHUNKS):

        def take_back(j, carry):
            part = back.at[pl.ds(j * per + first, size)]
            arrived(part, recv2.at[chunk, j])
            finish(j, part[...], first, size)
            return carry

        lax.fori_loop(0, members, take_back, 0)

    loss_all = collect(box_l3, z, recv_l3)
    loss_total = jnp.sum(loss_all, axis=1, keepdims=True)
    loss[...] = loss_total / (area_total * float(channels))

    for chunk, (first, size) in enumerate(CHUNKS):

        def wait_sent(j, carry):
            arrived(gat.at[j, pl.ds(first, size)], send1.at[chunk, j])
            arrived(sums.at[j, pl.ds(first, size)], send2.at[chunk, j])
            return carry

        lax.fori_loop(0, members, wait_sent, 0)
    arrived(box_row.at[0], row_sem.at[0])
    sent(box_a1, send_a1, near_peers)
    sent(box_a2, send_a2, far_peers)
    sent(box_l1, send_l1, near_peers)
    sent(box_l2, send_l2, upper)
    sent(box_l3, send_l3, z_peers)


def local(members, spaces, ensemble, target, chan_weight, lat_band):
    channels, points = target.shape
    units = channels * points // (ROWS * BLOCK)
    per = units // members
    far = spaces // NEAR
    ny = members // PLANES
    nz = far * PLANES
    f32 = jnp.float32
    dma = pltpu.SemaphoreType.DMA
    vmem = pl.BlockSpec(memory_space=pltpu.VMEM)
    hbm = pl.BlockSpec(memory_space=pltpu.HBM)
    whole = pltpu.VMEM((units, ROWS, BLOCK), f32)
    slabs = pltpu.VMEM((members, per, ROWS, BLOCK), f32)

    def box(n):
        return pltpu.VMEM((n, 1, BLOCK), f32)

    def in_hbm(x):
        return pltpu.with_memory_space_constraint(x, pltpu.HBM)

    def body(*refs):
        kernel(members, spaces, *refs)

    grad, loss = pl.pallas_call(
        body,
        out_shape=(
            jax.ShapeDtypeStruct((units, ROWS, BLOCK), f32),
            jax.ShapeDtypeStruct((1, 1), f32),
        ),
        in_specs=[hbm] * 4,
        out_specs=(vmem, vmem),
        scratch_shapes=[
            pltpu.SMEM(chan_weight.shape, f32),
            pltpu.VMEM((1, lat_band.shape[0]), lat_band.dtype),
            whole,
            pltpu.VMEM((channels, points), f32),
            whole,
            whole,
            slabs,
            slabs,
            whole,
            pltpu.VMEM((points // (ROWS * BLOCK), ROWS, BLOCK), f32),
            pltpu.VMEM((points // (ROWS * BLOCK), ROWS, BLOCK), f32),
            pltpu.VMEM((2, 1, lat_band.shape[0]), f32),
            box(NEAR),
            box(far),
            box(NEAR),
            box(1),
            box(ny),
            box(nz),
            dma((4,)),
            dma((2,)),
            dma((len(CHUNKS), members)),
            dma((len(CHUNKS), members)),
            dma((len(CHUNKS), members)),
            dma((len(CHUNKS), members)),
            dma((NEAR,)),
            dma((NEAR,)),
            dma((far,)),
            dma((far,)),
            dma((NEAR,)),
            dma((NEAR,)),
            dma((ny,)),
            dma((ny,)),
            dma((nz,)),
            dma((nz,)),
        ],
        compiler_params=pltpu.CompilerParams(
            collective_id=0, has_side_effects=True, vmem_limit_bytes=32 * 1024 * 1024
        ),
    )(
        in_hbm(ensemble.reshape(units, ROWS, BLOCK)),
        in_hbm(target),
        in_hbm(chan_weight),
        in_hbm(lat_band.reshape(1, -1)),
    )
    return loss.reshape(()), grad.reshape(1, channels, points)


def solution(mesh):
    members, spaces = mesh.shape["member"], mesh.shape["space"]

    def step(*args):
        return local(members, spaces, *args)

    in_specs = (P("member", None, "space"), P(None, "space"), P(), P("space"))
    out_specs = (P(), P("member", None, "space"))
    return jax.shard_map(step, mesh=mesh, in_specs=in_specs, out_specs=out_specs, check_vma=False)
```

```python
import math

import jax
import jax.numpy as jnp
from jax import lax
from jax.experimental import pallas as pl
from jax.experimental.pallas import tpu as pltpu
from jax.sharding import PartitionSpec as P

BLOCK = 128
BANDS = 720
MESH = pl.DeviceIdType.MESH
ROWS = 4
NEAR = 8
PLANES = 2
CHUNKS = ((0, 6), (6, 7))


def kernel(
    members,
    spaces,
    ens,
    tgt,
    cw_hbm,
    lat_hbm,
    grad,
    loss,
    cw,
    lat,
    own,
    tgt_rows,
    sgn,
    scl,
    gat,
    sums,
    back,
    area,
    met_area,
    box_row,
    box_a1,
    box_a2,
    box_l1,
    box_l2,
    box_l3,
    local_sem,
    row_sem,
    send1,
    recv1,
    send2,
    recv2,
    send_a1,
    recv_a1,
    send_a2,
    recv_a2,
    send_l1,
    recv_l1,
    send_l2,
    recv_l2,
    send_l3,
    recv_l3,
):
    m = lax.axis_index("member")
    s = lax.axis_index("space")
    far = spaces // NEAR
    ny = members // PLANES
    nz = far * PLANES
    near_at = lax.rem(s, NEAR)
    far_at = lax.div(s, NEAR)
    y = lax.div(m, PLANES)
    z = lax.rem(m, PLANES) * far + far_at
    units = ens.shape[0]
    per = units // members
    channels = tgt.shape[0]
    groups = units // channels
    blocks = groups * ROWS

    def member_of(yy, zz):
        return lax.rem(yy + ny, ny) * PLANES + lax.div(lax.rem(zz + nz, nz), far)

    def place(yy, zz):
        return (member_of(yy, zz), lax.rem(lax.rem(zz + nz, nz), far) * NEAR + near_at)

    def near_peer(k):
        return (m, s - near_at + lax.rem(near_at + k, NEAR))

    def far_peer(k):
        return (m, lax.rem(far_at + k, far) * NEAR + near_at)

    def z_peer(k):
        return place(y, z + k)

    def y_peer(k):
        return place(y + k, z)

    quarter = nz // 4

    def met(n):
        step = lax.div(lax.div(n, 2) + 1, 2)
        dy = ny // 2 + step * (2 * lax.rem(lax.div(n, 2), 2) - 1)
        return place(y + dy, z + quarter * (1 - 2 * lax.rem(n, 2)))

    barrier = pltpu.get_barrier_semaphore()

    def greet(peer):
        pl.semaphore_signal(barrier, inc=1, device_id=peer, device_id_type=MESH)

    def greet_all(peer, start, count):
        def one(k, carry):
            greet(peer(k))
            return carry

        lax.fori_loop(start, count, one, 0)

    greet_all(met, 0, members)
    greet_all(near_peer, 1, NEAR)
    greet_all(z_peer, 1, nz)
    greet_all(y_peer, 1, ny)
    own_copy = pltpu.make_async_copy(ens, own, local_sem.at[0])
    tgt_copy = pltpu.make_async_copy(tgt, tgt_rows, local_sem.at[1])
    cw_copy = pltpu.make_async_copy(cw_hbm, cw, local_sem.at[2])
    lat_copy = pltpu.make_async_copy(lat_hbm, lat, local_sem.at[3])
    lat_copy.start()
    cw_copy.start()
    own_copy.start()
    tgt_copy.start()

    pl.semaphore_wait(barrier, members + (NEAR - 1) + (nz - 1) + (ny - 1))

    def push(src, dst, send, recv, device):
        pltpu.make_async_remote_copy(
            src_ref=src,
            dst_ref=dst,
            send_sem=send,
            recv_sem=recv,
            device_id=device,
            device_id_type=MESH,
        ).start()

    def exchange(source, landing, send, recv, chunk):
        def one(n, carry):
            device = met(n)
            j = device[0]
            push(source(j), landing(m), send.at[chunk, j], recv.at[chunk, m], device)
            return carry

        lax.fori_loop(0, members, one, 0)

    def arrived(ref, sem):
        pltpu.make_async_copy(ref, ref, sem).wait()

    def share(box, at, send, recv, peer, count):
        def one(k, carry):
            push(box.at[at], box.at[at], send.at[k], recv.at[at], peer(k))
            return carry

        lax.fori_loop(1, count, one, 0)

    def collect(box, at, send, recv, count):
        def one(k, carry):
            j = lax.rem(at + k, count)
            pltpu.make_async_copy(box.at[j], box.at[j], recv.at[j]).wait()
            pltpu.make_async_copy(box.at[at], box.at[at], send.at[k]).wait()
            return carry

        lax.fori_loop(1, count, one, 0)
        total = box[0]
        for j in range(1, count):
            total = total + box[j]
        return total

    for chunk, (first, size) in enumerate(CHUNKS):
        exchange(
            lambda j: ens.at[pl.ds(j * per + first, size)],
            lambda i: gat.at[i, pl.ds(first, size)],
            send1,
            recv1,
            chunk,
        )

    def along_rows(row):
        square = jnp.broadcast_to(row, (blocks, blocks))
        diagonal = lax.broadcasted_iota(jnp.int32, (blocks, blocks), 0) == lax.broadcasted_iota(
            jnp.int32, (blocks, blocks), 1
        )
        column = jnp.sum(jnp.where(diagonal, square, 0.0), axis=1, keepdims=True)
        return jnp.broadcast_to(column, (blocks, BLOCK))

    lat_copy.wait()
    latitude = ((lat[...].astype(jnp.float32) + 0.5) / BANDS - 0.5) * math.pi
    block_area = jnp.cos(latitude)
    box_row[0] = block_area
    push(box_row.at[0], box_row.at[1], row_sem.at[0], row_sem.at[1], place(y, z + quarter))
    wide = along_rows(block_area)
    for g in range(groups):
        area[g] = wide[g * ROWS : (g + 1) * ROWS]
    box_a1[near_at] = jnp.sum(wide, axis=0, keepdims=True)
    share(box_a1, near_at, send_a1, recv_a1, near_peer, NEAR)

    cw_copy.wait()
    own_copy.wait()
    tgt_copy.wait()

    def skill_rows(first, rows, acc):
        for g in range(groups):
            tiles = [
                tgt_rows[pl.ds(first, rows), pl.ds((g * ROWS + i) * BLOCK, BLOCK)] for i in range(ROWS)
            ]
            part = jnp.zeros((ROWS, BLOCK), jnp.float32)
            for r in range(rows):
                u = (first + r) * groups + g
                skill = own[u] - jnp.concatenate([tile[r : r + 1] for tile in tiles], axis=0)
                sgn[u] = jnp.clip(skill * 64.0, -1.0, 1.0) * 0.0625
                part = part + cw[first + r] * jnp.abs(skill)
            acc = acc + area[g] * part
        return acc

    def skill_octet(k, acc):
        return skill_rows(pl.multiple_of(k * 8, 8), 8, acc)

    octets = channels // 8
    skill_sum = lax.fori_loop(0, octets, skill_octet, jnp.zeros((ROWS, BLOCK), jnp.float32))
    if channels % 8:
        skill_sum = skill_rows(octets * 8, channels % 8, skill_sum)

    arrived(box_row.at[1], row_sem.at[1])
    met_wide = along_rows(box_row[1])
    for g in range(groups):
        met_area[g] = met_wide[g * ROWS : (g + 1) * ROWS]
    count = float(members)

    def pairs(places, acc):
        values = [
            jnp.concatenate([gat[j, i] for i in places], axis=0) * 64.0 for j in range(members)
        ]
        signs = [jnp.zeros_like(values[0]) for j in range(members)]
        for a in range(members):
            for b in range(a + 1, members):
                d = jnp.clip(values[a] - values[b], -1.0, 1.0)
                signs[a] = signs[a] + d
                signs[b] = signs[b] - d
        dot = values[0] * signs[0]
        for j in range(1, members):
            dot = dot + values[j] * signs[j]
        for n, i in enumerate(places):
            part = slice(n * ROWS, (n + 1) * ROWS)
            for j in range(members):
                sums[j, i] = signs[j][part]
            u = m * per + i
            acc = acc + (met_area[lax.rem(u, groups)] * cw[lax.div(u, groups)]) * dot[part]
        return acc

    spread_sum = jnp.zeros((ROWS, BLOCK), jnp.float32)
    for chunk, (first, size) in enumerate(CHUNKS):

        def wait_chunk(j, carry):
            arrived(gat.at[j, pl.ds(first, size)], recv1.at[chunk, j])
            return carry

        lax.fori_loop(0, members, wait_chunk, 0)
        if chunk == 0:
            area_near = collect(box_a1, near_at, send_a1, recv_a1, NEAR)
            box_a2[far_at] = area_near
            share(box_a2, far_at, send_a2, recv_a2, far_peer, far)
        spread_sum = lax.fori_loop(
            0,
            size // 2,
            lambda k, acc: pairs((first + 2 * k, first + 2 * k + 1), acc),
            spread_sum,
        )
        if size % 2:
            spread_sum = pairs((first + size - 1,), spread_sum)
        if first + size == per:
            mine = skill_sum * (1.0 / count) - spread_sum * (1.0 / (64.0 * count * (count - 1.0)))
            box_l1[near_at] = jnp.sum(mine, axis=0, keepdims=True)
            share(box_l1, near_at, send_l1, recv_l1, near_peer, NEAR)
        exchange(
            lambda j: sums.at[j, pl.ds(first, size)],
            lambda i: back.at[pl.ds(i * per + first, size)],
            send2,
            recv2,
            chunk,
        )

    loss_near = collect(box_l1, near_at, send_l1, recv_l1, NEAR)
    box_l2[z] = loss_near
    share(box_l2, z, send_l2, recv_l2, z_peer, nz)
    loss_z = collect(box_l2, z, send_l2, recv_l2, nz)
    box_l3[y] = loss_z
    share(box_l3, y, send_l3, recv_l3, y_peer, ny)

    area_all = collect(box_a2, far_at, send_a2, recv_a2, far)
    area_total = jnp.sum(area_all, axis=1, keepdims=True)
    points = float(units * ROWS * BLOCK // channels * spaces)
    factor = jnp.broadcast_to(points / area_total, (ROWS, BLOCK))

    def scale_channel(c, carry):
        weight = cw[c]
        for g in range(groups):
            u = c * groups + g
            scale = area[g] * factor * weight
            sgn[u] = sgn[u] * scale
            scl[u] = scale * (1.0 / (count * (count - 1.0)))
        return carry

    lax.fori_loop(0, channels, scale_channel, 0)

    def finish(j, source, first, size):
        part = pl.ds(j * per + first, size)
        grad[part] = sgn[part] - scl[part] * source


    for chunk, (first, size) in enumerate(CHUNKS):

        def take_back(n, carry):
            j = met(n)[0]
            part = back.at[pl.ds(j * per + first, size)]
            arrived(part, recv2.at[chunk, j])
            finish(j, part[...], first, size)
            return carry

        lax.fori_loop(0, members, take_back, 0)

    loss_all = collect(box_l3, y, send_l3, recv_l3, ny)
    loss_total = jnp.sum(loss_all, axis=1, keepdims=True)
    loss[...] = loss_total / (area_total * float(channels))

    for chunk, (first, size) in enumerate(CHUNKS):

        def wait_sent(j, carry):
            arrived(gat.at[j, pl.ds(first, size)], send1.at[chunk, j])
            arrived(sums.at[j, pl.ds(first, size)], send2.at[chunk, j])
            return carry

        lax.fori_loop(0, members, wait_sent, 0)
    arrived(box_row.at[0], row_sem.at[0])


def local(members, spaces, ensemble, target, chan_weight, lat_band):
    channels, points = target.shape
    units = channels * points // (ROWS * BLOCK)
    per = units // members
    far = spaces // NEAR
    ny = members // PLANES
    nz = far * PLANES
    f32 = jnp.float32
    dma = pltpu.SemaphoreType.DMA
    vmem = pl.BlockSpec(memory_space=pltpu.VMEM)
    hbm = pl.BlockSpec(memory_space=pltpu.HBM)
    whole = pltpu.VMEM((units, ROWS, BLOCK), f32)
    slabs = pltpu.VMEM((members, per, ROWS, BLOCK), f32)

    def box(n):
        return pltpu.VMEM((n, 1, BLOCK), f32)

    def in_hbm(x):
        return pltpu.with_memory_space_constraint(x, pltpu.HBM)

    def body(*refs):
        kernel(members, spaces, *refs)

    grad, loss = pl.pallas_call(
        body,
        out_shape=(
            jax.ShapeDtypeStruct((units, ROWS, BLOCK), f32),
            jax.ShapeDtypeStruct((1, 1), f32),
        ),
        in_specs=[hbm] * 4,
        out_specs=(vmem, vmem),
        scratch_shapes=[
            pltpu.SMEM(chan_weight.shape, f32),
            pltpu.VMEM((1, lat_band.shape[0]), lat_band.dtype),
            whole,
            pltpu.VMEM((channels, points), f32),
            whole,
            whole,
            slabs,
            slabs,
            whole,
            pltpu.VMEM((points // (ROWS * BLOCK), ROWS, BLOCK), f32),
            pltpu.VMEM((points // (ROWS * BLOCK), ROWS, BLOCK), f32),
            pltpu.VMEM((2, 1, lat_band.shape[0]), f32),
            box(NEAR),
            box(far),
            box(NEAR),
            box(nz),
            box(ny),
            dma((4,)),
            dma((2,)),
            dma((len(CHUNKS), members)),
            dma((len(CHUNKS), members)),
            dma((len(CHUNKS), members)),
            dma((len(CHUNKS), members)),
            dma((NEAR,)),
            dma((NEAR,)),
            dma((far,)),
            dma((far,)),
            dma((NEAR,)),
            dma((NEAR,)),
            dma((nz,)),
            dma((nz,)),
            dma((ny,)),
            dma((ny,)),
        ],
        compiler_params=pltpu.CompilerParams(
            collective_id=0, has_side_effects=True, vmem_limit_bytes=32 * 1024 * 1024
        ),
    )(
        in_hbm(ensemble.reshape(units, ROWS, BLOCK)),
        in_hbm(target),
        in_hbm(chan_weight),
        in_hbm(lat_band.reshape(1, -1)),
    )
    return loss.reshape(()), grad.reshape(1, channels, points)


def solution(mesh):
    members, spaces = mesh.shape["member"], mesh.shape["space"]

    def step(*args):
        return local(members, spaces, *args)

    in_specs = (P("member", None, "space"), P(None, "space"), P(), P("space"))
    out_specs = (P(), P("member", None, "space"))
    return jax.shard_map(step, mesh=mesh, in_specs=in_specs, out_specs=out_specs, check_vma=False)
```

```python
import math

import jax
import jax.numpy as jnp
from jax import lax
from jax.experimental import pallas as pl
from jax.experimental.pallas import tpu as pltpu
from jax.sharding import PartitionSpec as P

BLOCK = 128
BANDS = 720
MESH = pl.DeviceIdType.MESH
ROWS = 4
NEAR = 8
PLANES = 2
CHUNKS = ((0, 6), (6, 7))


def kernel(
    members,
    spaces,
    ens,
    tgt,
    cw_hbm,
    lat_hbm,
    result,
    cw,
    lat,
    own,
    tgt_rows,
    sgn,
    scl,
    gat,
    sums,
    back,
    area,
    met_area,
    box_row,
    box_a1,
    box_a2,
    box_l1,
    box_l2,
    box_l3,
    local_sem,
    row_sem,
    send1,
    recv1,
    send2,
    recv2,
    send_a1,
    recv_a1,
    send_a2,
    recv_a2,
    send_l1,
    recv_l1,
    send_l2,
    recv_l2,
    send_l3,
    recv_l3,
):
    m = lax.axis_index("member")
    s = lax.axis_index("space")
    far = spaces // NEAR
    ny = members // PLANES
    nz = far * PLANES
    near_at = lax.rem(s, NEAR)
    far_at = lax.div(s, NEAR)
    y = lax.div(m, PLANES)
    z = lax.rem(m, PLANES) * far + far_at
    units = ens.shape[0]
    per = units // members
    channels = tgt.shape[0]
    groups = units // channels
    blocks = groups * ROWS

    def member_of(yy, zz):
        return lax.rem(yy + ny, ny) * PLANES + lax.div(lax.rem(zz + nz, nz), far)

    def place(yy, zz):
        return (member_of(yy, zz), lax.rem(lax.rem(zz + nz, nz), far) * NEAR + near_at)

    def near_peer(k):
        return (m, s - near_at + lax.rem(near_at + k, NEAR))

    def far_peer(k):
        return (m, lax.rem(far_at + k, far) * NEAR + near_at)

    def z_peer(k):
        return place(y, z + k)

    def y_peer(k):
        return place(y + k, z)

    quarter = nz // 4

    def met(n):
        pair, turn = lax.div(n, 4), lax.rem(n, 4)
        dy = ny // 2 - pair + lax.rem(turn, 2) * (2 * pair - ny + 1)
        dz = quarter * (1 - 2 * lax.rem(lax.div(turn + 1, 2), 2))
        return place(y + dy, z + dz)

    barrier = pltpu.get_barrier_semaphore()

    def greet(peer):
        pl.semaphore_signal(barrier, inc=1, device_id=peer, device_id_type=MESH)

    def greet_all(peer, start, count):
        def one(k, carry):
            greet(peer(k))
            return carry

        lax.fori_loop(start, count, one, 0)

    greet_all(met, 0, members)
    greet_all(near_peer, 1, NEAR)
    greet_all(z_peer, 1, nz)
    greet_all(y_peer, 1, ny)
    own_copy = pltpu.make_async_copy(ens, own, local_sem.at[0])
    tgt_copy = pltpu.make_async_copy(tgt, tgt_rows, local_sem.at[1])
    cw_copy = pltpu.make_async_copy(cw_hbm, cw, local_sem.at[2])
    lat_copy = pltpu.make_async_copy(lat_hbm, lat, local_sem.at[3])
    lat_copy.start()
    cw_copy.start()
    own_copy.start()
    tgt_copy.start()

    pl.semaphore_wait(barrier, members + (NEAR - 1) + (nz - 1) + (ny - 1))

    def push(src, dst, send, recv, device):
        pltpu.make_async_remote_copy(
            src_ref=src,
            dst_ref=dst,
            send_sem=send,
            recv_sem=recv,
            device_id=device,
            device_id_type=MESH,
        ).start()

    def exchange(source, landing, send, recv, chunk):
        def one(n, carry):
            device = met(n)
            j = device[0]
            push(source(j), landing(m), send.at[chunk, j], recv.at[chunk, m], device)
            return carry

        lax.fori_loop(0, members, one, 0)

    def arrived(ref, sem):
        pltpu.make_async_copy(ref, ref, sem).wait()

    def share(box, at, send, recv, peer, count):
        def one(k, carry):
            push(box.at[at], box.at[at], send.at[k], recv.at[at], peer(k))
            return carry

        lax.fori_loop(1, count, one, 0)

    def collect(box, at, send, recv, count):
        def one(k, carry):
            j = lax.rem(at + k, count)
            pltpu.make_async_copy(box.at[j], box.at[j], recv.at[j]).wait()
            pltpu.make_async_copy(box.at[at], box.at[at], send.at[k]).wait()
            return carry

        lax.fori_loop(1, count, one, 0)
        total = box[0]
        for j in range(1, count):
            total = total + box[j]
        return total

    for chunk, (first, size) in enumerate(CHUNKS):
        exchange(
            lambda j: ens.at[pl.ds(j * per + first, size)],
            lambda i: gat.at[i, pl.ds(first, size)],
            send1,
            recv1,
            chunk,
        )

    def along_rows(row):
        square = jnp.broadcast_to(row, (blocks, blocks))
        diagonal = lax.broadcasted_iota(jnp.int32, (blocks, blocks), 0) == lax.broadcasted_iota(
            jnp.int32, (blocks, blocks), 1
        )
        column = jnp.sum(jnp.where(diagonal, square, 0.0), axis=1, keepdims=True)
        return jnp.broadcast_to(column, (blocks, BLOCK))

    lat_copy.wait()
    latitude = ((lat[...].astype(jnp.float32) + 0.5) / BANDS - 0.5) * math.pi
    block_area = jnp.cos(latitude)
    box_row[0] = block_area
    push(box_row.at[0], box_row.at[1], row_sem.at[0], row_sem.at[1], place(y, z + quarter))
    wide = along_rows(block_area)
    for g in range(groups):
        area[g] = wide[g * ROWS : (g + 1) * ROWS]
    box_a1[near_at] = jnp.sum(wide, axis=0, keepdims=True)
    share(box_a1, near_at, send_a1, recv_a1, near_peer, NEAR)

    cw_copy.wait()
    own_copy.wait()
    tgt_copy.wait()

    def skill_rows(first, rows, acc):
        for g in range(groups):
            tiles = [
                tgt_rows[pl.ds(first, rows), pl.ds((g * ROWS + i) * BLOCK, BLOCK)] for i in range(ROWS)
            ]
            part = jnp.zeros((ROWS, BLOCK), jnp.float32)
            for r in range(rows):
                u = (first + r) * groups + g
                skill = own[u] - jnp.concatenate([tile[r : r + 1] for tile in tiles], axis=0)
                sgn[u] = jnp.clip(skill * 64.0, -1.0, 1.0) * 0.0625
                part = part + cw[first + r] * jnp.abs(skill)
            acc = acc + area[g] * part
        return acc

    def skill_octet(k, acc):
        return skill_rows(pl.multiple_of(k * 8, 8), 8, acc)

    octets = channels // 8
    skill_sum = lax.fori_loop(0, octets, skill_octet, jnp.zeros((ROWS, BLOCK), jnp.float32))
    if channels % 8:
        skill_sum = skill_rows(octets * 8, channels % 8, skill_sum)

    arrived(box_row.at[1], row_sem.at[1])
    met_wide = along_rows(box_row[1])
    for g in range(groups):
        met_area[g] = met_wide[g * ROWS : (g + 1) * ROWS]
    count = float(members)

    def pairs(places, acc):
        values = [
            jnp.concatenate([gat[j, i] for i in places], axis=0) * 64.0 for j in range(members)
        ]
        signs = [jnp.zeros_like(values[0]) for j in range(members)]
        for a in range(members):
            for b in range(a + 1, members):
                d = jnp.clip(values[a] - values[b], -1.0, 1.0)
                signs[a] = signs[a] + d
                signs[b] = signs[b] - d
        dot = values[0] * signs[0]
        for j in range(1, members):
            dot = dot + values[j] * signs[j]
        for n, i in enumerate(places):
            part = slice(n * ROWS, (n + 1) * ROWS)
            for j in range(members):
                sums[j, i] = signs[j][part]
            u = m * per + i
            acc = acc + (met_area[lax.rem(u, groups)] * cw[lax.div(u, groups)]) * dot[part]
        return acc

    spread_sum = jnp.zeros((ROWS, BLOCK), jnp.float32)
    for chunk, (first, size) in enumerate(CHUNKS):

        def wait_chunk(j, carry):
            arrived(gat.at[j, pl.ds(first, size)], recv1.at[chunk, j])
            return carry

        lax.fori_loop(0, members, wait_chunk, 0)
        if chunk == 0:
            area_near = collect(box_a1, near_at, send_a1, recv_a1, NEAR)
            box_a2[far_at] = area_near
            share(box_a2, far_at, send_a2, recv_a2, far_peer, far)
        spread_sum = lax.fori_loop(
            0,
            size // 2,
            lambda k, acc: pairs((first + 2 * k, first + 2 * k + 1), acc),
            spread_sum,
        )
        if size % 2:
            spread_sum = pairs((first + size - 1,), spread_sum)
        if first + size == per:
            mine = skill_sum * (1.0 / count) - spread_sum * (1.0 / (64.0 * count * (count - 1.0)))
            box_l1[near_at] = jnp.sum(mine, axis=0, keepdims=True)
            share(box_l1, near_at, send_l1, recv_l1, near_peer, NEAR)
        exchange(
            lambda j: sums.at[j, pl.ds(first, size)],
            lambda i: back.at[pl.ds(i * per + first, size)],
            send2,
            recv2,
            chunk,
        )

    loss_near = collect(box_l1, near_at, send_l1, recv_l1, NEAR)
    box_l2[z] = loss_near
    share(box_l2, z, send_l2, recv_l2, z_peer, nz)
    loss_z = collect(box_l2, z, send_l2, recv_l2, nz)
    box_l3[y] = loss_z
    share(box_l3, y, send_l3, recv_l3, y_peer, ny)

    area_all = collect(box_a2, far_at, send_a2, recv_a2, far)
    area_total = jnp.sum(area_all, axis=1, keepdims=True)
    points = float(units * ROWS * BLOCK // channels * spaces)
    factor = jnp.broadcast_to(points / area_total, (ROWS, BLOCK))

    def scale_channel(c, carry):
        weight = cw[c]
        for g in range(groups):
            u = c * groups + g
            scale = area[g] * factor * weight
            sgn[u] = sgn[u] * scale
            scl[u] = scale * (1.0 / (count * (count - 1.0)))
        return carry

    lax.fori_loop(0, channels, scale_channel, 0)

    def finish(j, source, first, size):
        part = pl.ds(j * per + first, size)
        result[part] = sgn[part] - scl[part] * source


    for chunk, (first, size) in enumerate(CHUNKS):

        def take_back(n, carry):
            j = met(n)[0]
            part = back.at[pl.ds(j * per + first, size)]
            arrived(part, recv2.at[chunk, j])
            finish(j, part[...], first, size)
            return carry

        lax.fori_loop(0, members, take_back, 0)

    loss_all = collect(box_l3, y, send_l3, recv_l3, ny)
    loss_total = jnp.sum(loss_all, axis=1, keepdims=True)
    result[units] = jnp.broadcast_to(loss_total / (area_total * float(channels)), (ROWS, BLOCK))

    for chunk, (first, size) in enumerate(CHUNKS):

        def wait_sent(j, carry):
            arrived(gat.at[j, pl.ds(first, size)], send1.at[chunk, j])
            arrived(sums.at[j, pl.ds(first, size)], send2.at[chunk, j])
            return carry

        lax.fori_loop(0, members, wait_sent, 0)
    arrived(box_row.at[0], row_sem.at[0])


def deliver(result, grad, loss, last, sem):
    grad_copy = pltpu.make_async_copy(result.at[pl.ds(0, grad.shape[0])], grad, sem.at[0])
    grad_copy.start()
    last[...] = result[grad.shape[0], 0:1, 0:1]
    loss_copy = pltpu.make_async_copy(last, loss, sem.at[1])
    loss_copy.start()
    loss_copy.wait()
    grad_copy.wait()


def local(members, spaces, ensemble, target, chan_weight, lat_band):
    channels, points = target.shape
    units = channels * points // (ROWS * BLOCK)
    per = units // members
    far = spaces // NEAR
    ny = members // PLANES
    nz = far * PLANES
    f32 = jnp.float32
    dma = pltpu.SemaphoreType.DMA
    vmem = pl.BlockSpec(memory_space=pltpu.VMEM)
    hbm = pl.BlockSpec(memory_space=pltpu.HBM)
    whole = pltpu.VMEM((units, ROWS, BLOCK), f32)
    slabs = pltpu.VMEM((members, per, ROWS, BLOCK), f32)

    def box(n):
        return pltpu.VMEM((n, 1, BLOCK), f32)

    def in_hbm(x):
        return pltpu.with_memory_space_constraint(x, pltpu.HBM)

    def body(*refs):
        kernel(members, spaces, *refs)

    result = pl.pallas_call(
        body,
        out_shape=jax.ShapeDtypeStruct((units + 1, ROWS, BLOCK), f32),
        in_specs=[hbm] * 4,
        out_specs=vmem,
        scratch_shapes=[
            pltpu.SMEM(chan_weight.shape, f32),
            pltpu.VMEM((1, lat_band.shape[0]), lat_band.dtype),
            whole,
            pltpu.VMEM((channels, points), f32),
            whole,
            whole,
            slabs,
            slabs,
            whole,
            pltpu.VMEM((points // (ROWS * BLOCK), ROWS, BLOCK), f32),
            pltpu.VMEM((points // (ROWS * BLOCK), ROWS, BLOCK), f32),
            pltpu.VMEM((2, 1, lat_band.shape[0]), f32),
            box(NEAR),
            box(far),
            box(NEAR),
            box(nz),
            box(ny),
            dma((4,)),
            dma((2,)),
            dma((len(CHUNKS), members)),
            dma((len(CHUNKS), members)),
            dma((len(CHUNKS), members)),
            dma((len(CHUNKS), members)),
            dma((NEAR,)),
            dma((NEAR,)),
            dma((far,)),
            dma((far,)),
            dma((NEAR,)),
            dma((NEAR,)),
            dma((nz,)),
            dma((nz,)),
            dma((ny,)),
            dma((ny,)),
        ],
        compiler_params=pltpu.CompilerParams(
            collective_id=0, has_side_effects=True, vmem_limit_bytes=32 * 1024 * 1024
        ),
    )(
        in_hbm(ensemble.reshape(units, ROWS, BLOCK)),
        in_hbm(target),
        in_hbm(chan_weight),
        in_hbm(lat_band.reshape(1, -1)),
    )
    grad, loss = pl.pallas_call(
        deliver,
        out_shape=(
            jax.ShapeDtypeStruct((units, ROWS, BLOCK), f32),
            jax.ShapeDtypeStruct((1, 1), f32),
        ),
        in_specs=[vmem],
        out_specs=(hbm, hbm),
        scratch_shapes=[pltpu.VMEM((1, 1), f32), dma((2,))],
        compiler_params=pltpu.CompilerParams(vmem_limit_bytes=32 * 1024 * 1024),
    )(result)
    return loss.reshape(()), grad.reshape(1, channels, points)


def solution(mesh):
    members, spaces = mesh.shape["member"], mesh.shape["space"]

    def step(*args):
        return local(members, spaces, *args)

    in_specs = (P("member", None, "space"), P(None, "space"), P(), P("space"))
    out_specs = (P(), P("member", None, "space"))
    return jax.shard_map(step, mesh=mesh, in_specs=in_specs, out_specs=out_specs, check_vma=False)
```

```python
import math

import jax
import jax.numpy as jnp
from jax import lax
from jax.experimental import pallas as pl
from jax.experimental.pallas import tpu as pltpu
from jax.sharding import PartitionSpec as P

BLOCK = 128
BANDS = 720
MESH = pl.DeviceIdType.MESH
ROWS = 4
NEAR = 8
PLANES = 2
CHUNKS = ((0, 7), (7, 6))


def kernel(
    members,
    spaces,
    ens,
    tgt,
    cw_hbm,
    lat_hbm,
    result,
    cw,
    lat,
    own,
    tgt_rows,
    sgn,
    scl,
    gat,
    sums,
    back,
    area,
    met_area,
    box_row,
    box_a1,
    box_a2,
    box_l1,
    box_l2,
    box_l3,
    local_sem,
    row_sem,
    send1,
    recv1,
    send2,
    recv2,
    send_a1,
    recv_a1,
    send_a2,
    recv_a2,
    send_l1,
    recv_l1,
    send_l2,
    recv_l2,
    send_l3,
    recv_l3,
):
    m = lax.axis_index("member")
    s = lax.axis_index("space")
    far = spaces // NEAR
    ny = members // PLANES
    nz = far * PLANES
    near_at = lax.rem(s, NEAR)
    far_at = lax.div(s, NEAR)
    y = lax.div(m, PLANES)
    z = lax.rem(m, PLANES) * far + far_at
    units = ens.shape[0]
    per = units // members
    channels = tgt.shape[0]
    groups = units // channels
    blocks = groups * ROWS

    def member_of(yy, zz):
        return lax.rem(yy + ny, ny) * PLANES + lax.div(lax.rem(zz + nz, nz), far)

    def place(yy, zz):
        return (member_of(yy, zz), lax.rem(lax.rem(zz + nz, nz), far) * NEAR + near_at)

    def near_peer(k):
        return (m, s - near_at + lax.rem(near_at + k, NEAR))

    def far_peer(k):
        return (m, lax.rem(far_at + k, far) * NEAR + near_at)

    def z_peer(k):
        return place(y, z + k)

    def y_peer(k):
        return place(y + k, z)

    quarter = nz // 4

    def met(n):
        pair, turn = lax.div(n, 4), lax.rem(n, 4)
        dy = ny // 2 - pair + lax.rem(turn, 2) * (2 * pair - ny + 1)
        dz = quarter * (1 - 2 * lax.rem(lax.div(turn + 1, 2), 2))
        return place(y + dy, z + dz)

    barrier = pltpu.get_barrier_semaphore()

    steps = sorted(range(ny), key=lambda k: -min(k, ny - k))
    greeted = [place(y + k, z + dz) for k in steps for dz in (quarter, -quarter)]
    greeted += [y_peer(k) for k in steps if k]
    greeted += [z_peer(k) for k in range(1, nz) if k not in (quarter, nz - quarter)]
    greeted += [near_peer(k) for k in range(1, NEAR)]
    for peer in greeted:
        pl.semaphore_signal(barrier, inc=1, device_id=peer, device_id_type=MESH)
    own_copy = pltpu.make_async_copy(ens, own, local_sem.at[0])
    tgt_copy = pltpu.make_async_copy(tgt, tgt_rows, local_sem.at[1])
    cw_copy = pltpu.make_async_copy(cw_hbm, cw, local_sem.at[2])
    lat_copy = pltpu.make_async_copy(lat_hbm, lat, local_sem.at[3])
    lat_copy.start()
    cw_copy.start()
    own_copy.start()
    tgt_copy.start()

    pl.semaphore_wait(barrier, len(greeted))

    def push(src, dst, send, recv, device):
        pltpu.make_async_remote_copy(
            src_ref=src,
            dst_ref=dst,
            send_sem=send,
            recv_sem=recv,
            device_id=device,
            device_id_type=MESH,
        ).start()

    def exchange(source, landing, send, recv, chunk):
        def one(n, carry):
            device = met(n)
            j = device[0]
            push(source(j), landing(m), send.at[chunk, j], recv.at[chunk, m], device)
            return carry

        lax.fori_loop(0, members, one, 0)

    def arrived(ref, sem):
        pltpu.make_async_copy(ref, ref, sem).wait()

    def share(box, at, send, recv, peer, count):
        def one(k, carry):
            push(box.at[at], box.at[at], send.at[k], recv.at[at], peer(k))
            return carry

        lax.fori_loop(1, count, one, 0)

    def collect(box, at, send, recv, count):
        def one(k, carry):
            j = lax.rem(at + k, count)
            pltpu.make_async_copy(box.at[j], box.at[j], recv.at[j]).wait()
            pltpu.make_async_copy(box.at[at], box.at[at], send.at[k]).wait()
            return carry

        lax.fori_loop(1, count, one, 0)
        total = box[0]
        for j in range(1, count):
            total = total + box[j]
        return total

    for chunk, (first, size) in enumerate(CHUNKS):
        exchange(
            lambda j: ens.at[pl.ds(j * per + first, size)],
            lambda i: gat.at[i, pl.ds(first, size)],
            send1,
            recv1,
            chunk,
        )

    def along_rows(row):
        square = jnp.broadcast_to(row, (blocks, blocks))
        diagonal = lax.broadcasted_iota(jnp.int32, (blocks, blocks), 0) == lax.broadcasted_iota(
            jnp.int32, (blocks, blocks), 1
        )
        column = jnp.sum(jnp.where(diagonal, square, 0.0), axis=1, keepdims=True)
        return jnp.broadcast_to(column, (blocks, BLOCK))

    lat_copy.wait()
    latitude = ((lat[...].astype(jnp.float32) + 0.5) / BANDS - 0.5) * math.pi
    block_area = jnp.cos(latitude)
    box_row[0] = block_area
    push(box_row.at[0], box_row.at[1], row_sem.at[0], row_sem.at[1], place(y, z + quarter))
    wide = along_rows(block_area)
    for g in range(groups):
        area[g] = wide[g * ROWS : (g + 1) * ROWS]
    box_a1[near_at] = jnp.sum(wide, axis=0, keepdims=True)
    share(box_a1, near_at, send_a1, recv_a1, near_peer, NEAR)

    cw_copy.wait()
    own_copy.wait()
    tgt_copy.wait()

    def skill_rows(first, rows, acc):
        for g in range(groups):
            tiles = [
                tgt_rows[pl.ds(first, rows), pl.ds((g * ROWS + i) * BLOCK, BLOCK)] for i in range(ROWS)
            ]
            part = jnp.zeros((ROWS, BLOCK), jnp.float32)
            for r in range(rows):
                u = (first + r) * groups + g
                skill = own[u] - jnp.concatenate([tile[r : r + 1] for tile in tiles], axis=0)
                sgn[u] = jnp.clip(skill * 64.0, -1.0, 1.0) * 0.0625
                part = part + cw[first + r] * jnp.abs(skill)
            acc = acc + area[g] * part
        return acc

    def skill_octet(k, acc):
        return skill_rows(pl.multiple_of(k * 8, 8), 8, acc)

    octets = channels // 8
    skill_sum = lax.fori_loop(0, octets, skill_octet, jnp.zeros((ROWS, BLOCK), jnp.float32))
    if channels % 8:
        skill_sum = skill_rows(octets * 8, channels % 8, skill_sum)

    arrived(box_row.at[1], row_sem.at[1])
    met_wide = along_rows(box_row[1])
    for g in range(groups):
        met_area[g] = met_wide[g * ROWS : (g + 1) * ROWS]
    count = float(members)

    def pairs(places, acc):
        values = [
            jnp.concatenate([gat[j, i] for i in places], axis=0) * 64.0 for j in range(members)
        ]
        signs = [jnp.zeros_like(values[0]) for j in range(members)]
        for a in range(members):
            for b in range(a + 1, members):
                d = jnp.clip(values[a] - values[b], -1.0, 1.0)
                signs[a] = signs[a] + d
                signs[b] = signs[b] - d
        dot = values[0] * signs[0]
        for j in range(1, members):
            dot = dot + values[j] * signs[j]
        for n, i in enumerate(places):
            part = slice(n * ROWS, (n + 1) * ROWS)
            for j in range(members):
                sums[j, i] = signs[j][part]
            u = m * per + i
            acc = acc + (met_area[lax.rem(u, groups)] * cw[lax.div(u, groups)]) * dot[part]
        return acc

    spread_sum = jnp.zeros((ROWS, BLOCK), jnp.float32)
    for chunk, (first, size) in enumerate(CHUNKS):

        def wait_chunk(j, carry):
            arrived(gat.at[j, pl.ds(first, size)], recv1.at[chunk, j])
            return carry

        lax.fori_loop(0, members, wait_chunk, 0)
        if chunk == 0:
            area_near = collect(box_a1, near_at, send_a1, recv_a1, NEAR)
            box_a2[far_at] = area_near
            share(box_a2, far_at, send_a2, recv_a2, far_peer, far)
        spread_sum = lax.fori_loop(
            0,
            size // 2,
            lambda k, acc: pairs((first + 2 * k, first + 2 * k + 1), acc),
            spread_sum,
        )
        if size % 2:
            spread_sum = pairs((first + size - 1,), spread_sum)
        if first + size == per:
            mine = skill_sum * (1.0 / count) - spread_sum * (1.0 / (64.0 * count * (count - 1.0)))
            box_l1[near_at] = jnp.sum(mine, axis=0, keepdims=True)
            share(box_l1, near_at, send_l1, recv_l1, near_peer, NEAR)
        exchange(
            lambda j: sums.at[j, pl.ds(first, size)],
            lambda i: back.at[pl.ds(i * per + first, size)],
            send2,
            recv2,
            chunk,
        )

    loss_near = collect(box_l1, near_at, send_l1, recv_l1, NEAR)
    box_l2[z] = loss_near
    share(box_l2, z, send_l2, recv_l2, z_peer, nz)
    loss_z = collect(box_l2, z, send_l2, recv_l2, nz)
    box_l3[y] = loss_z
    share(box_l3, y, send_l3, recv_l3, y_peer, ny)

    area_all = collect(box_a2, far_at, send_a2, recv_a2, far)
    area_total = jnp.sum(area_all, axis=1, keepdims=True)
    points = float(units * ROWS * BLOCK // channels * spaces)
    factor = jnp.broadcast_to(points / area_total, (ROWS, BLOCK))

    def scale_channel(c, carry):
        weight = cw[c]
        for g in range(groups):
            u = c * groups + g
            scale = area[g] * factor * weight
            sgn[u] = sgn[u] * scale
            scl[u] = scale * (1.0 / (count * (count - 1.0)))
        return carry

    lax.fori_loop(0, channels, scale_channel, 0)

    def finish(j, source, first, size):
        part = pl.ds(j * per + first, size)
        result[part] = sgn[part] - scl[part] * source


    for chunk, (first, size) in enumerate(CHUNKS):

        def take_back(n, carry):
            j = met(n)[0]
            part = back.at[pl.ds(j * per + first, size)]
            arrived(part, recv2.at[chunk, j])
            finish(j, part[...], first, size)
            return carry

        lax.fori_loop(0, members, take_back, 0)

    loss_all = collect(box_l3, y, send_l3, recv_l3, ny)
    loss_total = jnp.sum(loss_all, axis=1, keepdims=True)
    result[units] = jnp.broadcast_to(loss_total / (area_total * float(channels)), (ROWS, BLOCK))

    for chunk, (first, size) in enumerate(CHUNKS):

        def wait_sent(j, carry):
            arrived(gat.at[j, pl.ds(first, size)], send1.at[chunk, j])
            arrived(sums.at[j, pl.ds(first, size)], send2.at[chunk, j])
            return carry

        lax.fori_loop(0, members, wait_sent, 0)
    arrived(box_row.at[0], row_sem.at[0])


def deliver(result, grad, loss, last, sem):
    grad_copy = pltpu.make_async_copy(result.at[pl.ds(0, grad.shape[0])], grad, sem.at[0])
    grad_copy.start()
    last[...] = result[grad.shape[0], 0:1, 0:1]
    loss_copy = pltpu.make_async_copy(last, loss, sem.at[1])
    loss_copy.start()
    loss_copy.wait()
    grad_copy.wait()


def local(members, spaces, ensemble, target, chan_weight, lat_band):
    channels, points = target.shape
    units = channels * points // (ROWS * BLOCK)
    per = units // members
    far = spaces // NEAR
    ny = members // PLANES
    nz = far * PLANES
    f32 = jnp.float32
    dma = pltpu.SemaphoreType.DMA
    vmem = pl.BlockSpec(memory_space=pltpu.VMEM)
    hbm = pl.BlockSpec(memory_space=pltpu.HBM)
    whole = pltpu.VMEM((units, ROWS, BLOCK), f32)
    slabs = pltpu.VMEM((members, per, ROWS, BLOCK), f32)

    def box(n):
        return pltpu.VMEM((n, 1, BLOCK), f32)

    def in_hbm(x):
        return pltpu.with_memory_space_constraint(x, pltpu.HBM)

    def body(*refs):
        kernel(members, spaces, *refs)

    result = pl.pallas_call(
        body,
        out_shape=jax.ShapeDtypeStruct((units + 1, ROWS, BLOCK), f32),
        in_specs=[hbm] * 4,
        out_specs=vmem,
        scratch_shapes=[
            pltpu.SMEM(chan_weight.shape, f32),
            pltpu.VMEM((1, lat_band.shape[0]), lat_band.dtype),
            whole,
            pltpu.VMEM((channels, points), f32),
            whole,
            whole,
            slabs,
            slabs,
            whole,
            pltpu.VMEM((points // (ROWS * BLOCK), ROWS, BLOCK), f32),
            pltpu.VMEM((points // (ROWS * BLOCK), ROWS, BLOCK), f32),
            pltpu.VMEM((2, 1, lat_band.shape[0]), f32),
            box(NEAR),
            box(far),
            box(NEAR),
            box(nz),
            box(ny),
            dma((4,)),
            dma((2,)),
            dma((len(CHUNKS), members)),
            dma((len(CHUNKS), members)),
            dma((len(CHUNKS), members)),
            dma((len(CHUNKS), members)),
            dma((NEAR,)),
            dma((NEAR,)),
            dma((far,)),
            dma((far,)),
            dma((NEAR,)),
            dma((NEAR,)),
            dma((nz,)),
            dma((nz,)),
            dma((ny,)),
            dma((ny,)),
        ],
        compiler_params=pltpu.CompilerParams(
            collective_id=0, has_side_effects=True, vmem_limit_bytes=32 * 1024 * 1024
        ),
    )(
        in_hbm(ensemble.reshape(units, ROWS, BLOCK)),
        in_hbm(target),
        in_hbm(chan_weight),
        in_hbm(lat_band.reshape(1, -1)),
    )
    grad, loss = pl.pallas_call(
        deliver,
        out_shape=(
            jax.ShapeDtypeStruct((units, ROWS, BLOCK), f32),
            jax.ShapeDtypeStruct((1, 1), f32),
        ),
        in_specs=[vmem],
        out_specs=(hbm, hbm),
        scratch_shapes=[pltpu.VMEM((1, 1), f32), dma((2,))],
        compiler_params=pltpu.CompilerParams(vmem_limit_bytes=32 * 1024 * 1024),
    )(result)
    return loss.reshape(()), grad.reshape(1, channels, points)


def solution(mesh):
    members, spaces = mesh.shape["member"], mesh.shape["space"]

    def step(*args):
        return local(members, spaces, *args)

    in_specs = (P("member", None, "space"), P(None, "space"), P(), P("space"))
    out_specs = (P(), P("member", None, "space"))
    return jax.shard_map(step, mesh=mesh, in_specs=in_specs, out_specs=out_specs, check_vma=False)
```

```python
import math

import jax
import jax.numpy as jnp
from jax import lax
from jax.experimental import pallas as pl
from jax.experimental.pallas import tpu as pltpu
from jax.sharding import PartitionSpec as P

BLOCK = 128
BANDS = 720
MESH = pl.DeviceIdType.MESH
ROWS = 4
NEAR = 8
PLANES = 2
CHUNKS = ((0, 6), (6, 7))


def kernel(
    members,
    spaces,
    ens,
    tgt,
    cw_hbm,
    lat_hbm,
    result,
    cw,
    lat,
    own,
    tgt_rows,
    sgn,
    scl,
    gat,
    sums,
    back,
    area,
    met_area,
    box_row,
    box_a1,
    box_a2,
    box_l1,
    box_l2,
    box_l3,
    local_sem,
    row_sem,
    send1,
    recv1,
    send2,
    recv2,
    send_a1,
    recv_a1,
    send_a2,
    recv_a2,
    send_l1,
    recv_l1,
    send_l2,
    recv_l2,
    send_l3,
    recv_l3,
):
    m = lax.axis_index("member")
    s = lax.axis_index("space")
    far = spaces // NEAR
    ny = members // PLANES
    nz = far * PLANES
    near_at = lax.rem(s, NEAR)
    far_at = lax.div(s, NEAR)
    y = lax.div(m, PLANES)
    z = lax.rem(m, PLANES) * far + far_at
    units = ens.shape[0]
    per = units // members
    channels = tgt.shape[0]
    groups = units // channels
    blocks = groups * ROWS

    def member_of(yy, zz):
        return lax.rem(yy + ny, ny) * PLANES + lax.div(lax.rem(zz + nz, nz), far)

    def place(yy, zz):
        return (member_of(yy, zz), lax.rem(lax.rem(zz + nz, nz), far) * NEAR + near_at)

    def near_peer(k):
        return (m, s - near_at + lax.rem(near_at + k, NEAR))

    def far_peer(k):
        return (m, lax.rem(far_at + k, far) * NEAR + near_at)

    def z_peer(k):
        return place(y, z + k)

    def y_peer(k):
        return place(y + k, z)

    quarter = nz // 4

    def met(n):
        pair, turn = lax.div(n, 4), lax.rem(n, 4)
        dy = ny // 2 - pair + lax.rem(turn, 2) * (2 * pair - ny + 1)
        dz = quarter * (1 - 2 * lax.rem(lax.div(turn + 1, 2), 2))
        return place(y + dy, z + dz)

    barrier = pltpu.get_barrier_semaphore()

    def greet(peer):
        pl.semaphore_signal(barrier, inc=1, device_id=peer, device_id_type=MESH)

    def greet_all(peer, start, count):
        def one(k, carry):
            greet(peer(k))
            return carry

        lax.fori_loop(start, count, one, 0)

    greet_all(met, 0, members)
    greet_all(near_peer, 1, NEAR)
    greet_all(z_peer, 1, nz)
    greet_all(y_peer, 1, ny)
    own_copy = pltpu.make_async_copy(ens, own, local_sem.at[0])
    tgt_copy = pltpu.make_async_copy(tgt, tgt_rows, local_sem.at[1])
    cw_copy = pltpu.make_async_copy(cw_hbm, cw, local_sem.at[2])
    lat_copy = pltpu.make_async_copy(lat_hbm, lat, local_sem.at[3])
    lat_copy.start()
    cw_copy.start()
    own_copy.start()
    tgt_copy.start()

    pl.semaphore_wait(barrier, members + (NEAR - 1) + (nz - 1) + (ny - 1))

    def push(src, dst, send, recv, device):
        pltpu.make_async_remote_copy(
            src_ref=src,
            dst_ref=dst,
            send_sem=send,
            recv_sem=recv,
            device_id=device,
            device_id_type=MESH,
        ).start()

    def exchange(source, landing, send, recv, chunk):
        def one(n, carry):
            device = met(n)
            j = device[0]
            push(source(j), landing(m), send.at[chunk, j], recv.at[chunk, m], device)
            return carry

        lax.fori_loop(0, members, one, 0)

    def arrived(ref, sem):
        pltpu.make_async_copy(ref, ref, sem).wait()

    def share(box, at, send, recv, peer, count):
        def one(k, carry):
            push(box.at[at], box.at[at], send.at[k], recv.at[at], peer(k))
            return carry

        lax.fori_loop(1, count, one, 0)

    def collect(box, at, send, recv, count):
        def one(k, carry):
            j = lax.rem(at + k, count)
            pltpu.make_async_copy(box.at[j], box.at[j], recv.at[j]).wait()
            pltpu.make_async_copy(box.at[at], box.at[at], send.at[k]).wait()
            return carry

        lax.fori_loop(1, count, one, 0)
        total = box[0]
        for j in range(1, count):
            total = total + box[j]
        return total

    for chunk, (first, size) in enumerate(CHUNKS):
        exchange(
            lambda j: ens.at[pl.ds(j * per + first, size)],
            lambda i: gat.at[i, pl.ds(first, size)],
            send1,
            recv1,
            chunk,
        )

    def along_rows(row):
        square = jnp.broadcast_to(row, (blocks, blocks))
        diagonal = lax.broadcasted_iota(jnp.int32, (blocks, blocks), 0) == lax.broadcasted_iota(
            jnp.int32, (blocks, blocks), 1
        )
        column = jnp.sum(jnp.where(diagonal, square, 0.0), axis=1, keepdims=True)
        return jnp.broadcast_to(column, (blocks, BLOCK))

    lat_copy.wait()
    latitude = ((lat[...].astype(jnp.float32) + 0.5) / BANDS - 0.5) * math.pi
    block_area = jnp.cos(latitude)
    box_row[0] = block_area
    push(box_row.at[0], box_row.at[1], row_sem.at[0], row_sem.at[1], place(y, z + quarter))
    wide = along_rows(block_area)
    for g in range(groups):
        area[g] = wide[g * ROWS : (g + 1) * ROWS]
    box_a1[near_at] = jnp.sum(wide, axis=0, keepdims=True)
    share(box_a1, near_at, send_a1, recv_a1, near_peer, NEAR)

    cw_copy.wait()
    own_copy.wait()
    tgt_copy.wait()

    def skill_rows(first, rows, acc):
        def group(g, acc):
            tiles = [
                tgt_rows[
                    pl.ds(first, rows), pl.ds(pl.multiple_of((g * ROWS + i) * BLOCK, BLOCK), BLOCK)
                ]
                for i in range(ROWS)
            ]
            part = jnp.zeros((ROWS, BLOCK), jnp.float32)
            for r in range(rows):
                u = (first + r) * groups + g
                skill = own[u] - jnp.concatenate([tile[r : r + 1] for tile in tiles], axis=0)
                sgn[u] = jnp.clip(skill * 64.0, -1.0, 1.0) * 0.0625
                part = part + cw[first + r] * jnp.abs(skill)
            return acc + area[g] * part

        return lax.fori_loop(0, groups, group, acc)

    def skill_octet(k, acc):
        return skill_rows(pl.multiple_of(k * 8, 8), 8, acc)

    octets = channels // 8
    skill_sum = lax.fori_loop(0, octets, skill_octet, jnp.zeros((ROWS, BLOCK), jnp.float32))
    if channels % 8:
        skill_sum = skill_rows(octets * 8, channels % 8, skill_sum)

    arrived(box_row.at[1], row_sem.at[1])
    met_wide = along_rows(box_row[1])
    for g in range(groups):
        met_area[g] = met_wide[g * ROWS : (g + 1) * ROWS]
    count = float(members)

    def pairs(k, acc):
        last = jnp.minimum(2 * k + 1, per - 1)
        counted = jnp.where(2 * k + 1 < per, 1.0, 0.0)
        values = [
            jnp.concatenate([gat[j, 2 * k], gat[j, last]], axis=0) * 64.0 for j in range(members)
        ]
        signs = [jnp.zeros_like(values[0]) for j in range(members)]
        for a in range(members):
            for b in range(a + 1, members):
                d = jnp.clip(values[a] - values[b], -1.0, 1.0)
                signs[a] = signs[a] + d
                signs[b] = signs[b] - d
        dot = values[0] * signs[0]
        for j in range(1, members):
            dot = dot + values[j] * signs[j]
        for i, part, factor in ((2 * k, slice(0, ROWS), 1.0), (last, slice(ROWS, 2 * ROWS), counted)):
            for j in range(members):
                sums[j, i] = signs[j][part]
            u = m * per + i
            acc = acc + (met_area[lax.rem(u, groups)] * (cw[lax.div(u, groups)] * factor)) * dot[part]
        return acc

    def wait_chunk(chunk):
        first, size = CHUNKS[chunk]

        def one(j, carry):
            arrived(gat.at[j, pl.ds(first, size)], recv1.at[chunk, j])
            return carry

        lax.fori_loop(0, members, one, 0)

    def send_back(chunk):
        first, size = CHUNKS[chunk]
        exchange(
            lambda j: sums.at[j, pl.ds(first, size)],
            lambda i: back.at[pl.ds(i * per + first, size)],
            send2,
            recv2,
            chunk,
        )

    middle = CHUNKS[1][0] // 2

    def chunk_step(chunk, acc):
        @pl.when(chunk == 0)
        def _():
            wait_chunk(0)
            area_near = collect(box_a1, near_at, send_a1, recv_a1, NEAR)
            box_a2[far_at] = area_near
            share(box_a2, far_at, send_a2, recv_a2, far_peer, far)

        @pl.when(chunk == 1)
        def _():
            send_back(0)
            wait_chunk(1)

        return lax.fori_loop(chunk * middle, middle + chunk * ((per + 1) // 2 - middle), pairs, acc)

    spread_sum = lax.fori_loop(0, len(CHUNKS), chunk_step, jnp.zeros((ROWS, BLOCK), jnp.float32))
    mine = skill_sum * (1.0 / count) - spread_sum * (1.0 / (64.0 * count * (count - 1.0)))
    box_l1[near_at] = jnp.sum(mine, axis=0, keepdims=True)
    share(box_l1, near_at, send_l1, recv_l1, near_peer, NEAR)
    send_back(1)

    loss_near = collect(box_l1, near_at, send_l1, recv_l1, NEAR)
    box_l2[z] = loss_near
    share(box_l2, z, send_l2, recv_l2, z_peer, nz)
    loss_z = collect(box_l2, z, send_l2, recv_l2, nz)
    box_l3[y] = loss_z
    share(box_l3, y, send_l3, recv_l3, y_peer, ny)

    area_all = collect(box_a2, far_at, send_a2, recv_a2, far)
    area_total = jnp.sum(area_all, axis=1, keepdims=True)
    points = float(units * ROWS * BLOCK // channels * spaces)
    factor = jnp.broadcast_to(points / area_total, (ROWS, BLOCK))

    def scale_channel(c, carry):
        weight = cw[c]
        for g in range(groups):
            u = c * groups + g
            scale = area[g] * factor * weight
            sgn[u] = sgn[u] * scale
            scl[u] = scale * (1.0 / (count * (count - 1.0)))
        return carry

    lax.fori_loop(0, channels, scale_channel, 0)

    def finish(j, source, first, size):
        part = pl.ds(j * per + first, size)
        result[part] = sgn[part] - scl[part] * source


    for chunk, (first, size) in enumerate(CHUNKS):

        def take_back(n, carry):
            j = met(n)[0]
            part = back.at[pl.ds(j * per + first, size)]
            arrived(part, recv2.at[chunk, j])
            finish(j, part[...], first, size)
            return carry

        lax.fori_loop(0, members, take_back, 0)

    loss_all = collect(box_l3, y, send_l3, recv_l3, ny)
    loss_total = jnp.sum(loss_all, axis=1, keepdims=True)
    result[units] = jnp.broadcast_to(loss_total / (area_total * float(channels)), (ROWS, BLOCK))

    for chunk, (first, size) in enumerate(CHUNKS):

        def wait_sent(j, carry):
            arrived(gat.at[j, pl.ds(first, size)], send1.at[chunk, j])
            arrived(sums.at[j, pl.ds(first, size)], send2.at[chunk, j])
            return carry

        lax.fori_loop(0, members, wait_sent, 0)
    arrived(box_row.at[0], row_sem.at[0])


def deliver(result, grad, loss, last, sem):
    grad_copy = pltpu.make_async_copy(result.at[pl.ds(0, grad.shape[0])], grad, sem.at[0])
    grad_copy.start()
    last[...] = result[grad.shape[0], 0:1, 0:1]
    loss_copy = pltpu.make_async_copy(last, loss, sem.at[1])
    loss_copy.start()
    loss_copy.wait()
    grad_copy.wait()


def local(members, spaces, ensemble, target, chan_weight, lat_band):
    channels, points = target.shape
    units = channels * points // (ROWS * BLOCK)
    per = units // members
    far = spaces // NEAR
    ny = members // PLANES
    nz = far * PLANES
    f32 = jnp.float32
    dma = pltpu.SemaphoreType.DMA
    vmem = pl.BlockSpec(memory_space=pltpu.VMEM)
    hbm = pl.BlockSpec(memory_space=pltpu.HBM)
    whole = pltpu.VMEM((units, ROWS, BLOCK), f32)
    slabs = pltpu.VMEM((members, per, ROWS, BLOCK), f32)

    def box(n):
        return pltpu.VMEM((n, 1, BLOCK), f32)

    def in_hbm(x):
        return pltpu.with_memory_space_constraint(x, pltpu.HBM)

    def body(*refs):
        kernel(members, spaces, *refs)

    result = pl.pallas_call(
        body,
        out_shape=jax.ShapeDtypeStruct((units + 1, ROWS, BLOCK), f32),
        in_specs=[hbm] * 4,
        out_specs=vmem,
        scratch_shapes=[
            pltpu.SMEM(chan_weight.shape, f32),
            pltpu.VMEM((1, lat_band.shape[0]), lat_band.dtype),
            whole,
            pltpu.VMEM((channels, points), f32),
            whole,
            whole,
            slabs,
            slabs,
            whole,
            pltpu.VMEM((points // (ROWS * BLOCK), ROWS, BLOCK), f32),
            pltpu.VMEM((points // (ROWS * BLOCK), ROWS, BLOCK), f32),
            pltpu.VMEM((2, 1, lat_band.shape[0]), f32),
            box(NEAR),
            box(far),
            box(NEAR),
            box(nz),
            box(ny),
            dma((4,)),
            dma((2,)),
            dma((len(CHUNKS), members)),
            dma((len(CHUNKS), members)),
            dma((len(CHUNKS), members)),
            dma((len(CHUNKS), members)),
            dma((NEAR,)),
            dma((NEAR,)),
            dma((far,)),
            dma((far,)),
            dma((NEAR,)),
            dma((NEAR,)),
            dma((nz,)),
            dma((nz,)),
            dma((ny,)),
            dma((ny,)),
        ],
        compiler_params=pltpu.CompilerParams(
            collective_id=0, has_side_effects=True, vmem_limit_bytes=32 * 1024 * 1024
        ),
    )(
        in_hbm(ensemble.reshape(units, ROWS, BLOCK)),
        in_hbm(target),
        in_hbm(chan_weight),
        in_hbm(lat_band.reshape(1, -1)),
    )
    grad, loss = pl.pallas_call(
        deliver,
        out_shape=(
            jax.ShapeDtypeStruct((units, ROWS, BLOCK), f32),
            jax.ShapeDtypeStruct((1, 1), f32),
        ),
        in_specs=[vmem],
        out_specs=(hbm, hbm),
        scratch_shapes=[pltpu.VMEM((1, 1), f32), dma((2,))],
        compiler_params=pltpu.CompilerParams(vmem_limit_bytes=32 * 1024 * 1024),
    )(result)
    return loss.reshape(()), grad.reshape(1, channels, points)


def solution(mesh):
    members, spaces = mesh.shape["member"], mesh.shape["space"]

    def step(*args):
        return local(members, spaces, *args)

    in_specs = (P("member", None, "space"), P(None, "space"), P(), P("space"))
    out_specs = (P(), P("member", None, "space"))
    return jax.shard_map(step, mesh=mesh, in_specs=in_specs, out_specs=out_specs, check_vma=False)
```

```python
import math

import jax
import jax.numpy as jnp
from jax import lax
from jax.experimental import pallas as pl
from jax.experimental.pallas import tpu as pltpu
from jax.sharding import PartitionSpec as P

BLOCK = 128
BANDS = 720
MESH = pl.DeviceIdType.MESH
ROWS = 4
NEAR = 8
PLANES = 2
CHUNKS = ((0, 6), (6, 7))


def kernel(
    members,
    spaces,
    ens,
    tgt,
    cw_hbm,
    lat_hbm,
    result,
    cw,
    lat,
    own,
    tgt_rows,
    sgn,
    scl,
    gat,
    sums,
    back,
    area,
    met_area,
    box_row,
    box_a1,
    box_a2,
    box_l1,
    box_l2,
    box_l3,
    local_sem,
    row_sem,
    send1,
    recv1,
    send2,
    recv2,
    send_a1,
    recv_a1,
    send_a2,
    recv_a2,
    send_l1,
    recv_l1,
    send_l2,
    recv_l2,
    send_l3,
    recv_l3,
):
    m = lax.axis_index("member")
    s = lax.axis_index("space")
    far = spaces // NEAR
    ny = members // PLANES
    nz = far * PLANES
    near_at = lax.rem(s, NEAR)
    far_at = lax.div(s, NEAR)
    y = lax.div(m, PLANES)
    z = lax.rem(m, PLANES) * far + far_at
    units = ens.shape[0]
    per = units // members
    channels = tgt.shape[0]
    groups = units // channels
    blocks = groups * ROWS

    def member_of(yy, zz):
        return lax.rem(yy + ny, ny) * PLANES + lax.div(lax.rem(zz + nz, nz), far)

    def place(yy, zz):
        return (member_of(yy, zz), lax.rem(lax.rem(zz + nz, nz), far) * NEAR + near_at)

    def near_peer(k):
        return (m, s - near_at + lax.rem(near_at + k, NEAR))

    def far_peer(k):
        return (m, lax.rem(far_at + k, far) * NEAR + near_at)

    def z_peer(k):
        return place(y, z + k)

    def y_peer(k):
        return place(y + k, z)

    quarter = nz // 4

    def met(n):
        pair, turn = lax.div(n, 4), lax.rem(n, 4)
        dy = ny // 2 - pair + lax.rem(turn, 2) * (2 * pair - ny + 1)
        dz = quarter * (1 - 2 * lax.rem(lax.div(turn + 1, 2), 2))
        return place(y + dy, z + dz)

    barrier = pltpu.get_barrier_semaphore()

    def greet(peer):
        pl.semaphore_signal(barrier, inc=1, device_id=peer, device_id_type=MESH)

    def greet_all(peer, start, count):
        def one(k, carry):
            greet(peer(k))
            return carry

        lax.fori_loop(start, count, one, 0)

    greet_all(met, 0, members)
    greet_all(near_peer, 1, NEAR)
    greet_all(z_peer, 1, nz)
    greet_all(y_peer, 1, ny)
    own_copy = pltpu.make_async_copy(ens, own, local_sem.at[0])
    tgt_copy = pltpu.make_async_copy(tgt, tgt_rows, local_sem.at[1])
    cw_copy = pltpu.make_async_copy(cw_hbm, cw, local_sem.at[2])
    lat_copy = pltpu.make_async_copy(lat_hbm, lat, local_sem.at[3])
    lat_copy.start()
    cw_copy.start()
    own_copy.start()
    tgt_copy.start()

    pl.semaphore_wait(barrier, members + (NEAR - 1) + (nz - 1) + (ny - 1))

    def push(src, dst, send, recv, device):
        pltpu.make_async_remote_copy(
            src_ref=src,
            dst_ref=dst,
            send_sem=send,
            recv_sem=recv,
            device_id=device,
            device_id_type=MESH,
        ).start()

    def exchange(source, landing, send, recv, chunk):
        def one(n, carry):
            device = met(n)
            j = device[0]
            push(source(j), landing(m), send.at[chunk, j], recv.at[chunk, m], device)
            return carry

        lax.fori_loop(0, members, one, 0)

    def arrived(ref, sem):
        pltpu.make_async_copy(ref, ref, sem).wait()

    def share(box, at, send, recv, peer, count):
        def one(k, carry):
            push(box.at[at], box.at[at], send.at[k], recv.at[at], peer(k))
            return carry

        lax.fori_loop(1, count, one, 0)

    def collect(box, at, send, recv, count):
        def one(k, carry):
            j = lax.rem(at + k, count)
            pltpu.make_async_copy(box.at[j], box.at[j], recv.at[j]).wait()
            pltpu.make_async_copy(box.at[at], box.at[at], send.at[k]).wait()
            return carry

        lax.fori_loop(1, count, one, 0)
        total = box[0]
        for j in range(1, count):
            total = total + box[j]
        return total

    for chunk, (first, size) in enumerate(CHUNKS):
        exchange(
            lambda j: ens.at[pl.ds(j * per + first, size)],
            lambda i: gat.at[i, pl.ds(first, size)],
            send1,
            recv1,
            chunk,
        )

    def along_rows(row):
        square = jnp.broadcast_to(row, (blocks, blocks))
        diagonal = lax.broadcasted_iota(jnp.int32, (blocks, blocks), 0) == lax.broadcasted_iota(
            jnp.int32, (blocks, blocks), 1
        )
        column = jnp.sum(jnp.where(diagonal, square, 0.0), axis=1, keepdims=True)
        return jnp.broadcast_to(column, (blocks, BLOCK))

    lat_copy.wait()
    latitude = ((lat[...].astype(jnp.float32) + 0.5) / BANDS - 0.5) * math.pi
    block_area = jnp.cos(latitude)
    box_row[0] = block_area
    push(box_row.at[0], box_row.at[1], row_sem.at[0], row_sem.at[1], place(y, z + quarter))
    wide = along_rows(block_area)
    for g in range(groups):
        area[g] = wide[g * ROWS : (g + 1) * ROWS]
    box_a1[near_at] = jnp.sum(wide, axis=0, keepdims=True)
    share(box_a1, near_at, send_a1, recv_a1, near_peer, NEAR)

    cw_copy.wait()
    own_copy.wait()
    tgt_copy.wait()

    def skill_rows(first, rows, acc):
        def group(g, acc):
            tiles = [
                tgt_rows[
                    pl.ds(first, rows), pl.ds(pl.multiple_of((g * ROWS + i) * BLOCK, BLOCK), BLOCK)
                ]
                for i in range(ROWS)
            ]
            part = jnp.zeros((ROWS, BLOCK), jnp.float32)
            for r in range(rows):
                u = (first + r) * groups + g
                skill = own[u] - jnp.concatenate([tile[r : r + 1] for tile in tiles], axis=0)
                sgn[u] = jnp.clip(skill * 64.0, -1.0, 1.0) * 0.0625
                part = part + cw[first + r] * jnp.abs(skill)
            return acc + area[g] * part

        return lax.fori_loop(0, groups, group, acc)

    def skill_octet(k, acc):
        return skill_rows(pl.multiple_of(k * 8, 8), 8, acc)

    octets = channels // 8
    skill_sum = lax.fori_loop(0, octets, skill_octet, jnp.zeros((ROWS, BLOCK), jnp.float32))
    if channels % 8:
        skill_sum = skill_rows(octets * 8, channels % 8, skill_sum)

    arrived(box_row.at[1], row_sem.at[1])
    met_wide = along_rows(box_row[1])
    for g in range(groups):
        met_area[g] = met_wide[g * ROWS : (g + 1) * ROWS]
    count = float(members)

    def pairs(k, acc):
        last = jnp.minimum(2 * k + 1, per - 1)
        counted = jnp.where(2 * k + 1 < per, 1.0, 0.0)
        values = [
            jnp.concatenate([gat[j, 2 * k], gat[j, last]], axis=0) * 64.0 for j in range(members)
        ]
        signs = [jnp.zeros_like(values[0]) for j in range(members)]
        for a in range(members):
            for b in range(a + 1, members):
                d = jnp.clip(values[a] - values[b], -1.0, 1.0)
                signs[a] = signs[a] + d
                signs[b] = signs[b] - d
        dot = values[0] * signs[0]
        for j in range(1, members):
            dot = dot + values[j] * signs[j]
        for i, part, factor in ((2 * k, slice(0, ROWS), 1.0), (last, slice(ROWS, 2 * ROWS), counted)):
            for j in range(members):
                sums[j, i] = signs[j][part]
            u = m * per + i
            acc = acc + (met_area[lax.rem(u, groups)] * (cw[lax.div(u, groups)] * factor)) * dot[part]
        return acc

    def wait_chunk(chunk):
        first, size = CHUNKS[chunk]

        def one(j, carry):
            arrived(gat.at[j, pl.ds(first, size)], recv1.at[chunk, j])
            return carry

        lax.fori_loop(0, members, one, 0)

    def send_back(chunk):
        first, size = CHUNKS[chunk]
        exchange(
            lambda j: sums.at[j, pl.ds(first, size)],
            lambda i: back.at[pl.ds(i * per + first, size)],
            send2,
            recv2,
            chunk,
        )

    middle = CHUNKS[1][0] // 2

    def chunk_step(chunk, acc):
        @pl.when(chunk == 0)
        def _():
            wait_chunk(0)
            area_near = collect(box_a1, near_at, send_a1, recv_a1, NEAR)
            box_a2[far_at] = area_near
            share(box_a2, far_at, send_a2, recv_a2, far_peer, far)

        @pl.when(chunk == 1)
        def _():
            send_back(0)
            wait_chunk(1)

        return lax.fori_loop(chunk * middle, middle + chunk * ((per + 1) // 2 - middle), pairs, acc)

    spread_sum = lax.fori_loop(0, len(CHUNKS), chunk_step, jnp.zeros((ROWS, BLOCK), jnp.float32))
    mine = skill_sum * (1.0 / count) - spread_sum * (1.0 / (64.0 * count * (count - 1.0)))
    box_l1[z] = jnp.sum(mine, axis=0, keepdims=True)
    share(box_l1, z, send_l1, recv_l1, z_peer, nz)
    send_back(1)

    loss_z = collect(box_l1, z, send_l1, recv_l1, nz)
    box_l2[y] = loss_z
    share(box_l2, y, send_l2, recv_l2, y_peer, ny)
    loss_y = collect(box_l2, y, send_l2, recv_l2, ny)
    box_l3[near_at] = loss_y
    share(box_l3, near_at, send_l3, recv_l3, near_peer, NEAR)

    area_all = collect(box_a2, far_at, send_a2, recv_a2, far)
    area_total = jnp.sum(area_all, axis=1, keepdims=True)
    points = float(units * ROWS * BLOCK // channels * spaces)
    factor = jnp.broadcast_to(points / area_total, (ROWS, BLOCK))

    def scale_channel(c, carry):
        weight = cw[c]
        for g in range(groups):
            u = c * groups + g
            scale = area[g] * factor * weight
            sgn[u] = sgn[u] * scale
            scl[u] = scale * (1.0 / (count * (count - 1.0)))
        return carry

    lax.fori_loop(0, channels, scale_channel, 0)

    def finish(j, source, first, size):
        part = pl.ds(j * per + first, size)
        result[part] = sgn[part] - scl[part] * source


    for chunk, (first, size) in enumerate(CHUNKS):

        def take_back(n, carry):
            j = met(n)[0]
            part = back.at[pl.ds(j * per + first, size)]
            arrived(part, recv2.at[chunk, j])
            finish(j, part[...], first, size)
            return carry

        lax.fori_loop(0, members, take_back, 0)

    loss_all = collect(box_l3, near_at, send_l3, recv_l3, NEAR)
    loss_total = jnp.sum(loss_all, axis=1, keepdims=True)
    result[units] = jnp.broadcast_to(loss_total / (area_total * float(channels)), (ROWS, BLOCK))

    for chunk, (first, size) in enumerate(CHUNKS):

        def wait_sent(j, carry):
            arrived(gat.at[j, pl.ds(first, size)], send1.at[chunk, j])
            arrived(sums.at[j, pl.ds(first, size)], send2.at[chunk, j])
            return carry

        lax.fori_loop(0, members, wait_sent, 0)
    arrived(box_row.at[0], row_sem.at[0])


def deliver(result, grad, loss, last, sem):
    grad_copy = pltpu.make_async_copy(result.at[pl.ds(0, grad.shape[0])], grad, sem.at[0])
    grad_copy.start()
    last[...] = result[grad.shape[0], 0:1, 0:1]
    loss_copy = pltpu.make_async_copy(last, loss, sem.at[1])
    loss_copy.start()
    loss_copy.wait()
    grad_copy.wait()


def local(members, spaces, ensemble, target, chan_weight, lat_band):
    channels, points = target.shape
    units = channels * points // (ROWS * BLOCK)
    per = units // members
    far = spaces // NEAR
    ny = members // PLANES
    nz = far * PLANES
    f32 = jnp.float32
    dma = pltpu.SemaphoreType.DMA
    vmem = pl.BlockSpec(memory_space=pltpu.VMEM)
    hbm = pl.BlockSpec(memory_space=pltpu.HBM)
    whole = pltpu.VMEM((units, ROWS, BLOCK), f32)
    slabs = pltpu.VMEM((members, per, ROWS, BLOCK), f32)

    def box(n):
        return pltpu.VMEM((n, 1, BLOCK), f32)

    def in_hbm(x):
        return pltpu.with_memory_space_constraint(x, pltpu.HBM)

    def body(*refs):
        kernel(members, spaces, *refs)

    result = pl.pallas_call(
        body,
        out_shape=jax.ShapeDtypeStruct((units + 1, ROWS, BLOCK), f32),
        in_specs=[hbm] * 4,
        out_specs=vmem,
        scratch_shapes=[
            pltpu.SMEM(chan_weight.shape, f32),
            pltpu.VMEM((1, lat_band.shape[0]), lat_band.dtype),
            whole,
            pltpu.VMEM((channels, points), f32),
            whole,
            whole,
            slabs,
            slabs,
            whole,
            pltpu.VMEM((points // (ROWS * BLOCK), ROWS, BLOCK), f32),
            pltpu.VMEM((points // (ROWS * BLOCK), ROWS, BLOCK), f32),
            pltpu.VMEM((2, 1, lat_band.shape[0]), f32),
            box(NEAR),
            box(far),
            box(nz),
            box(ny),
            box(NEAR),
            dma((4,)),
            dma((2,)),
            dma((len(CHUNKS), members)),
            dma((len(CHUNKS), members)),
            dma((len(CHUNKS), members)),
            dma((len(CHUNKS), members)),
            dma((NEAR,)),
            dma((NEAR,)),
            dma((far,)),
            dma((far,)),
            dma((nz,)),
            dma((nz,)),
            dma((ny,)),
            dma((ny,)),
            dma((NEAR,)),
            dma((NEAR,)),
        ],
        compiler_params=pltpu.CompilerParams(
            collective_id=0, has_side_effects=True, vmem_limit_bytes=32 * 1024 * 1024
        ),
    )(
        in_hbm(ensemble.reshape(units, ROWS, BLOCK)),
        in_hbm(target),
        in_hbm(chan_weight),
        in_hbm(lat_band.reshape(1, -1)),
    )
    grad, loss = pl.pallas_call(
        deliver,
        out_shape=(
            jax.ShapeDtypeStruct((units, ROWS, BLOCK), f32),
            jax.ShapeDtypeStruct((1, 1), f32),
        ),
        in_specs=[vmem],
        out_specs=(hbm, hbm),
        scratch_shapes=[pltpu.VMEM((1, 1), f32), dma((2,))],
        compiler_params=pltpu.CompilerParams(vmem_limit_bytes=32 * 1024 * 1024),
    )(result)
    return loss.reshape(()), grad.reshape(1, channels, points)


def solution(mesh):
    members, spaces = mesh.shape["member"], mesh.shape["space"]

    def step(*args):
        return local(members, spaces, *args)

    in_specs = (P("member", None, "space"), P(None, "space"), P(), P("space"))
    out_specs = (P(), P("member", None, "space"))
    return jax.shard_map(step, mesh=mesh, in_specs=in_specs, out_specs=out_specs, check_vma=False)
```

```python
import math

import jax
import jax.numpy as jnp
from jax import lax
from jax.experimental import pallas as pl
from jax.experimental.pallas import tpu as pltpu
from jax.sharding import PartitionSpec as P

BLOCK = 128
BANDS = 720
MESH = pl.DeviceIdType.MESH
ROWS = 4
NEAR = 8
PLANES = 2
CHUNKS = ((0, 6), (6, 7))


def kernel(
    members,
    spaces,
    ens,
    tgt,
    cw_hbm,
    lat_hbm,
    result,
    cw,
    lat,
    own,
    tgt_rows,
    sgn,
    scl,
    gat,
    sums,
    back,
    area,
    met_area,
    box_row,
    box_a1,
    box_a2,
    box_l1,
    box_l2,
    box_l3,
    local_sem,
    row_sem,
    send1,
    recv1,
    send2,
    recv2,
    send_a1,
    recv_a1,
    send_a2,
    recv_a2,
    send_l1,
    recv_l1,
    send_l2,
    recv_l2,
    send_l3,
    recv_l3,
):
    m = lax.axis_index("member")
    s = lax.axis_index("space")
    far = spaces // NEAR
    ny = members // PLANES
    nz = far * PLANES
    near_at = lax.rem(s, NEAR)
    far_at = lax.div(s, NEAR)
    y = lax.div(m, PLANES)
    z = lax.rem(m, PLANES) * far + far_at
    units = ens.shape[0]
    per = units // members
    channels = tgt.shape[0]
    groups = units // channels
    blocks = groups * ROWS

    def member_of(yy, zz):
        return lax.rem(yy + ny, ny) * PLANES + lax.div(lax.rem(zz + nz, nz), far)

    def place(yy, zz):
        return (member_of(yy, zz), lax.rem(lax.rem(zz + nz, nz), far) * NEAR + near_at)

    def near_peer(k):
        return (m, s - near_at + lax.rem(near_at + k, NEAR))

    def far_peer(k):
        return (m, lax.rem(far_at + k, far) * NEAR + near_at)

    def z_peer(k):
        return place(y, z + k)

    def y_peer(k):
        return place(y + k, z)

    quarter = nz // 4

    def met(n):
        pair, turn = lax.div(n, 4), lax.rem(n, 4)
        dy = ny // 2 - pair + lax.rem(turn, 2) * (2 * pair - ny + 1)
        dz = quarter * (1 - 2 * lax.rem(lax.div(turn + 1, 2), 2))
        return place(y + dy, z + dz)

    barrier = pltpu.get_barrier_semaphore()

    def greet(peer):
        pl.semaphore_signal(barrier, inc=1, device_id=peer, device_id_type=MESH)

    def greet_all(peer, start, count):
        def one(k, carry):
            greet(peer(k))
            return carry

        lax.fori_loop(start, count, one, 0)

    greet_all(met, 0, members)
    greet_all(near_peer, 1, NEAR)
    greet_all(z_peer, 1, nz)
    greet_all(y_peer, 1, ny)
    own_copy = pltpu.make_async_copy(ens, own, local_sem.at[0])
    tgt_copy = pltpu.make_async_copy(tgt, tgt_rows, local_sem.at[1])
    cw_copy = pltpu.make_async_copy(cw_hbm, cw, local_sem.at[2])
    lat_copy = pltpu.make_async_copy(lat_hbm, lat, local_sem.at[3])
    lat_copy.start()
    cw_copy.start()
    own_copy.start()
    tgt_copy.start()

    pl.semaphore_wait(barrier, members + (NEAR - 1) + (nz - 1) + (ny - 1))

    def push(src, dst, send, recv, device):
        pltpu.make_async_remote_copy(
            src_ref=src,
            dst_ref=dst,
            send_sem=send,
            recv_sem=recv,
            device_id=device,
            device_id_type=MESH,
        ).start()

    def exchange(source, landing, send, recv, chunk, start, stop):
        def one(n, carry):
            device = met(n)
            j = device[0]
            push(source(j), landing(m), send.at[chunk, j], recv.at[chunk, m], device)
            return carry

        lax.fori_loop(start, stop, one, 0)

    def arrived(ref, sem):
        pltpu.make_async_copy(ref, ref, sem).wait()

    def share(box, at, send, recv, peer, count):
        def one(k, carry):
            push(box.at[at], box.at[at], send.at[k], recv.at[at], peer(k))
            return carry

        lax.fori_loop(1, count, one, 0)

    def collect(box, at, send, recv, count):
        def one(k, carry):
            j = lax.rem(at + k, count)
            pltpu.make_async_copy(box.at[j], box.at[j], recv.at[j]).wait()
            pltpu.make_async_copy(box.at[at], box.at[at], send.at[k]).wait()
            return carry

        lax.fori_loop(1, count, one, 0)
        total = box[0]
        for j in range(1, count):
            total = total + box[j]
        return total

    for chunk, (first, size) in enumerate(CHUNKS):
        exchange(
            lambda j: ens.at[pl.ds(j * per + first, size)],
            lambda i: gat.at[i, pl.ds(first, size)],
            send1,
            recv1,
            chunk,
            0,
            members,
        )

    def along_rows(row):
        square = jnp.broadcast_to(row, (blocks, blocks))
        diagonal = lax.broadcasted_iota(jnp.int32, (blocks, blocks), 0) == lax.broadcasted_iota(
            jnp.int32, (blocks, blocks), 1
        )
        column = jnp.sum(jnp.where(diagonal, square, 0.0), axis=1, keepdims=True)
        return jnp.broadcast_to(column, (blocks, BLOCK))

    lat_copy.wait()
    latitude = ((lat[...].astype(jnp.float32) + 0.5) / BANDS - 0.5) * math.pi
    block_area = jnp.cos(latitude)
    box_row[0] = block_area
    push(box_row.at[0], box_row.at[1], row_sem.at[0], row_sem.at[1], place(y, z + quarter))
    wide = along_rows(block_area)
    for g in range(groups):
        area[g] = wide[g * ROWS : (g + 1) * ROWS]
    box_a1[near_at] = jnp.sum(wide, axis=0, keepdims=True)
    share(box_a1, near_at, send_a1, recv_a1, near_peer, NEAR)

    cw_copy.wait()
    own_copy.wait()
    tgt_copy.wait()

    def skill_rows(first, rows, acc):
        def group(g, acc):
            tiles = [
                tgt_rows[
                    pl.ds(first, rows), pl.ds(pl.multiple_of((g * ROWS + i) * BLOCK, BLOCK), BLOCK)
                ]
                for i in range(ROWS)
            ]
            part = jnp.zeros((ROWS, BLOCK), jnp.float32)
            for r in range(rows):
                u = (first + r) * groups + g
                skill = own[u] - jnp.concatenate([tile[r : r + 1] for tile in tiles], axis=0)
                sgn[u] = jnp.clip(skill * 64.0, -1.0, 1.0) * 0.0625
                part = part + cw[first + r] * jnp.abs(skill)
            return acc + area[g] * part

        return lax.fori_loop(0, groups, group, acc)

    def skill_octet(k, acc):
        return skill_rows(pl.multiple_of(k * 8, 8), 8, acc)

    octets = channels // 8
    skill_sum = lax.fori_loop(0, octets, skill_octet, jnp.zeros((ROWS, BLOCK), jnp.float32))
    if channels % 8:
        skill_sum = skill_rows(octets * 8, channels % 8, skill_sum)

    arrived(box_row.at[1], row_sem.at[1])
    met_wide = along_rows(box_row[1])
    for g in range(groups):
        met_area[g] = met_wide[g * ROWS : (g + 1) * ROWS]
    count = float(members)

    def pairs(k, acc):
        last = jnp.minimum(2 * k + 1, per - 1)
        counted = jnp.where(2 * k + 1 < per, 1.0, 0.0)
        values = [
            jnp.concatenate([gat[j, 2 * k], gat[j, last]], axis=0) * 64.0 for j in range(members)
        ]
        signs = [jnp.zeros_like(values[0]) for j in range(members)]
        for a in range(members):
            for b in range(a + 1, members):
                d = jnp.clip(values[a] - values[b], -1.0, 1.0)
                signs[a] = signs[a] + d
                signs[b] = signs[b] - d
        dot = values[0] * signs[0]
        for j in range(1, members):
            dot = dot + values[j] * signs[j]
        for i, part, factor in ((2 * k, slice(0, ROWS), 1.0), (last, slice(ROWS, 2 * ROWS), counted)):
            for j in range(members):
                sums[j, i] = signs[j][part]
            u = m * per + i
            acc = acc + (met_area[lax.rem(u, groups)] * (cw[lax.div(u, groups)] * factor)) * dot[part]
        return acc

    def wait_chunk(chunk):
        first, size = CHUNKS[chunk]

        def one(j, carry):
            arrived(gat.at[j, pl.ds(first, size)], recv1.at[chunk, j])
            return carry

        lax.fori_loop(0, members, one, 0)

    def send_back(chunk, start, stop):
        first, size = CHUNKS[chunk]
        exchange(
            lambda j: sums.at[j, pl.ds(first, size)],
            lambda i: back.at[pl.ds(i * per + first, size)],
            send2,
            recv2,
            chunk,
            start,
            stop,
        )

    middle = CHUNKS[1][0] // 2

    def chunk_step(chunk, acc):
        @pl.when(chunk == 0)
        def _():
            wait_chunk(0)
            area_near = collect(box_a1, near_at, send_a1, recv_a1, NEAR)
            box_a2[far_at] = area_near
            share(box_a2, far_at, send_a2, recv_a2, far_peer, far)

        @pl.when(chunk == 1)
        def _():
            send_back(0, 0, members)
            wait_chunk(1)

        return lax.fori_loop(chunk * middle, middle + chunk * ((per + 1) // 2 - middle), pairs, acc)

    spread_sum = lax.fori_loop(0, len(CHUNKS), chunk_step, jnp.zeros((ROWS, BLOCK), jnp.float32))
    mine = skill_sum * (1.0 / count) - spread_sum * (1.0 / (64.0 * count * (count - 1.0)))
    box_l1[near_at] = jnp.sum(mine, axis=0, keepdims=True)
    share(box_l1, near_at, send_l1, recv_l1, near_peer, NEAR)
    send_back(1, 0, members // 2)
    loss_near = collect(box_l1, near_at, send_l1, recv_l1, NEAR)
    box_l2[z] = loss_near
    share(box_l2, z, send_l2, recv_l2, z_peer, nz)
    send_back(1, members // 2, members)
    loss_z = collect(box_l2, z, send_l2, recv_l2, nz)
    box_l3[y] = loss_z
    share(box_l3, y, send_l3, recv_l3, y_peer, ny)

    area_all = collect(box_a2, far_at, send_a2, recv_a2, far)
    area_total = jnp.sum(area_all, axis=1, keepdims=True)
    points = float(units * ROWS * BLOCK // channels * spaces)
    factor = jnp.broadcast_to(points / area_total, (ROWS, BLOCK))

    def scale_channel(c, carry):
        weight = cw[c]
        for g in range(groups):
            u = c * groups + g
            scale = area[g] * factor * weight
            sgn[u] = sgn[u] * scale
            scl[u] = scale * (1.0 / (count * (count - 1.0)))
        return carry

    lax.fori_loop(0, channels, scale_channel, 0)

    def finish(j, source, first, size):
        part = pl.ds(j * per + first, size)
        result[part] = sgn[part] - scl[part] * source


    for chunk, (first, size) in enumerate(CHUNKS):

        def take_back(n, carry):
            j = met(n)[0]
            part = back.at[pl.ds(j * per + first, size)]
            arrived(part, recv2.at[chunk, j])
            finish(j, part[...], first, size)
            return carry

        lax.fori_loop(0, members, take_back, 0)

    loss_all = collect(box_l3, y, send_l3, recv_l3, ny)
    loss_total = jnp.sum(loss_all, axis=1, keepdims=True)
    result[units] = jnp.broadcast_to(loss_total / (area_total * float(channels)), (ROWS, BLOCK))

    for chunk, (first, size) in enumerate(CHUNKS):

        def wait_sent(j, carry):
            arrived(gat.at[j, pl.ds(first, size)], send1.at[chunk, j])
            arrived(sums.at[j, pl.ds(first, size)], send2.at[chunk, j])
            return carry

        lax.fori_loop(0, members, wait_sent, 0)
    arrived(box_row.at[0], row_sem.at[0])


def deliver(result, grad, loss, last, sem):
    grad_copy = pltpu.make_async_copy(result.at[pl.ds(0, grad.shape[0])], grad, sem.at[0])
    grad_copy.start()
    last[...] = result[grad.shape[0], 0:1, 0:1]
    loss_copy = pltpu.make_async_copy(last, loss, sem.at[1])
    loss_copy.start()
    loss_copy.wait()
    grad_copy.wait()


def local(members, spaces, ensemble, target, chan_weight, lat_band):
    channels, points = target.shape
    units = channels * points // (ROWS * BLOCK)
    per = units // members
    far = spaces // NEAR
    ny = members // PLANES
    nz = far * PLANES
    f32 = jnp.float32
    dma = pltpu.SemaphoreType.DMA
    vmem = pl.BlockSpec(memory_space=pltpu.VMEM)
    hbm = pl.BlockSpec(memory_space=pltpu.HBM)
    whole = pltpu.VMEM((units, ROWS, BLOCK), f32)
    slabs = pltpu.VMEM((members, per, ROWS, BLOCK), f32)

    def box(n):
        return pltpu.VMEM((n, 1, BLOCK), f32)

    def in_hbm(x):
        return pltpu.with_memory_space_constraint(x, pltpu.HBM)

    def body(*refs):
        kernel(members, spaces, *refs)

    result = pl.pallas_call(
        body,
        out_shape=jax.ShapeDtypeStruct((units + 1, ROWS, BLOCK), f32),
        in_specs=[hbm] * 4,
        out_specs=vmem,
        scratch_shapes=[
            pltpu.SMEM(chan_weight.shape, f32),
            pltpu.VMEM((1, lat_band.shape[0]), lat_band.dtype),
            whole,
            pltpu.VMEM((channels, points), f32),
            whole,
            whole,
            slabs,
            slabs,
            whole,
            pltpu.VMEM((points // (ROWS * BLOCK), ROWS, BLOCK), f32),
            pltpu.VMEM((points // (ROWS * BLOCK), ROWS, BLOCK), f32),
            pltpu.VMEM((2, 1, lat_band.shape[0]), f32),
            box(NEAR),
            box(far),
            box(NEAR),
            box(nz),
            box(ny),
            dma((4,)),
            dma((2,)),
            dma((len(CHUNKS), members)),
            dma((len(CHUNKS), members)),
            dma((len(CHUNKS), members)),
            dma((len(CHUNKS), members)),
            dma((NEAR,)),
            dma((NEAR,)),
            dma((far,)),
            dma((far,)),
            dma((NEAR,)),
            dma((NEAR,)),
            dma((nz,)),
            dma((nz,)),
            dma((ny,)),
            dma((ny,)),
        ],
        compiler_params=pltpu.CompilerParams(
            collective_id=0, has_side_effects=True, vmem_limit_bytes=32 * 1024 * 1024
        ),
    )(
        in_hbm(ensemble.reshape(units, ROWS, BLOCK)),
        in_hbm(target),
        in_hbm(chan_weight),
        in_hbm(lat_band.reshape(1, -1)),
    )
    grad, loss = pl.pallas_call(
        deliver,
        out_shape=(
            jax.ShapeDtypeStruct((units, ROWS, BLOCK), f32),
            jax.ShapeDtypeStruct((1, 1), f32),
        ),
        in_specs=[vmem],
        out_specs=(hbm, hbm),
        scratch_shapes=[pltpu.VMEM((1, 1), f32), dma((2,))],
        compiler_params=pltpu.CompilerParams(vmem_limit_bytes=32 * 1024 * 1024),
    )(result)
    return loss.reshape(()), grad.reshape(1, channels, points)


def solution(mesh):
    members, spaces = mesh.shape["member"], mesh.shape["space"]

    def step(*args):
        return local(members, spaces, *args)

    in_specs = (P("member", None, "space"), P(None, "space"), P(), P("space"))
    out_specs = (P(), P("member", None, "space"))
    return jax.shard_map(step, mesh=mesh, in_specs=in_specs, out_specs=out_specs, check_vma=False)
```

```python
import math

import jax
import jax.numpy as jnp
from jax import lax
from jax.experimental import pallas as pl
from jax.experimental.pallas import tpu as pltpu
from jax.sharding import PartitionSpec as P

BLOCK = 128
BANDS = 720
MESH = pl.DeviceIdType.MESH
ROWS = 4
NEAR = 8
PLANES = 2
CHUNKS = ((0, 6), (6, 7))


def kernel(
    members,
    spaces,
    ens,
    tgt,
    cw_hbm,
    lat_hbm,
    result,
    cw,
    lat,
    own,
    tgt_rows,
    sgn,
    scl,
    gat,
    sums,
    back,
    area,
    met_area,
    box_row,
    box_a1,
    box_a2,
    box_l1,
    box_l2,
    box_l3,
    local_sem,
    row_sem,
    send1,
    recv1,
    send2,
    recv2,
    send_a1,
    recv_a1,
    send_a2,
    recv_a2,
    send_l1,
    recv_l1,
    send_l2,
    recv_l2,
    send_l3,
    recv_l3,
):
    m = lax.axis_index("member")
    s = lax.axis_index("space")
    far = spaces // NEAR
    ny = members // PLANES
    nz = far * PLANES
    near_at = lax.rem(s, NEAR)
    far_at = lax.div(s, NEAR)
    y = lax.div(m, PLANES)
    z = lax.rem(m, PLANES) * far + far_at
    units = ens.shape[0]
    per = units // members
    channels = tgt.shape[0]
    groups = units // channels
    blocks = groups * ROWS

    def member_of(yy, zz):
        return lax.rem(yy + ny, ny) * PLANES + lax.div(lax.rem(zz + nz, nz), far)

    def place(yy, zz):
        return (member_of(yy, zz), lax.rem(lax.rem(zz + nz, nz), far) * NEAR + near_at)

    def near_peer(k):
        return (m, s - near_at + lax.rem(near_at + k, NEAR))

    def far_peer(k):
        return (m, lax.rem(far_at + k, far) * NEAR + near_at)

    def z_peer(k):
        return place(y, z + k)

    def y_peer(k):
        return place(y + k, z)

    quarter = nz // 4

    def met(n):
        pair, turn = lax.div(n, 4), lax.rem(n, 4)
        dy = ny // 2 - pair + lax.rem(turn, 2) * (2 * pair - ny + 1)
        dz = quarter * (1 - 2 * lax.rem(lax.div(turn + 1, 2), 2))
        return place(y + dy, z + dz)

    barrier = pltpu.get_barrier_semaphore()

    own_copy = pltpu.make_async_copy(ens, own, local_sem.at[0])
    own_copy.start()

    def greet(peer):
        pl.semaphore_signal(barrier, inc=1, device_id=peer, device_id_type=MESH)

    def greet_all(peer, start, count):
        def one(k, carry):
            greet(peer(k))
            return carry

        lax.fori_loop(start, count, one, 0)

    greet_all(met, 0, members)
    greet_all(near_peer, 1, NEAR)
    greet_all(z_peer, 1, nz)
    greet_all(y_peer, 1, ny)
    tgt_copy = pltpu.make_async_copy(tgt, tgt_rows, local_sem.at[1])
    cw_copy = pltpu.make_async_copy(cw_hbm, cw, local_sem.at[2])
    lat_copy = pltpu.make_async_copy(lat_hbm, lat, local_sem.at[3])
    lat_copy.start()
    cw_copy.start()
    tgt_copy.start()

    pl.semaphore_wait(barrier, members + (NEAR - 1) + (nz - 1) + (ny - 1))

    def push(src, dst, send, recv, device):
        pltpu.make_async_remote_copy(
            src_ref=src,
            dst_ref=dst,
            send_sem=send,
            recv_sem=recv,
            device_id=device,
            device_id_type=MESH,
        ).start()

    def exchange(source, landing, send, recv, chunk):
        def one(n, carry):
            device = met(n)
            j = device[0]
            push(source(j), landing(m), send.at[chunk, j], recv.at[chunk, m], device)
            return carry

        lax.fori_loop(0, members, one, 0)

    def arrived(ref, sem):
        pltpu.make_async_copy(ref, ref, sem).wait()

    def share(box, at, send, recv, peer, count):
        def one(k, carry):
            push(box.at[at], box.at[at], send.at[k], recv.at[at], peer(k))
            return carry

        lax.fori_loop(1, count, one, 0)

    def collect(box, at, send, recv, count):
        def one(k, carry):
            j = lax.rem(at + k, count)
            pltpu.make_async_copy(box.at[j], box.at[j], recv.at[j]).wait()
            pltpu.make_async_copy(box.at[at], box.at[at], send.at[k]).wait()
            return carry

        lax.fori_loop(1, count, one, 0)
        total = box[0]
        for j in range(1, count):
            total = total + box[j]
        return total

    own_copy.wait()
    for chunk, (first, size) in enumerate(CHUNKS):
        exchange(
            lambda j: own.at[pl.ds(j * per + first, size)],
            lambda i: gat.at[i, pl.ds(first, size)],
            send1,
            recv1,
            chunk,
        )

    def along_rows(row):
        square = jnp.broadcast_to(row, (blocks, blocks))
        diagonal = lax.broadcasted_iota(jnp.int32, (blocks, blocks), 0) == lax.broadcasted_iota(
            jnp.int32, (blocks, blocks), 1
        )
        column = jnp.sum(jnp.where(diagonal, square, 0.0), axis=1, keepdims=True)
        return jnp.broadcast_to(column, (blocks, BLOCK))

    lat_copy.wait()
    latitude = ((lat[...].astype(jnp.float32) + 0.5) / BANDS - 0.5) * math.pi
    block_area = jnp.cos(latitude)
    box_row[0] = block_area
    push(box_row.at[0], box_row.at[1], row_sem.at[0], row_sem.at[1], place(y, z + quarter))
    wide = along_rows(block_area)
    for g in range(groups):
        area[g] = wide[g * ROWS : (g + 1) * ROWS]
    box_a1[near_at] = jnp.sum(wide, axis=0, keepdims=True)
    share(box_a1, near_at, send_a1, recv_a1, near_peer, NEAR)

    cw_copy.wait()
    tgt_copy.wait()

    def skill_rows(first, rows, acc):
        def group(g, acc):
            tiles = [
                tgt_rows[
                    pl.ds(first, rows), pl.ds(pl.multiple_of((g * ROWS + i) * BLOCK, BLOCK), BLOCK)
                ]
                for i in range(ROWS)
            ]
            part = jnp.zeros((ROWS, BLOCK), jnp.float32)
            for r in range(rows):
                u = (first + r) * groups + g
                skill = own[u] - jnp.concatenate([tile[r : r + 1] for tile in tiles], axis=0)
                sgn[u] = jnp.clip(skill * 64.0, -1.0, 1.0) * 0.0625
                part = part + cw[first + r] * jnp.abs(skill)
            return acc + area[g] * part

        return lax.fori_loop(0, groups, group, acc)

    def skill_octet(k, acc):
        return skill_rows(pl.multiple_of(k * 8, 8), 8, acc)

    octets = channels // 8
    skill_sum = lax.fori_loop(0, octets, skill_octet, jnp.zeros((ROWS, BLOCK), jnp.float32))
    if channels % 8:
        skill_sum = skill_rows(octets * 8, channels % 8, skill_sum)

    arrived(box_row.at[1], row_sem.at[1])
    met_wide = along_rows(box_row[1])
    for g in range(groups):
        met_area[g] = met_wide[g * ROWS : (g + 1) * ROWS]
    count = float(members)

    def pairs(k, acc):
        last = jnp.minimum(2 * k + 1, per - 1)
        counted = jnp.where(2 * k + 1 < per, 1.0, 0.0)
        values = [
            jnp.concatenate([gat[j, 2 * k], gat[j, last]], axis=0) * 64.0 for j in range(members)
        ]
        signs = [jnp.zeros_like(values[0]) for j in range(members)]
        for a in range(members):
            for b in range(a + 1, members):
                d = jnp.clip(values[a] - values[b], -1.0, 1.0)
                signs[a] = signs[a] + d
                signs[b] = signs[b] - d
        dot = values[0] * signs[0]
        for j in range(1, members):
            dot = dot + values[j] * signs[j]
        for i, part, factor in ((2 * k, slice(0, ROWS), 1.0), (last, slice(ROWS, 2 * ROWS), counted)):
            for j in range(members):
                sums[j, i] = signs[j][part]
            u = m * per + i
            acc = acc + (met_area[lax.rem(u, groups)] * (cw[lax.div(u, groups)] * factor)) * dot[part]
        return acc

    def wait_chunk(chunk):
        first, size = CHUNKS[chunk]

        def one(j, carry):
            arrived(gat.at[j, pl.ds(first, size)], recv1.at[chunk, j])
            return carry

        lax.fori_loop(0, members, one, 0)

    def send_back(chunk):
        first, size = CHUNKS[chunk]
        exchange(
            lambda j: sums.at[j, pl.ds(first, size)],
            lambda i: back.at[pl.ds(i * per + first, size)],
            send2,
            recv2,
            chunk,
        )

    middle = CHUNKS[1][0] // 2

    def chunk_step(chunk, acc):
        @pl.when(chunk == 0)
        def _():
            wait_chunk(0)
            area_near = collect(box_a1, near_at, send_a1, recv_a1, NEAR)
            box_a2[far_at] = area_near
            share(box_a2, far_at, send_a2, recv_a2, far_peer, far)

        @pl.when(chunk == 1)
        def _():
            send_back(0)
            wait_chunk(1)

        return lax.fori_loop(chunk * middle, middle + chunk * ((per + 1) // 2 - middle), pairs, acc)

    spread_sum = lax.fori_loop(0, len(CHUNKS), chunk_step, jnp.zeros((ROWS, BLOCK), jnp.float32))
    mine = skill_sum * (1.0 / count) - spread_sum * (1.0 / (64.0 * count * (count - 1.0)))
    box_l1[near_at] = jnp.sum(mine, axis=0, keepdims=True)
    share(box_l1, near_at, send_l1, recv_l1, near_peer, NEAR)
    send_back(1)

    loss_near = collect(box_l1, near_at, send_l1, recv_l1, NEAR)
    box_l2[z] = loss_near
    share(box_l2, z, send_l2, recv_l2, z_peer, nz)
    loss_z = collect(box_l2, z, send_l2, recv_l2, nz)
    box_l3[y] = loss_z
    share(box_l3, y, send_l3, recv_l3, y_peer, ny)

    area_all = collect(box_a2, far_at, send_a2, recv_a2, far)
    area_total = jnp.sum(area_all, axis=1, keepdims=True)
    points = float(units * ROWS * BLOCK // channels * spaces)
    factor = jnp.broadcast_to(points / area_total, (ROWS, BLOCK))

    def scale_channel(c, carry):
        weight = cw[c]
        for g in range(groups):
            u = c * groups + g
            scale = area[g] * factor * weight
            sgn[u] = sgn[u] * scale
            scl[u] = scale * (1.0 / (count * (count - 1.0)))
        return carry

    lax.fori_loop(0, channels, scale_channel, 0)

    def finish(j, source, first, size):
        part = pl.ds(j * per + first, size)
        result[part] = sgn[part] - scl[part] * source


    for chunk, (first, size) in enumerate(CHUNKS):

        def take_back(n, carry):
            j = met(n)[0]
            part = back.at[pl.ds(j * per + first, size)]
            arrived(part, recv2.at[chunk, j])
            finish(j, part[...], first, size)
            return carry

        lax.fori_loop(0, members, take_back, 0)

    loss_all = collect(box_l3, y, send_l3, recv_l3, ny)
    loss_total = jnp.sum(loss_all, axis=1, keepdims=True)
    result[units] = jnp.broadcast_to(loss_total / (area_total * float(channels)), (ROWS, BLOCK))

    for chunk, (first, size) in enumerate(CHUNKS):

        def wait_sent(j, carry):
            arrived(gat.at[j, pl.ds(first, size)], send1.at[chunk, j])
            arrived(sums.at[j, pl.ds(first, size)], send2.at[chunk, j])
            return carry

        lax.fori_loop(0, members, wait_sent, 0)
    arrived(box_row.at[0], row_sem.at[0])


def deliver(result, grad, loss, last, sem):
    grad_copy = pltpu.make_async_copy(result.at[pl.ds(0, grad.shape[0])], grad, sem.at[0])
    grad_copy.start()
    last[...] = result[grad.shape[0], 0:1, 0:1]
    loss_copy = pltpu.make_async_copy(last, loss, sem.at[1])
    loss_copy.start()
    loss_copy.wait()
    grad_copy.wait()


def local(members, spaces, ensemble, target, chan_weight, lat_band):
    channels, points = target.shape
    units = channels * points // (ROWS * BLOCK)
    per = units // members
    far = spaces // NEAR
    ny = members // PLANES
    nz = far * PLANES
    f32 = jnp.float32
    dma = pltpu.SemaphoreType.DMA
    vmem = pl.BlockSpec(memory_space=pltpu.VMEM)
    hbm = pl.BlockSpec(memory_space=pltpu.HBM)
    whole = pltpu.VMEM((units, ROWS, BLOCK), f32)
    slabs = pltpu.VMEM((members, per, ROWS, BLOCK), f32)

    def box(n):
        return pltpu.VMEM((n, 1, BLOCK), f32)

    def in_hbm(x):
        return pltpu.with_memory_space_constraint(x, pltpu.HBM)

    def body(*refs):
        kernel(members, spaces, *refs)

    result = pl.pallas_call(
        body,
        out_shape=jax.ShapeDtypeStruct((units + 1, ROWS, BLOCK), f32),
        in_specs=[hbm] * 4,
        out_specs=vmem,
        scratch_shapes=[
            pltpu.SMEM(chan_weight.shape, f32),
            pltpu.VMEM((1, lat_band.shape[0]), lat_band.dtype),
            whole,
            pltpu.VMEM((channels, points), f32),
            whole,
            whole,
            slabs,
            slabs,
            whole,
            pltpu.VMEM((points // (ROWS * BLOCK), ROWS, BLOCK), f32),
            pltpu.VMEM((points // (ROWS * BLOCK), ROWS, BLOCK), f32),
            pltpu.VMEM((2, 1, lat_band.shape[0]), f32),
            box(NEAR),
            box(far),
            box(NEAR),
            box(nz),
            box(ny),
            dma((4,)),
            dma((2,)),
            dma((len(CHUNKS), members)),
            dma((len(CHUNKS), members)),
            dma((len(CHUNKS), members)),
            dma((len(CHUNKS), members)),
            dma((NEAR,)),
            dma((NEAR,)),
            dma((far,)),
            dma((far,)),
            dma((NEAR,)),
            dma((NEAR,)),
            dma((nz,)),
            dma((nz,)),
            dma((ny,)),
            dma((ny,)),
        ],
        compiler_params=pltpu.CompilerParams(
            collective_id=0, has_side_effects=True, vmem_limit_bytes=32 * 1024 * 1024
        ),
    )(
        in_hbm(ensemble.reshape(units, ROWS, BLOCK)),
        in_hbm(target),
        in_hbm(chan_weight),
        in_hbm(lat_band.reshape(1, -1)),
    )
    grad, loss = pl.pallas_call(
        deliver,
        out_shape=(
            jax.ShapeDtypeStruct((units, ROWS, BLOCK), f32),
            jax.ShapeDtypeStruct((1, 1), f32),
        ),
        in_specs=[vmem],
        out_specs=(hbm, hbm),
        scratch_shapes=[pltpu.VMEM((1, 1), f32), dma((2,))],
        compiler_params=pltpu.CompilerParams(vmem_limit_bytes=32 * 1024 * 1024),
    )(result)
    return loss.reshape(()), grad.reshape(1, channels, points)


def solution(mesh):
    members, spaces = mesh.shape["member"], mesh.shape["space"]

    def step(*args):
        return local(members, spaces, *args)

    in_specs = (P("member", None, "space"), P(None, "space"), P(), P("space"))
    out_specs = (P(), P("member", None, "space"))
    return jax.shard_map(step, mesh=mesh, in_specs=in_specs, out_specs=out_specs, check_vma=False)
```

```python
import math

import jax
import jax.numpy as jnp
from jax import lax
from jax.experimental import pallas as pl
from jax.experimental.pallas import tpu as pltpu
from jax.sharding import PartitionSpec as P

BLOCK = 128
BANDS = 720
MESH = pl.DeviceIdType.MESH
ROWS = 4
NEAR = 8
PLANES = 2
CHUNKS = ((0, 8), (8, 5))


def kernel(
    members,
    spaces,
    ens,
    tgt,
    cw_hbm,
    lat_hbm,
    result,
    cw,
    lat,
    own,
    tgt_rows,
    sgn,
    scl,
    gat,
    sums,
    back,
    area,
    met_area,
    box_row,
    box_a1,
    box_a2,
    box_l1,
    box_l2,
    box_l3,
    local_sem,
    row_sem,
    send1,
    recv1,
    send2,
    recv2,
    send_a1,
    recv_a1,
    send_a2,
    recv_a2,
    send_l1,
    recv_l1,
    send_l2,
    recv_l2,
    send_l3,
    recv_l3,
):
    m = lax.axis_index("member")
    s = lax.axis_index("space")
    far = spaces // NEAR
    ny = members // PLANES
    nz = far * PLANES
    near_at = lax.rem(s, NEAR)
    far_at = lax.div(s, NEAR)
    y = lax.div(m, PLANES)
    z = lax.rem(m, PLANES) * far + far_at
    units = ens.shape[0]
    per = units // members
    channels = tgt.shape[0]
    groups = units // channels
    blocks = groups * ROWS

    def member_of(yy, zz):
        return lax.rem(yy + ny, ny) * PLANES + lax.div(lax.rem(zz + nz, nz), far)

    def place(yy, zz):
        return (member_of(yy, zz), lax.rem(lax.rem(zz + nz, nz), far) * NEAR + near_at)

    def near_peer(k):
        return (m, s - near_at + lax.rem(near_at + k, NEAR))

    def far_peer(k):
        return (m, lax.rem(far_at + k, far) * NEAR + near_at)

    def z_peer(k):
        return place(y, z + k)

    def y_peer(k):
        return place(y + k, z)

    quarter = nz // 4

    def met(n):
        pair, turn = lax.div(n, 4), lax.rem(n, 4)
        dy = ny // 2 - pair + lax.rem(turn, 2) * (2 * pair - ny + 1)
        dz = quarter * (1 - 2 * lax.rem(lax.div(turn + 1, 2), 2))
        return place(y + dy, z + dz)

    barrier = pltpu.get_barrier_semaphore()

    def greet(peer):
        pl.semaphore_signal(barrier, inc=1, device_id=peer, device_id_type=MESH)

    def greet_all(peer, start, count):
        def one(k, carry):
            greet(peer(k))
            return carry

        lax.fori_loop(start, count, one, 0)

    greet_all(met, 0, members)
    greet_all(near_peer, 1, NEAR)
    greet_all(z_peer, 1, nz)
    greet_all(y_peer, 1, ny)
    own_copy = pltpu.make_async_copy(ens, own, local_sem.at[0])
    tgt_copy = pltpu.make_async_copy(tgt, tgt_rows, local_sem.at[1])
    cw_copy = pltpu.make_async_copy(cw_hbm, cw, local_sem.at[2])
    lat_copy = pltpu.make_async_copy(lat_hbm, lat, local_sem.at[3])
    lat_copy.start()
    cw_copy.start()
    own_copy.start()
    tgt_copy.start()

    pl.semaphore_wait(barrier, members + (NEAR - 1) + (nz - 1) + (ny - 1))

    def push(src, dst, send, recv, device):
        pltpu.make_async_remote_copy(
            src_ref=src,
            dst_ref=dst,
            send_sem=send,
            recv_sem=recv,
            device_id=device,
            device_id_type=MESH,
        ).start()

    def exchange(source, landing, send, recv, chunk):
        def one(n, carry):
            device = met(n)
            j = device[0]
            push(source(j), landing(m), send.at[chunk, j], recv.at[chunk, m], device)
            return carry

        lax.fori_loop(0, members, one, 0)

    def arrived(ref, sem):
        pltpu.make_async_copy(ref, ref, sem).wait()

    def share(box, at, send, recv, peer, count):
        def one(k, carry):
            push(box.at[at], box.at[at], send.at[k], recv.at[at], peer(k))
            return carry

        lax.fori_loop(1, count, one, 0)

    def collect(box, at, send, recv, count):
        def one(k, carry):
            j = lax.rem(at + k, count)
            pltpu.make_async_copy(box.at[j], box.at[j], recv.at[j]).wait()
            pltpu.make_async_copy(box.at[at], box.at[at], send.at[k]).wait()
            return carry

        lax.fori_loop(1, count, one, 0)
        total = box[0]
        for j in range(1, count):
            total = total + box[j]
        return total

    for chunk, (first, size) in enumerate(CHUNKS):
        exchange(
            lambda j: ens.at[pl.ds(j * per + first, size)],
            lambda i: gat.at[i, pl.ds(first, size)],
            send1,
            recv1,
            chunk,
        )

    def along_rows(row):
        square = jnp.broadcast_to(row, (blocks, blocks))
        diagonal = lax.broadcasted_iota(jnp.int32, (blocks, blocks), 0) == lax.broadcasted_iota(
            jnp.int32, (blocks, blocks), 1
        )
        column = jnp.sum(jnp.where(diagonal, square, 0.0), axis=1, keepdims=True)
        return jnp.broadcast_to(column, (blocks, BLOCK))

    lat_copy.wait()
    latitude = ((lat[...].astype(jnp.float32) + 0.5) / BANDS - 0.5) * math.pi
    block_area = jnp.cos(latitude)
    box_row[0] = block_area
    push(box_row.at[0], box_row.at[1], row_sem.at[0], row_sem.at[1], place(y, z + quarter))
    wide = along_rows(block_area)
    for g in range(groups):
        area[g] = wide[g * ROWS : (g + 1) * ROWS]
    box_a1[near_at] = jnp.sum(wide, axis=0, keepdims=True)
    share(box_a1, near_at, send_a1, recv_a1, near_peer, NEAR)

    cw_copy.wait()
    own_copy.wait()
    tgt_copy.wait()

    def skill_rows(first, rows, acc):
        def group(g, acc):
            tiles = [
                tgt_rows[
                    pl.ds(first, rows), pl.ds(pl.multiple_of((g * ROWS + i) * BLOCK, BLOCK), BLOCK)
                ]
                for i in range(ROWS)
            ]
            part = jnp.zeros((ROWS, BLOCK), jnp.float32)
            for r in range(rows):
                u = (first + r) * groups + g
                skill = own[u] - jnp.concatenate([tile[r : r + 1] for tile in tiles], axis=0)
                sgn[u] = jnp.clip(skill * 64.0, -1.0, 1.0) * 0.0625
                part = part + cw[first + r] * jnp.abs(skill)
            return acc + area[g] * part

        return lax.fori_loop(0, groups, group, acc)

    def skill_octet(k, acc):
        return skill_rows(pl.multiple_of(k * 8, 8), 8, acc)

    octets = channels // 8
    skill_sum = lax.fori_loop(0, octets, skill_octet, jnp.zeros((ROWS, BLOCK), jnp.float32))
    if channels % 8:
        skill_sum = skill_rows(octets * 8, channels % 8, skill_sum)

    arrived(box_row.at[1], row_sem.at[1])
    met_wide = along_rows(box_row[1])
    for g in range(groups):
        met_area[g] = met_wide[g * ROWS : (g + 1) * ROWS]
    count = float(members)

    def pairs(k, acc):
        last = jnp.minimum(2 * k + 1, per - 1)
        counted = jnp.where(2 * k + 1 < per, 1.0, 0.0)
        values = [
            jnp.concatenate([gat[j, 2 * k], gat[j, last]], axis=0) * 64.0 for j in range(members)
        ]
        signs = [jnp.zeros_like(values[0]) for j in range(members)]
        for a in range(members):
            for b in range(a + 1, members):
                d = jnp.clip(values[a] - values[b], -1.0, 1.0)
                signs[a] = signs[a] + d
                signs[b] = signs[b] - d
        dot = values[0] * signs[0]
        for j in range(1, members):
            dot = dot + values[j] * signs[j]
        for i, part, factor in ((2 * k, slice(0, ROWS), 1.0), (last, slice(ROWS, 2 * ROWS), counted)):
            for j in range(members):
                sums[j, i] = signs[j][part]
            u = m * per + i
            acc = acc + (met_area[lax.rem(u, groups)] * (cw[lax.div(u, groups)] * factor)) * dot[part]
        return acc

    def wait_chunk(chunk):
        first, size = CHUNKS[chunk]

        def one(j, carry):
            arrived(gat.at[j, pl.ds(first, size)], recv1.at[chunk, j])
            return carry

        lax.fori_loop(0, members, one, 0)

    def send_back(chunk):
        first, size = CHUNKS[chunk]
        exchange(
            lambda j: sums.at[j, pl.ds(first, size)],
            lambda i: back.at[pl.ds(i * per + first, size)],
            send2,
            recv2,
            chunk,
        )

    middle = CHUNKS[1][0] // 2

    def chunk_step(chunk, acc):
        @pl.when(chunk == 0)
        def _():
            wait_chunk(0)
            area_near = collect(box_a1, near_at, send_a1, recv_a1, NEAR)
            box_a2[far_at] = area_near
            share(box_a2, far_at, send_a2, recv_a2, far_peer, far)

        @pl.when(chunk == 1)
        def _():
            send_back(0)
            wait_chunk(1)

        return lax.fori_loop(chunk * middle, middle + chunk * ((per + 1) // 2 - middle), pairs, acc)

    spread_sum = lax.fori_loop(0, len(CHUNKS), chunk_step, jnp.zeros((ROWS, BLOCK), jnp.float32))
    mine = skill_sum * (1.0 / count) - spread_sum * (1.0 / (64.0 * count * (count - 1.0)))
    box_l1[near_at] = jnp.sum(mine, axis=0, keepdims=True)
    share(box_l1, near_at, send_l1, recv_l1, near_peer, NEAR)
    send_back(1)

    loss_near = collect(box_l1, near_at, send_l1, recv_l1, NEAR)
    box_l2[z] = loss_near
    share(box_l2, z, send_l2, recv_l2, z_peer, nz)
    loss_z = collect(box_l2, z, send_l2, recv_l2, nz)
    box_l3[y] = loss_z
    share(box_l3, y, send_l3, recv_l3, y_peer, ny)

    area_all = collect(box_a2, far_at, send_a2, recv_a2, far)
    area_total = jnp.sum(area_all, axis=1, keepdims=True)
    points = float(units * ROWS * BLOCK // channels * spaces)
    factor = jnp.broadcast_to(points / area_total, (ROWS, BLOCK))

    def scale_channel(c, carry):
        weight = cw[c]
        for g in range(groups):
            u = c * groups + g
            scale = area[g] * factor * weight
            sgn[u] = sgn[u] * scale
            scl[u] = scale * (1.0 / (count * (count - 1.0)))
        return carry

    lax.fori_loop(0, channels, scale_channel, 0)

    def finish(j, source, first, size):
        part = pl.ds(j * per + first, size)
        result[part] = sgn[part] - scl[part] * source


    for chunk, (first, size) in enumerate(CHUNKS):

        def take_back(n, carry):
            j = met(n)[0]
            part = back.at[pl.ds(j * per + first, size)]
            arrived(part, recv2.at[chunk, j])
            finish(j, part[...], first, size)
            return carry

        lax.fori_loop(0, members, take_back, 0)

    loss_all = collect(box_l3, y, send_l3, recv_l3, ny)
    loss_total = jnp.sum(loss_all, axis=1, keepdims=True)
    result[units] = jnp.broadcast_to(loss_total / (area_total * float(channels)), (ROWS, BLOCK))

    for chunk, (first, size) in enumerate(CHUNKS):

        def wait_sent(j, carry):
            arrived(gat.at[j, pl.ds(first, size)], send1.at[chunk, j])
            arrived(sums.at[j, pl.ds(first, size)], send2.at[chunk, j])
            return carry

        lax.fori_loop(0, members, wait_sent, 0)
    arrived(box_row.at[0], row_sem.at[0])


def deliver(result, grad, loss, last, sem):
    grad_copy = pltpu.make_async_copy(result.at[pl.ds(0, grad.shape[0])], grad, sem.at[0])
    grad_copy.start()
    last[...] = result[grad.shape[0], 0:1, 0:1]
    loss_copy = pltpu.make_async_copy(last, loss, sem.at[1])
    loss_copy.start()
    loss_copy.wait()
    grad_copy.wait()


def local(members, spaces, ensemble, target, chan_weight, lat_band):
    channels, points = target.shape
    units = channels * points // (ROWS * BLOCK)
    per = units // members
    far = spaces // NEAR
    ny = members // PLANES
    nz = far * PLANES
    f32 = jnp.float32
    dma = pltpu.SemaphoreType.DMA
    vmem = pl.BlockSpec(memory_space=pltpu.VMEM)
    hbm = pl.BlockSpec(memory_space=pltpu.HBM)
    whole = pltpu.VMEM((units, ROWS, BLOCK), f32)
    slabs = pltpu.VMEM((members, per, ROWS, BLOCK), f32)

    def box(n):
        return pltpu.VMEM((n, 1, BLOCK), f32)

    def in_hbm(x):
        return pltpu.with_memory_space_constraint(x, pltpu.HBM)

    def body(*refs):
        kernel(members, spaces, *refs)

    result = pl.pallas_call(
        body,
        out_shape=jax.ShapeDtypeStruct((units + 1, ROWS, BLOCK), f32),
        in_specs=[hbm] * 4,
        out_specs=vmem,
        scratch_shapes=[
            pltpu.SMEM(chan_weight.shape, f32),
            pltpu.VMEM((1, lat_band.shape[0]), lat_band.dtype),
            whole,
            pltpu.VMEM((channels, points), f32),
            whole,
            whole,
            slabs,
            slabs,
            whole,
            pltpu.VMEM((points // (ROWS * BLOCK), ROWS, BLOCK), f32),
            pltpu.VMEM((points // (ROWS * BLOCK), ROWS, BLOCK), f32),
            pltpu.VMEM((2, 1, lat_band.shape[0]), f32),
            box(NEAR),
            box(far),
            box(NEAR),
            box(nz),
            box(ny),
            dma((4,)),
            dma((2,)),
            dma((len(CHUNKS), members)),
            dma((len(CHUNKS), members)),
            dma((len(CHUNKS), members)),
            dma((len(CHUNKS), members)),
            dma((NEAR,)),
            dma((NEAR,)),
            dma((far,)),
            dma((far,)),
            dma((NEAR,)),
            dma((NEAR,)),
            dma((nz,)),
            dma((nz,)),
            dma((ny,)),
            dma((ny,)),
        ],
        compiler_params=pltpu.CompilerParams(
            collective_id=0, has_side_effects=True, vmem_limit_bytes=32 * 1024 * 1024
        ),
    )(
        in_hbm(ensemble.reshape(units, ROWS, BLOCK)),
        in_hbm(target),
        in_hbm(chan_weight),
        in_hbm(lat_band.reshape(1, -1)),
    )
    grad, loss = pl.pallas_call(
        deliver,
        out_shape=(
            jax.ShapeDtypeStruct((units, ROWS, BLOCK), f32),
            jax.ShapeDtypeStruct((1, 1), f32),
        ),
        in_specs=[vmem],
        out_specs=(hbm, hbm),
        scratch_shapes=[pltpu.VMEM((1, 1), f32), dma((2,))],
        compiler_params=pltpu.CompilerParams(vmem_limit_bytes=32 * 1024 * 1024),
    )(result)
    return loss.reshape(()), grad.reshape(1, channels, points)


def solution(mesh):
    members, spaces = mesh.shape["member"], mesh.shape["space"]

    def step(*args):
        return local(members, spaces, *args)

    in_specs = (P("member", None, "space"), P(None, "space"), P(), P("space"))
    out_specs = (P(), P("member", None, "space"))
    return jax.shard_map(step, mesh=mesh, in_specs=in_specs, out_specs=out_specs, check_vma=False)
```

```python
import math

import jax
import jax.numpy as jnp
from jax import lax
from jax.experimental import pallas as pl
from jax.experimental.pallas import tpu as pltpu
from jax.sharding import PartitionSpec as P

BLOCK = 128
BANDS = 720
MESH = pl.DeviceIdType.MESH
ROWS = 4
NEAR = 8
PLANES = 2
CHUNKS = ((0, 4), (4, 9))


def kernel(
    members,
    spaces,
    ens,
    tgt,
    cw_hbm,
    lat_hbm,
    result,
    cw,
    lat,
    own,
    tgt_rows,
    sgn,
    scl,
    gat,
    sums,
    back,
    area,
    met_area,
    box_row,
    box_a1,
    box_a2,
    box_l1,
    box_l2,
    box_l3,
    local_sem,
    row_sem,
    send1,
    recv1,
    send2,
    recv2,
    send_a1,
    recv_a1,
    send_a2,
    recv_a2,
    send_l1,
    recv_l1,
    send_l2,
    recv_l2,
    send_l3,
    recv_l3,
):
    m = lax.axis_index("member")
    s = lax.axis_index("space")
    far = spaces // NEAR
    ny = members // PLANES
    nz = far * PLANES
    near_at = lax.rem(s, NEAR)
    far_at = lax.div(s, NEAR)
    y = lax.div(m, PLANES)
    z = lax.rem(m, PLANES) * far + far_at
    units = ens.shape[0]
    per = units // members
    channels = tgt.shape[0]
    groups = units // channels
    blocks = groups * ROWS

    def member_of(yy, zz):
        return lax.rem(yy + ny, ny) * PLANES + lax.div(lax.rem(zz + nz, nz), far)

    def place(yy, zz):
        return (member_of(yy, zz), lax.rem(lax.rem(zz + nz, nz), far) * NEAR + near_at)

    def near_peer(k):
        return (m, s - near_at + lax.rem(near_at + k, NEAR))

    def far_peer(k):
        return (m, lax.rem(far_at + k, far) * NEAR + near_at)

    def z_peer(k):
        return place(y, z + k)

    def y_peer(k):
        return place(y + k, z)

    quarter = nz // 4

    def met(n):
        pair, turn = lax.div(n, 4), lax.rem(n, 4)
        dy = ny // 2 - pair + lax.rem(turn, 2) * (2 * pair - ny + 1)
        dz = quarter * (1 - 2 * lax.rem(lax.div(turn + 1, 2), 2))
        return place(y + dy, z + dz)

    barrier = pltpu.get_barrier_semaphore()

    def greet(peer):
        pl.semaphore_signal(barrier, inc=1, device_id=peer, device_id_type=MESH)

    def greet_all(peer, start, count):
        def one(k, carry):
            greet(peer(k))
            return carry

        lax.fori_loop(start, count, one, 0)

    greet_all(met, 0, members)
    greet_all(near_peer, 1, NEAR)
    greet_all(z_peer, 1, nz)
    greet_all(y_peer, 1, ny)
    own_copy = pltpu.make_async_copy(ens, own, local_sem.at[0])
    tgt_copy = pltpu.make_async_copy(tgt, tgt_rows, local_sem.at[1])
    cw_copy = pltpu.make_async_copy(cw_hbm, cw, local_sem.at[2])
    lat_copy = pltpu.make_async_copy(lat_hbm, lat, local_sem.at[3])
    lat_copy.start()
    cw_copy.start()
    own_copy.start()
    tgt_copy.start()

    pl.semaphore_wait(barrier, members + (NEAR - 1) + (nz - 1) + (ny - 1))

    def push(src, dst, send, recv, device):
        pltpu.make_async_remote_copy(
            src_ref=src,
            dst_ref=dst,
            send_sem=send,
            recv_sem=recv,
            device_id=device,
            device_id_type=MESH,
        ).start()

    def exchange(source, landing, send, recv, chunk):
        def one(n, carry):
            device = met(n)
            j = device[0]
            push(source(j), landing(m), send.at[chunk, j], recv.at[chunk, m], device)
            return carry

        lax.fori_loop(0, members, one, 0)

    def arrived(ref, sem):
        pltpu.make_async_copy(ref, ref, sem).wait()

    def share(box, at, send, recv, peer, count):
        def one(k, carry):
            push(box.at[at], box.at[at], send.at[k], recv.at[at], peer(k))
            return carry

        lax.fori_loop(1, count, one, 0)

    def collect(box, at, send, recv, count):
        def one(k, carry):
            j = lax.rem(at + k, count)
            pltpu.make_async_copy(box.at[j], box.at[j], recv.at[j]).wait()
            pltpu.make_async_copy(box.at[at], box.at[at], send.at[k]).wait()
            return carry

        lax.fori_loop(1, count, one, 0)
        total = box[0]
        for j in range(1, count):
            total = total + box[j]
        return total

    for chunk, (first, size) in enumerate(CHUNKS):
        exchange(
            lambda j: ens.at[pl.ds(j * per + first, size)],
            lambda i: gat.at[i, pl.ds(first, size)],
            send1,
            recv1,
            chunk,
        )

    def along_rows(row):
        square = jnp.broadcast_to(row, (blocks, blocks))
        diagonal = lax.broadcasted_iota(jnp.int32, (blocks, blocks), 0) == lax.broadcasted_iota(
            jnp.int32, (blocks, blocks), 1
        )
        column = jnp.sum(jnp.where(diagonal, square, 0.0), axis=1, keepdims=True)
        return jnp.broadcast_to(column, (blocks, BLOCK))

    lat_copy.wait()
    latitude = ((lat[...].astype(jnp.float32) + 0.5) / BANDS - 0.5) * math.pi
    block_area = jnp.cos(latitude)
    box_row[0] = block_area
    push(box_row.at[0], box_row.at[1], row_sem.at[0], row_sem.at[1], place(y, z + quarter))
    wide = along_rows(block_area)
    for g in range(groups):
        area[g] = wide[g * ROWS : (g + 1) * ROWS]
    box_a1[near_at] = jnp.sum(wide, axis=0, keepdims=True)
    share(box_a1, near_at, send_a1, recv_a1, near_peer, NEAR)

    cw_copy.wait()
    own_copy.wait()
    tgt_copy.wait()

    def skill_rows(first, rows, acc):
        def group(g, acc):
            tiles = [
                tgt_rows[
                    pl.ds(first, rows), pl.ds(pl.multiple_of((g * ROWS + i) * BLOCK, BLOCK), BLOCK)
                ]
                for i in range(ROWS)
            ]
            part = jnp.zeros((ROWS, BLOCK), jnp.float32)
            for r in range(rows):
                u = (first + r) * groups + g
                skill = own[u] - jnp.concatenate([tile[r : r + 1] for tile in tiles], axis=0)
                sgn[u] = jnp.clip(skill * 64.0, -1.0, 1.0) * 0.0625
                part = part + cw[first + r] * jnp.abs(skill)
            return acc + area[g] * part

        return lax.fori_loop(0, groups, group, acc)

    def skill_octet(k, acc):
        return skill_rows(pl.multiple_of(k * 8, 8), 8, acc)

    octets = channels // 8
    skill_sum = lax.fori_loop(0, octets, skill_octet, jnp.zeros((ROWS, BLOCK), jnp.float32))
    if channels % 8:
        skill_sum = skill_rows(octets * 8, channels % 8, skill_sum)

    arrived(box_row.at[1], row_sem.at[1])
    met_wide = along_rows(box_row[1])
    for g in range(groups):
        met_area[g] = met_wide[g * ROWS : (g + 1) * ROWS]
    count = float(members)

    def pairs(k, acc):
        last = jnp.minimum(2 * k + 1, per - 1)
        counted = jnp.where(2 * k + 1 < per, 1.0, 0.0)
        values = [
            jnp.concatenate([gat[j, 2 * k], gat[j, last]], axis=0) * 64.0 for j in range(members)
        ]
        signs = [jnp.zeros_like(values[0]) for j in range(members)]
        for a in range(members):
            for b in range(a + 1, members):
                d = jnp.clip(values[a] - values[b], -1.0, 1.0)
                signs[a] = signs[a] + d
                signs[b] = signs[b] - d
        dot = values[0] * signs[0]
        for j in range(1, members):
            dot = dot + values[j] * signs[j]
        for i, part, factor in ((2 * k, slice(0, ROWS), 1.0), (last, slice(ROWS, 2 * ROWS), counted)):
            for j in range(members):
                sums[j, i] = signs[j][part]
            u = m * per + i
            acc = acc + (met_area[lax.rem(u, groups)] * (cw[lax.div(u, groups)] * factor)) * dot[part]
        return acc

    def wait_chunk(chunk):
        first, size = CHUNKS[chunk]

        def one(j, carry):
            arrived(gat.at[j, pl.ds(first, size)], recv1.at[chunk, j])
            return carry

        lax.fori_loop(0, members, one, 0)

    def send_back(chunk):
        first, size = CHUNKS[chunk]
        exchange(
            lambda j: sums.at[j, pl.ds(first, size)],
            lambda i: back.at[pl.ds(i * per + first, size)],
            send2,
            recv2,
            chunk,
        )

    middle = CHUNKS[1][0] // 2

    def chunk_step(chunk, acc):
        @pl.when(chunk == 0)
        def _():
            wait_chunk(0)
            area_near = collect(box_a1, near_at, send_a1, recv_a1, NEAR)
            box_a2[far_at] = area_near
            share(box_a2, far_at, send_a2, recv_a2, far_peer, far)

        @pl.when(chunk == 1)
        def _():
            send_back(0)
            wait_chunk(1)

        return lax.fori_loop(chunk * middle, middle + chunk * ((per + 1) // 2 - middle), pairs, acc)

    spread_sum = lax.fori_loop(0, len(CHUNKS), chunk_step, jnp.zeros((ROWS, BLOCK), jnp.float32))
    mine = skill_sum * (1.0 / count) - spread_sum * (1.0 / (64.0 * count * (count - 1.0)))
    box_l1[near_at] = jnp.sum(mine, axis=0, keepdims=True)
    share(box_l1, near_at, send_l1, recv_l1, near_peer, NEAR)
    send_back(1)

    loss_near = collect(box_l1, near_at, send_l1, recv_l1, NEAR)
    box_l2[z] = loss_near
    share(box_l2, z, send_l2, recv_l2, z_peer, nz)
    loss_z = collect(box_l2, z, send_l2, recv_l2, nz)
    box_l3[y] = loss_z
    share(box_l3, y, send_l3, recv_l3, y_peer, ny)

    area_all = collect(box_a2, far_at, send_a2, recv_a2, far)
    area_total = jnp.sum(area_all, axis=1, keepdims=True)
    points = float(units * ROWS * BLOCK // channels * spaces)
    factor = jnp.broadcast_to(points / area_total, (ROWS, BLOCK))

    def scale_channel(c, carry):
        weight = cw[c]
        for g in range(groups):
            u = c * groups + g
            scale = area[g] * factor * weight
            sgn[u] = sgn[u] * scale
            scl[u] = scale * (1.0 / (count * (count - 1.0)))
        return carry

    lax.fori_loop(0, channels, scale_channel, 0)

    def finish(j, source, first, size):
        part = pl.ds(j * per + first, size)
        result[part] = sgn[part] - scl[part] * source


    for chunk, (first, size) in enumerate(CHUNKS):

        def take_back(n, carry):
            j = met(n)[0]
            part = back.at[pl.ds(j * per + first, size)]
            arrived(part, recv2.at[chunk, j])
            finish(j, part[...], first, size)
            return carry

        lax.fori_loop(0, members, take_back, 0)

    loss_all = collect(box_l3, y, send_l3, recv_l3, ny)
    loss_total = jnp.sum(loss_all, axis=1, keepdims=True)
    result[units] = jnp.broadcast_to(loss_total / (area_total * float(channels)), (ROWS, BLOCK))

    for chunk, (first, size) in enumerate(CHUNKS):

        def wait_sent(j, carry):
            arrived(gat.at[j, pl.ds(first, size)], send1.at[chunk, j])
            arrived(sums.at[j, pl.ds(first, size)], send2.at[chunk, j])
            return carry

        lax.fori_loop(0, members, wait_sent, 0)
    arrived(box_row.at[0], row_sem.at[0])


def deliver(result, grad, loss, last, sem):
    grad_copy = pltpu.make_async_copy(result.at[pl.ds(0, grad.shape[0])], grad, sem.at[0])
    grad_copy.start()
    last[...] = result[grad.shape[0], 0:1, 0:1]
    loss_copy = pltpu.make_async_copy(last, loss, sem.at[1])
    loss_copy.start()
    loss_copy.wait()
    grad_copy.wait()


def local(members, spaces, ensemble, target, chan_weight, lat_band):
    channels, points = target.shape
    units = channels * points // (ROWS * BLOCK)
    per = units // members
    far = spaces // NEAR
    ny = members // PLANES
    nz = far * PLANES
    f32 = jnp.float32
    dma = pltpu.SemaphoreType.DMA
    vmem = pl.BlockSpec(memory_space=pltpu.VMEM)
    hbm = pl.BlockSpec(memory_space=pltpu.HBM)
    whole = pltpu.VMEM((units, ROWS, BLOCK), f32)
    slabs = pltpu.VMEM((members, per, ROWS, BLOCK), f32)

    def box(n):
        return pltpu.VMEM((n, 1, BLOCK), f32)

    def in_hbm(x):
        return pltpu.with_memory_space_constraint(x, pltpu.HBM)

    def body(*refs):
        kernel(members, spaces, *refs)

    result = pl.pallas_call(
        body,
        out_shape=jax.ShapeDtypeStruct((units + 1, ROWS, BLOCK), f32),
        in_specs=[hbm] * 4,
        out_specs=vmem,
        scratch_shapes=[
            pltpu.SMEM(chan_weight.shape, f32),
            pltpu.VMEM((1, lat_band.shape[0]), lat_band.dtype),
            whole,
            pltpu.VMEM((channels, points), f32),
            whole,
            whole,
            slabs,
            slabs,
            whole,
            pltpu.VMEM((points // (ROWS * BLOCK), ROWS, BLOCK), f32),
            pltpu.VMEM((points // (ROWS * BLOCK), ROWS, BLOCK), f32),
            pltpu.VMEM((2, 1, lat_band.shape[0]), f32),
            box(NEAR),
            box(far),
            box(NEAR),
            box(nz),
            box(ny),
            dma((4,)),
            dma((2,)),
            dma((len(CHUNKS), members)),
            dma((len(CHUNKS), members)),
            dma((len(CHUNKS), members)),
            dma((len(CHUNKS), members)),
            dma((NEAR,)),
            dma((NEAR,)),
            dma((far,)),
            dma((far,)),
            dma((NEAR,)),
            dma((NEAR,)),
            dma((nz,)),
            dma((nz,)),
            dma((ny,)),
            dma((ny,)),
        ],
        compiler_params=pltpu.CompilerParams(
            collective_id=0, has_side_effects=True, vmem_limit_bytes=32 * 1024 * 1024
        ),
    )(
        in_hbm(ensemble.reshape(units, ROWS, BLOCK)),
        in_hbm(target),
        in_hbm(chan_weight),
        in_hbm(lat_band.reshape(1, -1)),
    )
    grad, loss = pl.pallas_call(
        deliver,
        out_shape=(
            jax.ShapeDtypeStruct((units, ROWS, BLOCK), f32),
            jax.ShapeDtypeStruct((1, 1), f32),
        ),
        in_specs=[vmem],
        out_specs=(hbm, hbm),
        scratch_shapes=[pltpu.VMEM((1, 1), f32), dma((2,))],
        compiler_params=pltpu.CompilerParams(vmem_limit_bytes=32 * 1024 * 1024),
    )(result)
    return loss.reshape(()), grad.reshape(1, channels, points)


def solution(mesh):
    members, spaces = mesh.shape["member"], mesh.shape["space"]

    def step(*args):
        return local(members, spaces, *args)

    in_specs = (P("member", None, "space"), P(None, "space"), P(), P("space"))
    out_specs = (P(), P("member", None, "space"))
    return jax.shard_map(step, mesh=mesh, in_specs=in_specs, out_specs=out_specs, check_vma=False)
```

```python
import math

import jax
import jax.numpy as jnp
from jax import lax
from jax.experimental import pallas as pl
from jax.experimental.pallas import tpu as pltpu
from jax.sharding import PartitionSpec as P

BLOCK = 128
BANDS = 720
MESH = pl.DeviceIdType.MESH
ROWS = 4
NEAR = 8
PLANES = 2
CHUNKS = ((0, 6), (6, 7))


def kernel(
    members,
    spaces,
    ens,
    tgt,
    cw_hbm,
    lat_hbm,
    result,
    cw,
    lat,
    own,
    tgt_rows,
    sgn,
    scl,
    gat,
    sums,
    back,
    area,
    met_area,
    box_row,
    box_a1,
    box_a2,
    box_l1,
    box_l2,
    box_l3,
    local_sem,
    row_sem,
    send1,
    recv1,
    send2,
    recv2,
    send_a1,
    recv_a1,
    send_a2,
    recv_a2,
    send_l1,
    recv_l1,
    send_l2,
    recv_l2,
    send_l3,
    recv_l3,
):
    m = lax.axis_index("member")
    s = lax.axis_index("space")
    far = spaces // NEAR
    ny = members // PLANES
    nz = far * PLANES
    near_at = lax.rem(s, NEAR)
    far_at = lax.div(s, NEAR)
    y = lax.div(m, PLANES)
    z = lax.rem(m, PLANES) * far + far_at
    units = ens.shape[0]
    per = units // members
    channels = tgt.shape[0]
    groups = units // channels
    blocks = groups * ROWS

    def member_of(yy, zz):
        return lax.rem(yy + ny, ny) * PLANES + lax.div(lax.rem(zz + nz, nz), far)

    def place(yy, zz):
        return (member_of(yy, zz), lax.rem(lax.rem(zz + nz, nz), far) * NEAR + near_at)

    def near_peer(k):
        return (m, s - near_at + lax.rem(near_at + k, NEAR))

    def far_peer(k):
        return (m, lax.rem(far_at + k, far) * NEAR + near_at)

    def z_peer(k):
        return place(y, z + k)

    def y_peer(k):
        return place(y + k, z)

    quarter = nz // 4

    def met(n):
        pair, turn = lax.div(n, 4), lax.rem(n, 4)
        dy = ny // 2 - pair + lax.rem(turn, 2) * (2 * pair - ny + 1)
        dz = quarter * (1 - 2 * lax.rem(lax.div(turn + 1, 2), 2))
        return place(y + dy, z + dz)

    barrier = pltpu.get_barrier_semaphore()

    def greet(peer):
        pl.semaphore_signal(barrier, inc=1, device_id=peer, device_id_type=MESH)

    def greet_all(peer, start, count):
        def one(k, carry):
            greet(peer(k))
            return carry

        lax.fori_loop(start, count, one, 0)

    greet_all(met, 0, members)
    greet_all(near_peer, 1, NEAR)
    greet_all(z_peer, 1, nz)
    greet_all(y_peer, 1, ny)
    own_copy = pltpu.make_async_copy(ens, own, local_sem.at[0])
    tgt_copy = pltpu.make_async_copy(tgt, tgt_rows, local_sem.at[1])
    cw_copy = pltpu.make_async_copy(cw_hbm, cw, local_sem.at[2])
    lat_copy = pltpu.make_async_copy(lat_hbm, lat, local_sem.at[3])
    lat_copy.start()
    cw_copy.start()
    own_copy.start()
    tgt_copy.start()

    pl.semaphore_wait(barrier, members + (NEAR - 1) + (nz - 1) + (ny - 1))

    def push(src, dst, send, recv, device):
        pltpu.make_async_remote_copy(
            src_ref=src,
            dst_ref=dst,
            send_sem=send,
            recv_sem=recv,
            device_id=device,
            device_id_type=MESH,
        ).start()

    def exchange(source, landing, send, recv, chunk):
        def one(n, carry):
            device = met(n)
            j = device[0]
            push(source(j), landing(m), send.at[chunk, j], recv.at[chunk, m], device)
            return carry

        lax.fori_loop(0, members, one, 0)

    def arrived(ref, sem):
        pltpu.make_async_copy(ref, ref, sem).wait()

    def share(box, at, send, recv, peer, count):
        def one(k, carry):
            push(box.at[at], box.at[at], send.at[k], recv.at[at], peer(k))
            return carry

        lax.fori_loop(1, count, one, 0)

    def sent(box, send, count):
        def one(k, carry):
            arrived(box.at[0], send.at[k])
            return carry

        lax.fori_loop(1, count, one, 0)

    def collect(box, at, recv, count):
        def one(k, carry):
            j = lax.rem(at + k, count)
            arrived(box.at[j], recv.at[j])
            return carry

        lax.fori_loop(1, count, one, 0)
        total = box[0]
        for j in range(1, count):
            total = total + box[j]
        return total

    for chunk, (first, size) in enumerate(CHUNKS):
        exchange(
            lambda j: ens.at[pl.ds(j * per + first, size)],
            lambda i: gat.at[i, pl.ds(first, size)],
            send1,
            recv1,
            chunk,
        )

    def along_rows(row):
        square = jnp.broadcast_to(row, (blocks, blocks))
        diagonal = lax.broadcasted_iota(jnp.int32, (blocks, blocks), 0) == lax.broadcasted_iota(
            jnp.int32, (blocks, blocks), 1
        )
        column = jnp.sum(jnp.where(diagonal, square, 0.0), axis=1, keepdims=True)
        return jnp.broadcast_to(column, (blocks, BLOCK))

    lat_copy.wait()
    latitude = ((lat[...].astype(jnp.float32) + 0.5) / BANDS - 0.5) * math.pi
    block_area = jnp.cos(latitude)
    box_row[0] = block_area
    push(box_row.at[0], box_row.at[1], row_sem.at[0], row_sem.at[1], place(y, z + quarter))
    wide = along_rows(block_area)
    for g in range(groups):
        area[g] = wide[g * ROWS : (g + 1) * ROWS]
    box_a1[near_at] = jnp.sum(wide, axis=0, keepdims=True)
    share(box_a1, near_at, send_a1, recv_a1, near_peer, NEAR)

    cw_copy.wait()
    own_copy.wait()
    tgt_copy.wait()

    def skill_rows(first, rows, acc):
        def group(g, acc):
            tiles = [
                tgt_rows[
                    pl.ds(first, rows), pl.ds(pl.multiple_of((g * ROWS + i) * BLOCK, BLOCK), BLOCK)
                ]
                for i in range(ROWS)
            ]
            part = jnp.zeros((ROWS, BLOCK), jnp.float32)
            for r in range(rows):
                u = (first + r) * groups + g
                skill = own[u] - jnp.concatenate([tile[r : r + 1] for tile in tiles], axis=0)
                sgn[u] = jnp.clip(skill * 64.0, -1.0, 1.0) * 0.0625
                part = part + cw[first + r] * jnp.abs(skill)
            return acc + area[g] * part

        return lax.fori_loop(0, groups, group, acc)

    def skill_octet(k, acc):
        return skill_rows(pl.multiple_of(k * 8, 8), 8, acc)

    octets = channels // 8
    skill_sum = lax.fori_loop(0, octets, skill_octet, jnp.zeros((ROWS, BLOCK), jnp.float32))
    if channels % 8:
        skill_sum = skill_rows(octets * 8, channels % 8, skill_sum)

    arrived(box_row.at[1], row_sem.at[1])
    met_wide = along_rows(box_row[1])
    for g in range(groups):
        met_area[g] = met_wide[g * ROWS : (g + 1) * ROWS]
    count = float(members)

    def pairs(k, acc):
        last = jnp.minimum(2 * k + 1, per - 1)
        counted = jnp.where(2 * k + 1 < per, 1.0, 0.0)
        values = [
            jnp.concatenate([gat[j, 2 * k], gat[j, last]], axis=0) * 64.0 for j in range(members)
        ]
        signs = [jnp.zeros_like(values[0]) for j in range(members)]
        for a in range(members):
            for b in range(a + 1, members):
                d = jnp.clip(values[a] - values[b], -1.0, 1.0)
                signs[a] = signs[a] + d
                signs[b] = signs[b] - d
        dot = values[0] * signs[0]
        for j in range(1, members):
            dot = dot + values[j] * signs[j]
        for i, part, factor in ((2 * k, slice(0, ROWS), 1.0), (last, slice(ROWS, 2 * ROWS), counted)):
            for j in range(members):
                sums[j, i] = signs[j][part]
            u = m * per + i
            acc = acc + (met_area[lax.rem(u, groups)] * (cw[lax.div(u, groups)] * factor)) * dot[part]
        return acc

    def wait_chunk(chunk):
        first, size = CHUNKS[chunk]

        def one(j, carry):
            arrived(gat.at[j, pl.ds(first, size)], recv1.at[chunk, j])
            return carry

        lax.fori_loop(0, members, one, 0)

    def send_back(chunk):
        first, size = CHUNKS[chunk]
        exchange(
            lambda j: sums.at[j, pl.ds(first, size)],
            lambda i: back.at[pl.ds(i * per + first, size)],
            send2,
            recv2,
            chunk,
        )

    middle = CHUNKS[1][0] // 2

    def chunk_step(chunk, acc):
        @pl.when(chunk == 0)
        def _():
            wait_chunk(0)
            area_near = collect(box_a1, near_at, recv_a1, NEAR)
            box_a2[far_at] = area_near
            share(box_a2, far_at, send_a2, recv_a2, far_peer, far)

        @pl.when(chunk == 1)
        def _():
            send_back(0)
            wait_chunk(1)

        return lax.fori_loop(chunk * middle, middle + chunk * ((per + 1) // 2 - middle), pairs, acc)

    spread_sum = lax.fori_loop(0, len(CHUNKS), chunk_step, jnp.zeros((ROWS, BLOCK), jnp.float32))
    mine = skill_sum * (1.0 / count) - spread_sum * (1.0 / (64.0 * count * (count - 1.0)))
    box_l1[near_at] = jnp.sum(mine, axis=0, keepdims=True)
    share(box_l1, near_at, send_l1, recv_l1, near_peer, NEAR)
    send_back(1)

    loss_near = collect(box_l1, near_at, recv_l1, NEAR)
    box_l2[z] = loss_near
    share(box_l2, z, send_l2, recv_l2, z_peer, nz)
    loss_z = collect(box_l2, z, recv_l2, nz)
    box_l3[y] = loss_z
    share(box_l3, y, send_l3, recv_l3, y_peer, ny)

    area_all = collect(box_a2, far_at, recv_a2, far)
    area_total = jnp.sum(area_all, axis=1, keepdims=True)
    points = float(units * ROWS * BLOCK // channels * spaces)
    factor = jnp.broadcast_to(points / area_total, (ROWS, BLOCK))

    def scale_channel(c, carry):
        weight = cw[c]
        for g in range(groups):
            u = c * groups + g
            scale = area[g] * factor * weight
            sgn[u] = sgn[u] * scale
            scl[u] = scale * (1.0 / (count * (count - 1.0)))
        return carry

    lax.fori_loop(0, channels, scale_channel, 0)

    def finish(j, source, first, size):
        part = pl.ds(j * per + first, size)
        result[part] = sgn[part] - scl[part] * source


    for chunk, (first, size) in enumerate(CHUNKS):

        def take_back(n, carry):
            j = met(n)[0]
            part = back.at[pl.ds(j * per + first, size)]
            arrived(part, recv2.at[chunk, j])
            finish(j, part[...], first, size)
            return carry

        lax.fori_loop(0, members, take_back, 0)

    loss_all = collect(box_l3, y, recv_l3, ny)
    loss_total = jnp.sum(loss_all, axis=1, keepdims=True)
    result[units] = jnp.broadcast_to(loss_total / (area_total * float(channels)), (ROWS, BLOCK))

    for chunk, (first, size) in enumerate(CHUNKS):

        def wait_sent(j, carry):
            arrived(gat.at[j, pl.ds(first, size)], send1.at[chunk, j])
            arrived(sums.at[j, pl.ds(first, size)], send2.at[chunk, j])
            return carry

        lax.fori_loop(0, members, wait_sent, 0)
    arrived(box_row.at[0], row_sem.at[0])
    sent(box_a1, send_a1, NEAR)
    sent(box_a2, send_a2, far)
    sent(box_l1, send_l1, NEAR)
    sent(box_l2, send_l2, nz)
    sent(box_l3, send_l3, ny)


def deliver(result, grad, loss, last, sem):
    grad_copy = pltpu.make_async_copy(result.at[pl.ds(0, grad.shape[0])], grad, sem.at[0])
    grad_copy.start()
    last[...] = result[grad.shape[0], 0:1, 0:1]
    loss_copy = pltpu.make_async_copy(last, loss, sem.at[1])
    loss_copy.start()
    loss_copy.wait()
    grad_copy.wait()


def local(members, spaces, ensemble, target, chan_weight, lat_band):
    channels, points = target.shape
    units = channels * points // (ROWS * BLOCK)
    per = units // members
    far = spaces // NEAR
    ny = members // PLANES
    nz = far * PLANES
    f32 = jnp.float32
    dma = pltpu.SemaphoreType.DMA
    vmem = pl.BlockSpec(memory_space=pltpu.VMEM)
    hbm = pl.BlockSpec(memory_space=pltpu.HBM)
    whole = pltpu.VMEM((units, ROWS, BLOCK), f32)
    slabs = pltpu.VMEM((members, per, ROWS, BLOCK), f32)

    def box(n):
        return pltpu.VMEM((n, 1, BLOCK), f32)

    def in_hbm(x):
        return pltpu.with_memory_space_constraint(x, pltpu.HBM)

    def body(*refs):
        kernel(members, spaces, *refs)

    result = pl.pallas_call(
        body,
        out_shape=jax.ShapeDtypeStruct((units + 1, ROWS, BLOCK), f32),
        in_specs=[hbm] * 4,
        out_specs=vmem,
        scratch_shapes=[
            pltpu.SMEM(chan_weight.shape, f32),
            pltpu.VMEM((1, lat_band.shape[0]), lat_band.dtype),
            whole,
            pltpu.VMEM((channels, points), f32),
            whole,
            whole,
            slabs,
            slabs,
            whole,
            pltpu.VMEM((points // (ROWS * BLOCK), ROWS, BLOCK), f32),
            pltpu.VMEM((points // (ROWS * BLOCK), ROWS, BLOCK), f32),
            pltpu.VMEM((2, 1, lat_band.shape[0]), f32),
            box(NEAR),
            box(far),
            box(NEAR),
            box(nz),
            box(ny),
            dma((4,)),
            dma((2,)),
            dma((len(CHUNKS), members)),
            dma((len(CHUNKS), members)),
            dma((len(CHUNKS), members)),
            dma((len(CHUNKS), members)),
            dma((NEAR,)),
            dma((NEAR,)),
            dma((far,)),
            dma((far,)),
            dma((NEAR,)),
            dma((NEAR,)),
            dma((nz,)),
            dma((nz,)),
            dma((ny,)),
            dma((ny,)),
        ],
        compiler_params=pltpu.CompilerParams(
            collective_id=0, has_side_effects=True, vmem_limit_bytes=32 * 1024 * 1024
        ),
    )(
        in_hbm(ensemble.reshape(units, ROWS, BLOCK)),
        in_hbm(target),
        in_hbm(chan_weight),
        in_hbm(lat_band.reshape(1, -1)),
    )
    grad, loss = pl.pallas_call(
        deliver,
        out_shape=(
            jax.ShapeDtypeStruct((units, ROWS, BLOCK), f32),
            jax.ShapeDtypeStruct((1, 1), f32),
        ),
        in_specs=[vmem],
        out_specs=(hbm, hbm),
        scratch_shapes=[pltpu.VMEM((1, 1), f32), dma((2,))],
        compiler_params=pltpu.CompilerParams(vmem_limit_bytes=32 * 1024 * 1024),
    )(result)
    return loss.reshape(()), grad.reshape(1, channels, points)


def solution(mesh):
    members, spaces = mesh.shape["member"], mesh.shape["space"]

    def step(*args):
        return local(members, spaces, *args)

    in_specs = (P("member", None, "space"), P(None, "space"), P(), P("space"))
    out_specs = (P(), P("member", None, "space"))
    return jax.shard_map(step, mesh=mesh, in_specs=in_specs, out_specs=out_specs, check_vma=False)
```

```python
import math

import jax
import jax.numpy as jnp
from jax import lax
from jax.experimental import pallas as pl
from jax.experimental.pallas import tpu as pltpu
from jax.sharding import PartitionSpec as P

BLOCK = 128
BANDS = 720
MESH = pl.DeviceIdType.MESH
ROWS = 4
NEAR = 8
PLANES = 2
CHUNKS = ((0, 6), (6, 7))


def kernel(
    members,
    spaces,
    ens,
    tgt,
    cw_hbm,
    lat_hbm,
    result,
    cw,
    lat,
    own,
    tgt_rows,
    sgn,
    scl,
    gat,
    sums,
    back,
    area,
    met_area,
    box_row,
    box_a1,
    box_a2,
    box_l1,
    box_l2,
    box_l3,
    local_sem,
    row_sem,
    send1,
    recv1,
    send2,
    recv2,
    send_a1,
    recv_a1,
    send_a2,
    recv_a2,
    send_l1,
    recv_l1,
    send_l2,
    recv_l2,
    send_l3,
    recv_l3,
):
    m = lax.axis_index("member")
    s = lax.axis_index("space")
    far = spaces // NEAR
    ny = members // PLANES
    nz = far * PLANES
    near_at = lax.rem(s, NEAR)
    far_at = lax.div(s, NEAR)
    y = lax.div(m, PLANES)
    z = lax.rem(m, PLANES) * far + far_at
    units = ens.shape[0]
    per = units // members
    channels = tgt.shape[0]
    groups = units // channels
    blocks = groups * ROWS

    def member_of(yy, zz):
        return lax.rem(yy + ny, ny) * PLANES + lax.div(lax.rem(zz + nz, nz), far)

    def place(yy, zz):
        return (member_of(yy, zz), lax.rem(lax.rem(zz + nz, nz), far) * NEAR + near_at)

    def near_peer(k):
        return (m, s - near_at + lax.rem(near_at + k, NEAR))

    def far_peer(k):
        return (m, lax.rem(far_at + k, far) * NEAR + near_at)

    def z_peer(k):
        return place(y, z + k)

    def y_peer(k):
        return place(y + k, z)

    quarter = nz // 4

    def met(n):
        pair, turn = lax.div(n, 4), lax.rem(n, 4)
        dy = ny // 2 - pair + lax.rem(turn, 2) * (2 * pair - ny + 1)
        dz = quarter * (1 - 2 * lax.rem(lax.div(turn + 1, 2), 2))
        return place(y + dy, z + dz)

    barrier = pltpu.get_barrier_semaphore()

    def greet(peer):
        pl.semaphore_signal(barrier, inc=1, device_id=peer, device_id_type=MESH)

    def greet_all(peer, start, count):
        def one(k, carry):
            greet(peer(k))
            return carry

        lax.fori_loop(start, count, one, 0)

    greet_all(met, 0, members)
    greet_all(near_peer, 1, NEAR)
    greet_all(z_peer, 1, nz)
    greet_all(y_peer, 1, ny)
    own_copy = pltpu.make_async_copy(ens, own, local_sem.at[0])
    tgt_copy = pltpu.make_async_copy(tgt, tgt_rows, local_sem.at[1])
    cw_copy = pltpu.make_async_copy(cw_hbm, cw, local_sem.at[2])
    lat_copy = pltpu.make_async_copy(lat_hbm, lat, local_sem.at[3])
    lat_copy.start()
    cw_copy.start()
    own_copy.start()
    tgt_copy.start()

    pl.semaphore_wait(barrier, members + (NEAR - 1) + (nz - 1) + (ny - 1))

    def push(src, dst, send, recv, device):
        pltpu.make_async_remote_copy(
            src_ref=src,
            dst_ref=dst,
            send_sem=send,
            recv_sem=recv,
            device_id=device,
            device_id_type=MESH,
        ).start()

    def exchange(source, landing, send, recv, chunk):
        def one(n, carry):
            device = met(n)
            j = device[0]
            push(source(j), landing(m), send.at[chunk, j], recv.at[chunk, m], device)
            return carry

        lax.fori_loop(0, members, one, 0)

    def arrived(ref, sem):
        pltpu.make_async_copy(ref, ref, sem).wait()

    def share(box, at, send, recv, peer, count):
        def one(k, carry):
            push(box.at[at], box.at[at], send.at[k], recv.at[at], peer(k))
            return carry

        lax.fori_loop(1, count, one, 0)

    def sent(box, send, count):
        def one(k, carry):
            arrived(box.at[0], send.at[k])
            return carry

        lax.fori_loop(1, count, one, 0)

    def collect(box, at, recv, count):
        def one(k, carry):
            j = lax.rem(at + k, count)
            arrived(box.at[j], recv.at[j])
            return carry

        lax.fori_loop(1, count, one, 0)
        total = box[0]
        for j in range(1, count):
            total = total + box[j]
        return total

    for chunk, (first, size) in enumerate(CHUNKS):
        exchange(
            lambda j: ens.at[pl.ds(j * per + first, size)],
            lambda i: gat.at[i, pl.ds(first, size)],
            send1,
            recv1,
            chunk,
        )

    def along_rows(row):
        square = jnp.broadcast_to(row, (blocks, blocks))
        diagonal = lax.broadcasted_iota(jnp.int32, (blocks, blocks), 0) == lax.broadcasted_iota(
            jnp.int32, (blocks, blocks), 1
        )
        column = jnp.sum(jnp.where(diagonal, square, 0.0), axis=1, keepdims=True)
        return jnp.broadcast_to(column, (blocks, BLOCK))

    lat_copy.wait()
    latitude = ((lat[...].astype(jnp.float32) + 0.5) / BANDS - 0.5) * math.pi
    block_area = jnp.cos(latitude)
    box_row[0] = block_area
    push(box_row.at[0], box_row.at[1], row_sem.at[0], row_sem.at[1], place(y, z + quarter))
    wide = along_rows(block_area)
    for g in range(groups):
        area[g] = wide[g * ROWS : (g + 1) * ROWS]
    box_a1[near_at] = jnp.sum(wide, axis=0, keepdims=True)
    share(box_a1, near_at, send_a1, recv_a1, near_peer, NEAR)

    cw_copy.wait()
    own_copy.wait()
    tgt_copy.wait()

    def skill_rows(first, rows, acc):
        def group(g, acc):
            tiles = [
                tgt_rows[
                    pl.ds(first, rows), pl.ds(pl.multiple_of((g * ROWS + i) * BLOCK, BLOCK), BLOCK)
                ]
                for i in range(ROWS)
            ]
            part = jnp.zeros((ROWS, BLOCK), jnp.float32)
            for r in range(rows):
                u = (first + r) * groups + g
                skill = own[u] - jnp.concatenate([tile[r : r + 1] for tile in tiles], axis=0)
                sgn[u] = jnp.clip(skill * 64.0, -1.0, 1.0) * 0.0625
                part = part + cw[first + r] * jnp.abs(skill)
            return acc + area[g] * part

        return lax.fori_loop(0, groups, group, acc)

    def skill_octet(k, acc):
        return skill_rows(pl.multiple_of(k * 8, 8), 8, acc)

    octets = channels // 8
    skill_sum = lax.fori_loop(0, octets, skill_octet, jnp.zeros((ROWS, BLOCK), jnp.float32))
    if channels % 8:
        skill_sum = skill_rows(octets * 8, channels % 8, skill_sum)

    arrived(box_row.at[1], row_sem.at[1])
    met_wide = along_rows(box_row[1])
    for g in range(groups):
        met_area[g] = met_wide[g * ROWS : (g + 1) * ROWS]
    count = float(members)

    def pairs(k, acc):
        last = jnp.minimum(2 * k + 1, per - 1)
        counted = jnp.where(2 * k + 1 < per, 1.0, 0.0)
        values = [
            jnp.concatenate([gat[j, 2 * k], gat[j, last]], axis=0) * 64.0 for j in range(members)
        ]
        signs = [jnp.zeros_like(values[0]) for j in range(members)]
        for a in range(members):
            for b in range(a + 1, members):
                d = jnp.clip(values[a] - values[b], -1.0, 1.0)
                signs[a] = signs[a] + d
                signs[b] = signs[b] - d
        dot = values[0] * signs[0]
        for j in range(1, members):
            dot = dot + values[j] * signs[j]
        for i, part, factor in ((2 * k, slice(0, ROWS), 1.0), (last, slice(ROWS, 2 * ROWS), counted)):
            for j in range(members):
                sums[j, i] = signs[j][part]
            u = m * per + i
            acc = acc + (met_area[lax.rem(u, groups)] * (cw[lax.div(u, groups)] * factor)) * dot[part]
        return acc

    def wait_chunk(chunk):
        first, size = CHUNKS[chunk]

        def one(j, carry):
            arrived(gat.at[j, pl.ds(first, size)], recv1.at[chunk, j])
            return carry

        lax.fori_loop(0, members, one, 0)

    def send_back(chunk):
        first, size = CHUNKS[chunk]
        exchange(
            lambda j: sums.at[j, pl.ds(first, size)],
            lambda i: back.at[pl.ds(i * per + first, size)],
            send2,
            recv2,
            chunk,
        )

    middle = CHUNKS[1][0] // 2

    def chunk_step(chunk, acc):
        @pl.when(chunk == 0)
        def _():
            wait_chunk(0)

        @pl.when(chunk == 1)
        def _():
            send_back(0)
            area_near = collect(box_a1, near_at, recv_a1, NEAR)
            box_a2[far_at] = area_near
            share(box_a2, far_at, send_a2, recv_a2, far_peer, far)
            wait_chunk(1)

        return lax.fori_loop(chunk * middle, middle + chunk * ((per + 1) // 2 - middle), pairs, acc)

    spread_sum = lax.fori_loop(0, len(CHUNKS), chunk_step, jnp.zeros((ROWS, BLOCK), jnp.float32))
    send_back(1)
    mine = skill_sum * (1.0 / count) - spread_sum * (1.0 / (64.0 * count * (count - 1.0)))
    box_l1[near_at] = jnp.sum(mine, axis=0, keepdims=True)
    share(box_l1, near_at, send_l1, recv_l1, near_peer, NEAR)

    loss_near = collect(box_l1, near_at, recv_l1, NEAR)
    box_l2[z] = loss_near
    share(box_l2, z, send_l2, recv_l2, z_peer, nz)
    loss_z = collect(box_l2, z, recv_l2, nz)
    box_l3[y] = loss_z
    share(box_l3, y, send_l3, recv_l3, y_peer, ny)

    area_all = collect(box_a2, far_at, recv_a2, far)
    area_total = jnp.sum(area_all, axis=1, keepdims=True)
    points = float(units * ROWS * BLOCK // channels * spaces)
    factor = jnp.broadcast_to(points / area_total, (ROWS, BLOCK))

    def scale_channel(c, carry):
        weight = cw[c]
        for g in range(groups):
            u = c * groups + g
            scale = area[g] * factor * weight
            sgn[u] = sgn[u] * scale
            scl[u] = scale * (1.0 / (count * (count - 1.0)))
        return carry

    lax.fori_loop(0, channels, scale_channel, 0)

    def finish(j, source, first, size):
        part = pl.ds(j * per + first, size)
        result[part] = sgn[part] - scl[part] * source


    for chunk, (first, size) in enumerate(CHUNKS):

        def take_back(n, carry):
            j = met(n)[0]
            part = back.at[pl.ds(j * per + first, size)]
            arrived(part, recv2.at[chunk, j])
            finish(j, part[...], first, size)
            return carry

        lax.fori_loop(0, members, take_back, 0)

    loss_all = collect(box_l3, y, recv_l3, ny)
    loss_total = jnp.sum(loss_all, axis=1, keepdims=True)
    result[units] = jnp.broadcast_to(loss_total / (area_total * float(channels)), (ROWS, BLOCK))

    for chunk, (first, size) in enumerate(CHUNKS):

        def wait_sent(j, carry):
            arrived(gat.at[j, pl.ds(first, size)], send1.at[chunk, j])
            arrived(sums.at[j, pl.ds(first, size)], send2.at[chunk, j])
            return carry

        lax.fori_loop(0, members, wait_sent, 0)
    arrived(box_row.at[0], row_sem.at[0])
    sent(box_a1, send_a1, NEAR)
    sent(box_a2, send_a2, far)
    sent(box_l1, send_l1, NEAR)
    sent(box_l2, send_l2, nz)
    sent(box_l3, send_l3, ny)


def deliver(result, grad, loss, last, sem):
    grad_copy = pltpu.make_async_copy(result.at[pl.ds(0, grad.shape[0])], grad, sem.at[0])
    grad_copy.start()
    last[...] = result[grad.shape[0], 0:1, 0:1]
    loss_copy = pltpu.make_async_copy(last, loss, sem.at[1])
    loss_copy.start()
    loss_copy.wait()
    grad_copy.wait()


def local(members, spaces, ensemble, target, chan_weight, lat_band):
    channels, points = target.shape
    units = channels * points // (ROWS * BLOCK)
    per = units // members
    far = spaces // NEAR
    ny = members // PLANES
    nz = far * PLANES
    f32 = jnp.float32
    dma = pltpu.SemaphoreType.DMA
    vmem = pl.BlockSpec(memory_space=pltpu.VMEM)
    hbm = pl.BlockSpec(memory_space=pltpu.HBM)
    whole = pltpu.VMEM((units, ROWS, BLOCK), f32)
    slabs = pltpu.VMEM((members, per, ROWS, BLOCK), f32)

    def box(n):
        return pltpu.VMEM((n, 1, BLOCK), f32)

    def in_hbm(x):
        return pltpu.with_memory_space_constraint(x, pltpu.HBM)

    def body(*refs):
        kernel(members, spaces, *refs)

    result = pl.pallas_call(
        body,
        out_shape=jax.ShapeDtypeStruct((units + 1, ROWS, BLOCK), f32),
        in_specs=[hbm] * 4,
        out_specs=vmem,
        scratch_shapes=[
            pltpu.SMEM(chan_weight.shape, f32),
            pltpu.VMEM((1, lat_band.shape[0]), lat_band.dtype),
            whole,
            pltpu.VMEM((channels, points), f32),
            whole,
            whole,
            slabs,
            slabs,
            whole,
            pltpu.VMEM((points // (ROWS * BLOCK), ROWS, BLOCK), f32),
            pltpu.VMEM((points // (ROWS * BLOCK), ROWS, BLOCK), f32),
            pltpu.VMEM((2, 1, lat_band.shape[0]), f32),
            box(NEAR),
            box(far),
            box(NEAR),
            box(nz),
            box(ny),
            dma((4,)),
            dma((2,)),
            dma((len(CHUNKS), members)),
            dma((len(CHUNKS), members)),
            dma((len(CHUNKS), members)),
            dma((len(CHUNKS), members)),
            dma((NEAR,)),
            dma((NEAR,)),
            dma((far,)),
            dma((far,)),
            dma((NEAR,)),
            dma((NEAR,)),
            dma((nz,)),
            dma((nz,)),
            dma((ny,)),
            dma((ny,)),
        ],
        compiler_params=pltpu.CompilerParams(
            collective_id=0, has_side_effects=True, vmem_limit_bytes=32 * 1024 * 1024
        ),
    )(
        in_hbm(ensemble.reshape(units, ROWS, BLOCK)),
        in_hbm(target),
        in_hbm(chan_weight),
        in_hbm(lat_band.reshape(1, -1)),
    )
    grad, loss = pl.pallas_call(
        deliver,
        out_shape=(
            jax.ShapeDtypeStruct((units, ROWS, BLOCK), f32),
            jax.ShapeDtypeStruct((1, 1), f32),
        ),
        in_specs=[vmem],
        out_specs=(hbm, hbm),
        scratch_shapes=[pltpu.VMEM((1, 1), f32), dma((2,))],
        compiler_params=pltpu.CompilerParams(vmem_limit_bytes=32 * 1024 * 1024),
    )(result)
    return loss.reshape(()), grad.reshape(1, channels, points)


def solution(mesh):
    members, spaces = mesh.shape["member"], mesh.shape["space"]

    def step(*args):
        return local(members, spaces, *args)

    in_specs = (P("member", None, "space"), P(None, "space"), P(), P("space"))
    out_specs = (P(), P("member", None, "space"))
    return jax.shard_map(step, mesh=mesh, in_specs=in_specs, out_specs=out_specs, check_vma=False)
```

```python
import math

import jax
import jax.numpy as jnp
from jax import lax
from jax.experimental import pallas as pl
from jax.experimental.pallas import tpu as pltpu
from jax.sharding import PartitionSpec as P

BLOCK = 128
BANDS = 720
MESH = pl.DeviceIdType.MESH
ROWS = 4
NEAR = 8
PLANES = 2
CHUNKS = ((0, 6), (6, 7))


def kernel(
    members,
    spaces,
    ens,
    tgt,
    cw_hbm,
    lat_hbm,
    result,
    cw,
    lat,
    own,
    tgt_rows,
    sgn,
    scl,
    gat,
    sums,
    back,
    area,
    met_area,
    box_row,
    box_a1,
    box_a2,
    box_l1,
    box_l2,
    box_l3,
    local_sem,
    row_sem,
    send1,
    recv1,
    send2,
    recv2,
    send_a1,
    recv_a1,
    send_a2,
    recv_a2,
    send_l1,
    recv_l1,
    send_l2,
    recv_l2,
    send_l3,
    recv_l3,
):
    m = lax.axis_index("member")
    s = lax.axis_index("space")
    far = spaces // NEAR
    ny = members // PLANES
    nz = far * PLANES
    near_at = lax.rem(s, NEAR)
    far_at = lax.div(s, NEAR)
    y = lax.div(m, PLANES)
    z = lax.rem(m, PLANES) * far + far_at
    units = ens.shape[0]
    per = units // members
    channels = tgt.shape[0]
    groups = units // channels
    blocks = groups * ROWS

    def member_of(yy, zz):
        return lax.rem(yy + ny, ny) * PLANES + lax.div(lax.rem(zz + nz, nz), far)

    def place(yy, zz):
        return (member_of(yy, zz), lax.rem(lax.rem(zz + nz, nz), far) * NEAR + near_at)

    def near_peer(k):
        return (m, s - near_at + lax.rem(near_at + k, NEAR))

    def far_peer(k):
        return (m, lax.rem(far_at + k, far) * NEAR + near_at)

    def z_peer(k):
        return place(y, z + k)

    def y_peer(k):
        return place(y + k, z)

    quarter = nz // 4

    mirror = 1 - 2 * lax.rem(s, 2)

    def met(n):
        pair, turn = lax.div(n, 4), lax.rem(n, 4)
        dy = ny // 2 - pair + lax.rem(turn, 2) * (2 * pair - ny + 1)
        dz = quarter * (1 - 2 * lax.rem(lax.div(turn + 1, 2), 2))
        return place(y + mirror * dy, z + mirror * dz)

    barrier = pltpu.get_barrier_semaphore()

    def greet(peer):
        pl.semaphore_signal(barrier, inc=1, device_id=peer, device_id_type=MESH)

    def greet_all(peer, start, count):
        def one(k, carry):
            greet(peer(k))
            return carry

        lax.fori_loop(start, count, one, 0)

    greet_all(met, 0, members)
    greet_all(near_peer, 1, NEAR)
    greet_all(z_peer, 1, nz)
    greet_all(y_peer, 1, ny)
    own_copy = pltpu.make_async_copy(ens, own, local_sem.at[0])
    tgt_copy = pltpu.make_async_copy(tgt, tgt_rows, local_sem.at[1])
    cw_copy = pltpu.make_async_copy(cw_hbm, cw, local_sem.at[2])
    lat_copy = pltpu.make_async_copy(lat_hbm, lat, local_sem.at[3])
    lat_copy.start()
    cw_copy.start()
    own_copy.start()
    tgt_copy.start()

    pl.semaphore_wait(barrier, members + (NEAR - 1) + (nz - 1) + (ny - 1))

    def push(src, dst, send, recv, device):
        pltpu.make_async_remote_copy(
            src_ref=src,
            dst_ref=dst,
            send_sem=send,
            recv_sem=recv,
            device_id=device,
            device_id_type=MESH,
        ).start()

    def exchange(source, landing, send, recv, chunk):
        def one(n, carry):
            device = met(n)
            j = device[0]
            push(source(j), landing(m), send.at[chunk, j], recv.at[chunk, m], device)
            return carry

        lax.fori_loop(0, members, one, 0)

    def arrived(ref, sem):
        pltpu.make_async_copy(ref, ref, sem).wait()

    def share(box, at, send, recv, peer, count):
        def one(k, carry):
            push(box.at[at], box.at[at], send.at[k], recv.at[at], peer(k))
            return carry

        lax.fori_loop(1, count, one, 0)

    def collect(box, at, send, recv, count):
        def one(k, carry):
            j = lax.rem(at + k, count)
            pltpu.make_async_copy(box.at[j], box.at[j], recv.at[j]).wait()
            pltpu.make_async_copy(box.at[at], box.at[at], send.at[k]).wait()
            return carry

        lax.fori_loop(1, count, one, 0)
        total = box[0]
        for j in range(1, count):
            total = total + box[j]
        return total

    for chunk, (first, size) in enumerate(CHUNKS):
        exchange(
            lambda j: ens.at[pl.ds(j * per + first, size)],
            lambda i: gat.at[i, pl.ds(first, size)],
            send1,
            recv1,
            chunk,
        )

    def along_rows(row):
        square = jnp.broadcast_to(row, (blocks, blocks))
        diagonal = lax.broadcasted_iota(jnp.int32, (blocks, blocks), 0) == lax.broadcasted_iota(
            jnp.int32, (blocks, blocks), 1
        )
        column = jnp.sum(jnp.where(diagonal, square, 0.0), axis=1, keepdims=True)
        return jnp.broadcast_to(column, (blocks, BLOCK))

    lat_copy.wait()
    latitude = ((lat[...].astype(jnp.float32) + 0.5) / BANDS - 0.5) * math.pi
    block_area = jnp.cos(latitude)
    box_row[0] = block_area
    push(box_row.at[0], box_row.at[1], row_sem.at[0], row_sem.at[1], place(y, z + quarter))
    wide = along_rows(block_area)
    for g in range(groups):
        area[g] = wide[g * ROWS : (g + 1) * ROWS]
    box_a1[near_at] = jnp.sum(wide, axis=0, keepdims=True)
    share(box_a1, near_at, send_a1, recv_a1, near_peer, NEAR)

    cw_copy.wait()
    own_copy.wait()
    tgt_copy.wait()

    def skill_rows(first, rows, acc):
        def group(g, acc):
            tiles = [
                tgt_rows[
                    pl.ds(first, rows), pl.ds(pl.multiple_of((g * ROWS + i) * BLOCK, BLOCK), BLOCK)
                ]
                for i in range(ROWS)
            ]
            part = jnp.zeros((ROWS, BLOCK), jnp.float32)
            for r in range(rows):
                u = (first + r) * groups + g
                skill = own[u] - jnp.concatenate([tile[r : r + 1] for tile in tiles], axis=0)
                sgn[u] = jnp.clip(skill * 64.0, -1.0, 1.0) * 0.0625
                part = part + cw[first + r] * jnp.abs(skill)
            return acc + area[g] * part

        return lax.fori_loop(0, groups, group, acc)

    def skill_octet(k, acc):
        return skill_rows(pl.multiple_of(k * 8, 8), 8, acc)

    octets = channels // 8
    skill_sum = lax.fori_loop(0, octets, skill_octet, jnp.zeros((ROWS, BLOCK), jnp.float32))
    if channels % 8:
        skill_sum = skill_rows(octets * 8, channels % 8, skill_sum)

    arrived(box_row.at[1], row_sem.at[1])
    met_wide = along_rows(box_row[1])
    for g in range(groups):
        met_area[g] = met_wide[g * ROWS : (g + 1) * ROWS]
    count = float(members)

    def pairs(k, acc):
        last = jnp.minimum(2 * k + 1, per - 1)
        counted = jnp.where(2 * k + 1 < per, 1.0, 0.0)
        values = [
            jnp.concatenate([gat[j, 2 * k], gat[j, last]], axis=0) * 64.0 for j in range(members)
        ]
        signs = [jnp.zeros_like(values[0]) for j in range(members)]
        for a in range(members):
            for b in range(a + 1, members):
                d = jnp.clip(values[a] - values[b], -1.0, 1.0)
                signs[a] = signs[a] + d
                signs[b] = signs[b] - d
        dot = values[0] * signs[0]
        for j in range(1, members):
            dot = dot + values[j] * signs[j]
        for i, part, factor in ((2 * k, slice(0, ROWS), 1.0), (last, slice(ROWS, 2 * ROWS), counted)):
            for j in range(members):
                sums[j, i] = signs[j][part]
            u = m * per + i
            acc = acc + (met_area[lax.rem(u, groups)] * (cw[lax.div(u, groups)] * factor)) * dot[part]
        return acc

    def wait_chunk(chunk):
        first, size = CHUNKS[chunk]

        def one(j, carry):
            arrived(gat.at[j, pl.ds(first, size)], recv1.at[chunk, j])
            return carry

        lax.fori_loop(0, members, one, 0)

    def send_back(chunk):
        first, size = CHUNKS[chunk]
        exchange(
            lambda j: sums.at[j, pl.ds(first, size)],
            lambda i: back.at[pl.ds(i * per + first, size)],
            send2,
            recv2,
            chunk,
        )

    middle = CHUNKS[1][0] // 2

    def chunk_step(chunk, acc):
        @pl.when(chunk == 0)
        def _():
            wait_chunk(0)
            area_near = collect(box_a1, near_at, send_a1, recv_a1, NEAR)
            box_a2[far_at] = area_near
            share(box_a2, far_at, send_a2, recv_a2, far_peer, far)

        @pl.when(chunk == 1)
        def _():
            send_back(0)
            wait_chunk(1)

        return lax.fori_loop(chunk * middle, middle + chunk * ((per + 1) // 2 - middle), pairs, acc)

    spread_sum = lax.fori_loop(0, len(CHUNKS), chunk_step, jnp.zeros((ROWS, BLOCK), jnp.float32))
    mine = skill_sum * (1.0 / count) - spread_sum * (1.0 / (64.0 * count * (count - 1.0)))
    box_l1[near_at] = jnp.sum(mine, axis=0, keepdims=True)
    share(box_l1, near_at, send_l1, recv_l1, near_peer, NEAR)
    send_back(1)

    loss_near = collect(box_l1, near_at, send_l1, recv_l1, NEAR)
    box_l2[z] = loss_near
    share(box_l2, z, send_l2, recv_l2, z_peer, nz)
    loss_z = collect(box_l2, z, send_l2, recv_l2, nz)
    box_l3[y] = loss_z
    share(box_l3, y, send_l3, recv_l3, y_peer, ny)

    area_all = collect(box_a2, far_at, send_a2, recv_a2, far)
    area_total = jnp.sum(area_all, axis=1, keepdims=True)
    points = float(units * ROWS * BLOCK // channels * spaces)
    factor = jnp.broadcast_to(points / area_total, (ROWS, BLOCK))

    def scale_channel(c, carry):
        weight = cw[c]
        for g in range(groups):
            u = c * groups + g
            scale = area[g] * factor * weight
            sgn[u] = sgn[u] * scale
            scl[u] = scale * (1.0 / (count * (count - 1.0)))
        return carry

    lax.fori_loop(0, channels, scale_channel, 0)

    def finish(j, source, first, size):
        part = pl.ds(j * per + first, size)
        result[part] = sgn[part] - scl[part] * source


    for chunk, (first, size) in enumerate(CHUNKS):

        def take_back(n, carry):
            j = met(n)[0]
            part = back.at[pl.ds(j * per + first, size)]
            arrived(part, recv2.at[chunk, j])
            finish(j, part[...], first, size)
            return carry

        lax.fori_loop(0, members, take_back, 0)

    loss_all = collect(box_l3, y, send_l3, recv_l3, ny)
    loss_total = jnp.sum(loss_all, axis=1, keepdims=True)
    result[units] = jnp.broadcast_to(loss_total / (area_total * float(channels)), (ROWS, BLOCK))

    for chunk, (first, size) in enumerate(CHUNKS):

        def wait_sent(j, carry):
            arrived(gat.at[j, pl.ds(first, size)], send1.at[chunk, j])
            arrived(sums.at[j, pl.ds(first, size)], send2.at[chunk, j])
            return carry

        lax.fori_loop(0, members, wait_sent, 0)
    arrived(box_row.at[0], row_sem.at[0])


def deliver(result, grad, loss, last, sem):
    grad_copy = pltpu.make_async_copy(result.at[pl.ds(0, grad.shape[0])], grad, sem.at[0])
    grad_copy.start()
    last[...] = result[grad.shape[0], 0:1, 0:1]
    loss_copy = pltpu.make_async_copy(last, loss, sem.at[1])
    loss_copy.start()
    loss_copy.wait()
    grad_copy.wait()


def local(members, spaces, ensemble, target, chan_weight, lat_band):
    channels, points = target.shape
    units = channels * points // (ROWS * BLOCK)
    per = units // members
    far = spaces // NEAR
    ny = members // PLANES
    nz = far * PLANES
    f32 = jnp.float32
    dma = pltpu.SemaphoreType.DMA
    vmem = pl.BlockSpec(memory_space=pltpu.VMEM)
    hbm = pl.BlockSpec(memory_space=pltpu.HBM)
    whole = pltpu.VMEM((units, ROWS, BLOCK), f32)
    slabs = pltpu.VMEM((members, per, ROWS, BLOCK), f32)

    def box(n):
        return pltpu.VMEM((n, 1, BLOCK), f32)

    def in_hbm(x):
        return pltpu.with_memory_space_constraint(x, pltpu.HBM)

    def body(*refs):
        kernel(members, spaces, *refs)

    result = pl.pallas_call(
        body,
        out_shape=jax.ShapeDtypeStruct((units + 1, ROWS, BLOCK), f32),
        in_specs=[hbm] * 4,
        out_specs=vmem,
        scratch_shapes=[
            pltpu.SMEM(chan_weight.shape, f32),
            pltpu.VMEM((1, lat_band.shape[0]), lat_band.dtype),
            whole,
            pltpu.VMEM((channels, points), f32),
            whole,
            whole,
            slabs,
            slabs,
            whole,
            pltpu.VMEM((points // (ROWS * BLOCK), ROWS, BLOCK), f32),
            pltpu.VMEM((points // (ROWS * BLOCK), ROWS, BLOCK), f32),
            pltpu.VMEM((2, 1, lat_band.shape[0]), f32),
            box(NEAR),
            box(far),
            box(NEAR),
            box(nz),
            box(ny),
            dma((4,)),
            dma((2,)),
            dma((len(CHUNKS), members)),
            dma((len(CHUNKS), members)),
            dma((len(CHUNKS), members)),
            dma((len(CHUNKS), members)),
            dma((NEAR,)),
            dma((NEAR,)),
            dma((far,)),
            dma((far,)),
            dma((NEAR,)),
            dma((NEAR,)),
            dma((nz,)),
            dma((nz,)),
            dma((ny,)),
            dma((ny,)),
        ],
        compiler_params=pltpu.CompilerParams(
            collective_id=0, has_side_effects=True, vmem_limit_bytes=32 * 1024 * 1024
        ),
    )(
        in_hbm(ensemble.reshape(units, ROWS, BLOCK)),
        in_hbm(target),
        in_hbm(chan_weight),
        in_hbm(lat_band.reshape(1, -1)),
    )
    grad, loss = pl.pallas_call(
        deliver,
        out_shape=(
            jax.ShapeDtypeStruct((units, ROWS, BLOCK), f32),
            jax.ShapeDtypeStruct((1, 1), f32),
        ),
        in_specs=[vmem],
        out_specs=(hbm, hbm),
        scratch_shapes=[pltpu.VMEM((1, 1), f32), dma((2,))],
        compiler_params=pltpu.CompilerParams(vmem_limit_bytes=32 * 1024 * 1024),
    )(result)
    return loss.reshape(()), grad.reshape(1, channels, points)


def solution(mesh):
    members, spaces = mesh.shape["member"], mesh.shape["space"]

    def step(*args):
        return local(members, spaces, *args)

    in_specs = (P("member", None, "space"), P(None, "space"), P(), P("space"))
    out_specs = (P(), P("member", None, "space"))
    return jax.shard_map(step, mesh=mesh, in_specs=in_specs, out_specs=out_specs, check_vma=False)
```

```python
import math

import jax
import jax.numpy as jnp
from jax import lax
from jax.experimental import pallas as pl
from jax.experimental.pallas import tpu as pltpu
from jax.sharding import PartitionSpec as P

BLOCK = 128
BANDS = 720
MESH = pl.DeviceIdType.MESH
ROWS = 4
NEAR = 8
PLANES = 2
CHUNKS = ((0, 6), (6, 7))


def kernel(
    members,
    spaces,
    ens,
    tgt,
    cw_hbm,
    lat_hbm,
    result,
    cw,
    lat,
    own,
    tgt_rows,
    sgn,
    scl,
    gat,
    sums,
    back,
    area,
    met_area,
    box_row,
    box_a1,
    box_a2,
    box_l1,
    box_l2,
    box_l3,
    local_sem,
    row_sem,
    send1,
    recv1,
    send2,
    recv2,
    send_a1,
    recv_a1,
    send_a2,
    recv_a2,
    send_l1,
    recv_l1,
    send_l2,
    recv_l2,
    send_l3,
    recv_l3,
):
    m = lax.axis_index("member")
    s = lax.axis_index("space")
    far = spaces // NEAR
    ny = members // PLANES
    nz = far * PLANES
    near_at = lax.rem(s, NEAR)
    far_at = lax.div(s, NEAR)
    y = lax.div(m, PLANES)
    z = lax.rem(m, PLANES) * far + far_at
    units = ens.shape[0]
    per = units // members
    channels = tgt.shape[0]
    groups = units // channels
    blocks = groups * ROWS

    def member_of(yy, zz):
        return lax.rem(yy + ny, ny) * PLANES + lax.div(lax.rem(zz + nz, nz), far)

    def place(yy, zz):
        return (member_of(yy, zz), lax.rem(lax.rem(zz + nz, nz), far) * NEAR + near_at)

    def near_peer(k):
        return (m, s - near_at + lax.rem(near_at + k, NEAR))

    def far_peer(k):
        return (m, lax.rem(far_at + k, far) * NEAR + near_at)

    def z_peer(k):
        return place(y, z + k)

    def y_peer(k):
        return place(y + k, z)

    quarter = nz // 4

    up, down = place(0, z + quarter), place(0, z - quarter)

    def each_met(visit):
        def four(pair, carry):
            ahead = lax.rem(y + (ny + ny // 2) - pair, ny) * PLANES
            behind = lax.rem(y + (ny // 2 + 1) + pair, ny) * PLANES
            for along, plane in ((ahead, up), (behind, down), (ahead, down), (behind, up)):
                visit((along + plane[0], plane[1]))
            return carry

        lax.fori_loop(0, ny // 2, four, 0)

    barrier = pltpu.get_barrier_semaphore()

    def greet(peer):
        pl.semaphore_signal(barrier, inc=1, device_id=peer, device_id_type=MESH)

    def greet_all(peer, start, count):
        def one(k, carry):
            greet(peer(k))
            return carry

        lax.fori_loop(start, count, one, 0)

    each_met(greet)
    greet_all(near_peer, 1, NEAR)
    greet_all(z_peer, 1, nz)
    greet_all(y_peer, 1, ny)
    own_copy = pltpu.make_async_copy(ens, own, local_sem.at[0])
    tgt_copy = pltpu.make_async_copy(tgt, tgt_rows, local_sem.at[1])
    cw_copy = pltpu.make_async_copy(cw_hbm, cw, local_sem.at[2])
    lat_copy = pltpu.make_async_copy(lat_hbm, lat, local_sem.at[3])
    lat_copy.start()
    cw_copy.start()
    own_copy.start()
    tgt_copy.start()

    pl.semaphore_wait(barrier, members + (NEAR - 1) + (nz - 1) + (ny - 1))

    def push(src, dst, send, recv, device):
        pltpu.make_async_remote_copy(
            src_ref=src,
            dst_ref=dst,
            send_sem=send,
            recv_sem=recv,
            device_id=device,
            device_id_type=MESH,
        ).start()

    def exchange(source, landing, send, recv, chunk):
        def one(device):
            j = device[0]
            push(source(j), landing(m), send.at[chunk, j], recv.at[chunk, m], device)

        each_met(one)

    def arrived(ref, sem):
        pltpu.make_async_copy(ref, ref, sem).wait()

    def share(box, at, send, recv, peer, count):
        def one(k, carry):
            push(box.at[at], box.at[at], send.at[k], recv.at[at], peer(k))
            return carry

        lax.fori_loop(1, count, one, 0)

    def collect(box, at, send, recv, count):
        def one(k, carry):
            j = lax.rem(at + k, count)
            pltpu.make_async_copy(box.at[j], box.at[j], recv.at[j]).wait()
            pltpu.make_async_copy(box.at[at], box.at[at], send.at[k]).wait()
            return carry

        lax.fori_loop(1, count, one, 0)
        total = box[0]
        for j in range(1, count):
            total = total + box[j]
        return total

    for chunk, (first, size) in enumerate(CHUNKS):
        exchange(
            lambda j: ens.at[pl.ds(j * per + first, size)],
            lambda i: gat.at[i, pl.ds(first, size)],
            send1,
            recv1,
            chunk,
        )

    def along_rows(row):
        square = jnp.broadcast_to(row, (blocks, blocks))
        diagonal = lax.broadcasted_iota(jnp.int32, (blocks, blocks), 0) == lax.broadcasted_iota(
            jnp.int32, (blocks, blocks), 1
        )
        column = jnp.sum(jnp.where(diagonal, square, 0.0), axis=1, keepdims=True)
        return jnp.broadcast_to(column, (blocks, BLOCK))

    lat_copy.wait()
    latitude = ((lat[...].astype(jnp.float32) + 0.5) / BANDS - 0.5) * math.pi
    block_area = jnp.cos(latitude)
    box_row[0] = block_area
    push(box_row.at[0], box_row.at[1], row_sem.at[0], row_sem.at[1], place(y, z + quarter))
    wide = along_rows(block_area)
    for g in range(groups):
        area[g] = wide[g * ROWS : (g + 1) * ROWS]
    box_a1[near_at] = jnp.sum(wide, axis=0, keepdims=True)
    share(box_a1, near_at, send_a1, recv_a1, near_peer, NEAR)

    cw_copy.wait()
    own_copy.wait()
    tgt_copy.wait()

    def skill_rows(first, rows, acc):
        def group(g, acc):
            tiles = [
                tgt_rows[
                    pl.ds(first, rows), pl.ds(pl.multiple_of((g * ROWS + i) * BLOCK, BLOCK), BLOCK)
                ]
                for i in range(ROWS)
            ]
            part = jnp.zeros((ROWS, BLOCK), jnp.float32)
            for r in range(rows):
                u = (first + r) * groups + g
                skill = own[u] - jnp.concatenate([tile[r : r + 1] for tile in tiles], axis=0)
                sgn[u] = jnp.clip(skill * 64.0, -1.0, 1.0) * 0.0625
                part = part + cw[first + r] * jnp.abs(skill)
            return acc + area[g] * part

        return lax.fori_loop(0, groups, group, acc)

    def skill_octet(k, acc):
        return skill_rows(pl.multiple_of(k * 8, 8), 8, acc)

    octets = channels // 8
    skill_sum = lax.fori_loop(0, octets, skill_octet, jnp.zeros((ROWS, BLOCK), jnp.float32))
    if channels % 8:
        skill_sum = skill_rows(octets * 8, channels % 8, skill_sum)

    arrived(box_row.at[1], row_sem.at[1])
    met_wide = along_rows(box_row[1])
    for g in range(groups):
        met_area[g] = met_wide[g * ROWS : (g + 1) * ROWS]
    count = float(members)

    def pairs(k, acc):
        last = jnp.minimum(2 * k + 1, per - 1)
        counted = jnp.where(2 * k + 1 < per, 1.0, 0.0)
        values = [
            jnp.concatenate([gat[j, 2 * k], gat[j, last]], axis=0) * 64.0 for j in range(members)
        ]
        signs = [jnp.zeros_like(values[0]) for j in range(members)]
        for a in range(members):
            for b in range(a + 1, members):
                d = jnp.clip(values[a] - values[b], -1.0, 1.0)
                signs[a] = signs[a] + d
                signs[b] = signs[b] - d
        dot = values[0] * signs[0]
        for j in range(1, members):
            dot = dot + values[j] * signs[j]
        for i, part, factor in ((2 * k, slice(0, ROWS), 1.0), (last, slice(ROWS, 2 * ROWS), counted)):
            for j in range(members):
                sums[j, i] = signs[j][part]
            u = m * per + i
            acc = acc + (met_area[lax.rem(u, groups)] * (cw[lax.div(u, groups)] * factor)) * dot[part]
        return acc

    def wait_chunk(chunk):
        first, size = CHUNKS[chunk]

        def one(j, carry):
            arrived(gat.at[j, pl.ds(first, size)], recv1.at[chunk, j])
            return carry

        lax.fori_loop(0, members, one, 0)

    def send_back(chunk):
        first, size = CHUNKS[chunk]
        exchange(
            lambda j: sums.at[j, pl.ds(first, size)],
            lambda i: back.at[pl.ds(i * per + first, size)],
            send2,
            recv2,
            chunk,
        )

    middle = CHUNKS[1][0] // 2

    def chunk_step(chunk, acc):
        @pl.when(chunk == 0)
        def _():
            wait_chunk(0)
            area_near = collect(box_a1, near_at, send_a1, recv_a1, NEAR)
            box_a2[far_at] = area_near
            share(box_a2, far_at, send_a2, recv_a2, far_peer, far)

        @pl.when(chunk == 1)
        def _():
            send_back(0)
            wait_chunk(1)

        return lax.fori_loop(chunk * middle, middle + chunk * ((per + 1) // 2 - middle), pairs, acc)

    spread_sum = lax.fori_loop(0, len(CHUNKS), chunk_step, jnp.zeros((ROWS, BLOCK), jnp.float32))
    mine = skill_sum * (1.0 / count) - spread_sum * (1.0 / (64.0 * count * (count - 1.0)))
    box_l1[near_at] = jnp.sum(mine, axis=0, keepdims=True)
    share(box_l1, near_at, send_l1, recv_l1, near_peer, NEAR)
    send_back(1)

    loss_near = collect(box_l1, near_at, send_l1, recv_l1, NEAR)
    box_l2[z] = loss_near
    share(box_l2, z, send_l2, recv_l2, z_peer, nz)
    loss_z = collect(box_l2, z, send_l2, recv_l2, nz)
    box_l3[y] = loss_z
    share(box_l3, y, send_l3, recv_l3, y_peer, ny)

    area_all = collect(box_a2, far_at, send_a2, recv_a2, far)
    area_total = jnp.sum(area_all, axis=1, keepdims=True)
    points = float(units * ROWS * BLOCK // channels * spaces)
    factor = jnp.broadcast_to(points / area_total, (ROWS, BLOCK))

    def scale_channel(c, carry):
        weight = cw[c]
        for g in range(groups):
            u = c * groups + g
            scale = area[g] * factor * weight
            sgn[u] = sgn[u] * scale
            scl[u] = scale * (1.0 / (count * (count - 1.0)))
        return carry

    lax.fori_loop(0, channels, scale_channel, 0)

    def finish(j, source, first, size):
        part = pl.ds(j * per + first, size)
        result[part] = sgn[part] - scl[part] * source


    for chunk, (first, size) in enumerate(CHUNKS):

        def take_back(j, carry):
            part = back.at[pl.ds(j * per + first, size)]
            arrived(part, recv2.at[chunk, j])
            finish(j, part[...], first, size)
            return carry

        lax.fori_loop(0, members, take_back, 0)

    loss_all = collect(box_l3, y, send_l3, recv_l3, ny)
    loss_total = jnp.sum(loss_all, axis=1, keepdims=True)
    result[units] = jnp.broadcast_to(loss_total / (area_total * float(channels)), (ROWS, BLOCK))

    for chunk, (first, size) in enumerate(CHUNKS):

        def wait_sent(j, carry):
            arrived(gat.at[j, pl.ds(first, size)], send1.at[chunk, j])
            arrived(sums.at[j, pl.ds(first, size)], send2.at[chunk, j])
            return carry

        lax.fori_loop(0, members, wait_sent, 0)
    arrived(box_row.at[0], row_sem.at[0])


def deliver(result, grad, loss, last, sem):
    grad_copy = pltpu.make_async_copy(result.at[pl.ds(0, grad.shape[0])], grad, sem.at[0])
    grad_copy.start()
    last[...] = result[grad.shape[0], 0:1, 0:1]
    loss_copy = pltpu.make_async_copy(last, loss, sem.at[1])
    loss_copy.start()
    loss_copy.wait()
    grad_copy.wait()


def local(members, spaces, ensemble, target, chan_weight, lat_band):
    channels, points = target.shape
    units = channels * points // (ROWS * BLOCK)
    per = units // members
    far = spaces // NEAR
    ny = members // PLANES
    nz = far * PLANES
    f32 = jnp.float32
    dma = pltpu.SemaphoreType.DMA
    vmem = pl.BlockSpec(memory_space=pltpu.VMEM)
    hbm = pl.BlockSpec(memory_space=pltpu.HBM)
    whole = pltpu.VMEM((units, ROWS, BLOCK), f32)
    slabs = pltpu.VMEM((members, per, ROWS, BLOCK), f32)

    def box(n):
        return pltpu.VMEM((n, 1, BLOCK), f32)

    def in_hbm(x):
        return pltpu.with_memory_space_constraint(x, pltpu.HBM)

    def body(*refs):
        kernel(members, spaces, *refs)

    result = pl.pallas_call(
        body,
        out_shape=jax.ShapeDtypeStruct((units + 1, ROWS, BLOCK), f32),
        in_specs=[hbm] * 4,
        out_specs=vmem,
        scratch_shapes=[
            pltpu.SMEM(chan_weight.shape, f32),
            pltpu.VMEM((1, lat_band.shape[0]), lat_band.dtype),
            whole,
            pltpu.VMEM((channels, points), f32),
            whole,
            whole,
            slabs,
            slabs,
            whole,
            pltpu.VMEM((points // (ROWS * BLOCK), ROWS, BLOCK), f32),
            pltpu.VMEM((points // (ROWS * BLOCK), ROWS, BLOCK), f32),
            pltpu.VMEM((2, 1, lat_band.shape[0]), f32),
            box(NEAR),
            box(far),
            box(NEAR),
            box(nz),
            box(ny),
            dma((4,)),
            dma((2,)),
            dma((len(CHUNKS), members)),
            dma((len(CHUNKS), members)),
            dma((len(CHUNKS), members)),
            dma((len(CHUNKS), members)),
            dma((NEAR,)),
            dma((NEAR,)),
            dma((far,)),
            dma((far,)),
            dma((NEAR,)),
            dma((NEAR,)),
            dma((nz,)),
            dma((nz,)),
            dma((ny,)),
            dma((ny,)),
        ],
        compiler_params=pltpu.CompilerParams(
            collective_id=0, has_side_effects=True, vmem_limit_bytes=32 * 1024 * 1024
        ),
    )(
        in_hbm(ensemble.reshape(units, ROWS, BLOCK)),
        in_hbm(target),
        in_hbm(chan_weight),
        in_hbm(lat_band.reshape(1, -1)),
    )
    grad, loss = pl.pallas_call(
        deliver,
        out_shape=(
            jax.ShapeDtypeStruct((units, ROWS, BLOCK), f32),
            jax.ShapeDtypeStruct((1, 1), f32),
        ),
        in_specs=[vmem],
        out_specs=(hbm, hbm),
        scratch_shapes=[pltpu.VMEM((1, 1), f32), dma((2,))],
        compiler_params=pltpu.CompilerParams(vmem_limit_bytes=32 * 1024 * 1024),
    )(result)
    return loss.reshape(()), grad.reshape(1, channels, points)


def solution(mesh):
    members, spaces = mesh.shape["member"], mesh.shape["space"]

    def step(*args):
        return local(members, spaces, *args)

    in_specs = (P("member", None, "space"), P(None, "space"), P(), P("space"))
    out_specs = (P(), P("member", None, "space"))
    return jax.shard_map(step, mesh=mesh, in_specs=in_specs, out_specs=out_specs, check_vma=False)
```

```python
import math

import jax
import jax.numpy as jnp
from jax import lax
from jax.experimental import pallas as pl
from jax.experimental.pallas import tpu as pltpu
from jax.sharding import PartitionSpec as P

BLOCK = 128
BANDS = 720
MESH = pl.DeviceIdType.MESH
ROWS = 4
NEAR = 8
PLANES = 2
CHUNKS = ((0, 6), (6, 7))


def kernel(
    members,
    spaces,
    ens,
    tgt,
    cw_hbm,
    lat_hbm,
    result,
    cw,
    lat,
    own,
    tgt_rows,
    sgn,
    scl,
    gat,
    sums,
    back,
    area,
    met_area,
    box_row,
    box_a1,
    box_a2,
    box_l1,
    box_l2,
    box_l3,
    local_sem,
    row_sem,
    send1,
    recv1,
    send2,
    recv2,
    send_a1,
    recv_a1,
    send_a2,
    recv_a2,
    send_l1,
    recv_l1,
    send_l2,
    recv_l2,
    send_l3,
    recv_l3,
):
    m = lax.axis_index("member")
    s = lax.axis_index("space")
    far = spaces // NEAR
    ny = members // PLANES
    nz = far * PLANES
    near_at = lax.rem(s, NEAR)
    far_at = lax.div(s, NEAR)
    y = lax.div(m, PLANES)
    z = lax.rem(m, PLANES) * far + far_at
    units = ens.shape[0]
    per = units // members
    channels = tgt.shape[0]
    groups = units // channels
    blocks = groups * ROWS

    def member_of(yy, zz):
        return lax.rem(yy + ny, ny) * PLANES + lax.div(lax.rem(zz + nz, nz), far)

    def place(yy, zz):
        return (member_of(yy, zz), lax.rem(lax.rem(zz + nz, nz), far) * NEAR + near_at)

    def near_peer(k):
        return (m, s - near_at + lax.rem(near_at + k, NEAR))

    def far_peer(k):
        return (m, lax.rem(far_at + k, far) * NEAR + near_at)

    def z_peer(k):
        zz = lax.rem(z + k, nz)
        return (y * PLANES + lax.div(zz, far), lax.rem(zz, far) * NEAR + near_at)

    def y_peer(k):
        return (lax.rem(m + k * PLANES, members), s)

    quarter = nz // 4

    up, down = place(0, z + quarter), place(0, z - quarter)

    def each_met(visit):
        def four(pair, carry):
            ahead = lax.rem(y + (ny + ny // 2) - pair, ny) * PLANES
            behind = lax.rem(y + (ny // 2 + 1) + pair, ny) * PLANES
            for along, plane in ((ahead, up), (behind, down), (ahead, down), (behind, up)):
                visit((along + plane[0], plane[1]))
            return carry

        lax.fori_loop(0, ny // 2, four, 0)

    barrier = pltpu.get_barrier_semaphore()

    def greet(peer):
        pl.semaphore_signal(barrier, inc=1, device_id=peer, device_id_type=MESH)

    def greet_all(peer, start, count):
        def one(k, carry):
            greet(peer(k))
            return carry

        lax.fori_loop(start, count, one, 0)

    each_met(greet)
    greet_all(near_peer, 1, NEAR)
    greet_all(z_peer, 1, nz)
    greet_all(y_peer, 1, ny)
    own_copy = pltpu.make_async_copy(ens, own, local_sem.at[0])
    tgt_copy = pltpu.make_async_copy(tgt, tgt_rows, local_sem.at[1])
    cw_copy = pltpu.make_async_copy(cw_hbm, cw, local_sem.at[2])
    lat_copy = pltpu.make_async_copy(lat_hbm, lat, local_sem.at[3])
    lat_copy.start()
    cw_copy.start()
    own_copy.start()
    tgt_copy.start()

    pl.semaphore_wait(barrier, members + (NEAR - 1) + (nz - 1) + (ny - 1))

    def push(src, dst, send, recv, device):
        pltpu.make_async_remote_copy(
            src_ref=src,
            dst_ref=dst,
            send_sem=send,
            recv_sem=recv,
            device_id=device,
            device_id_type=MESH,
        ).start()

    def exchange(source, landing, send, recv, chunk):
        def one(device):
            j = device[0]
            push(source(j), landing(m), send.at[chunk, j], recv.at[chunk, m], device)

        each_met(one)

    def arrived(ref, sem):
        pltpu.make_async_copy(ref, ref, sem).wait()

    def share(box, at, send, recv, peer, count):
        def one(k, carry):
            push(box.at[at], box.at[at], send.at[k], recv.at[at], peer(k))
            return carry

        lax.fori_loop(1, count, one, 0)

    def collect(box, at, send, recv, count):
        def one(k, carry):
            j = lax.rem(at + k, count)
            pltpu.make_async_copy(box.at[j], box.at[j], recv.at[j]).wait()
            pltpu.make_async_copy(box.at[at], box.at[at], send.at[k]).wait()
            return carry

        lax.fori_loop(1, count, one, 0)
        total = box[0]
        for j in range(1, count):
            total = total + box[j]
        return total

    for chunk, (first, size) in enumerate(CHUNKS):
        exchange(
            lambda j: ens.at[pl.ds(j * per + first, size)],
            lambda i: gat.at[i, pl.ds(first, size)],
            send1,
            recv1,
            chunk,
        )

    def along_rows(row):
        square = jnp.broadcast_to(row, (blocks, blocks))
        diagonal = lax.broadcasted_iota(jnp.int32, (blocks, blocks), 0) == lax.broadcasted_iota(
            jnp.int32, (blocks, blocks), 1
        )
        column = jnp.sum(jnp.where(diagonal, square, 0.0), axis=1, keepdims=True)
        return jnp.broadcast_to(column, (blocks, BLOCK))

    lat_copy.wait()
    latitude = ((lat[...].astype(jnp.float32) + 0.5) / BANDS - 0.5) * math.pi
    block_area = jnp.cos(latitude)
    box_row[0] = block_area
    push(box_row.at[0], box_row.at[1], row_sem.at[0], row_sem.at[1], place(y, z + quarter))
    wide = along_rows(block_area)
    for g in range(groups):
        area[g] = wide[g * ROWS : (g + 1) * ROWS]
    box_a1[near_at] = jnp.sum(wide, axis=0, keepdims=True)
    share(box_a1, near_at, send_a1, recv_a1, near_peer, NEAR)

    cw_copy.wait()
    own_copy.wait()
    tgt_copy.wait()

    def skill_rows(first, rows, acc):
        def group(g, acc):
            tiles = [
                tgt_rows[
                    pl.ds(first, rows), pl.ds(pl.multiple_of((g * ROWS + i) * BLOCK, BLOCK), BLOCK)
                ]
                for i in range(ROWS)
            ]
            part = jnp.zeros((ROWS, BLOCK), jnp.float32)
            for r in range(rows):
                u = (first + r) * groups + g
                skill = own[u] - jnp.concatenate([tile[r : r + 1] for tile in tiles], axis=0)
                sgn[u] = jnp.clip(skill * 64.0, -1.0, 1.0) * 0.0625
                part = part + cw[first + r] * jnp.abs(skill)
            return acc + area[g] * part

        return lax.fori_loop(0, groups, group, acc)

    def skill_octet(k, acc):
        return skill_rows(pl.multiple_of(k * 8, 8), 8, acc)

    octets = channels // 8
    skill_sum = lax.fori_loop(0, octets, skill_octet, jnp.zeros((ROWS, BLOCK), jnp.float32))
    if channels % 8:
        skill_sum = skill_rows(octets * 8, channels % 8, skill_sum)

    arrived(box_row.at[1], row_sem.at[1])
    met_wide = along_rows(box_row[1])
    for g in range(groups):
        met_area[g] = met_wide[g * ROWS : (g + 1) * ROWS]
    count = float(members)

    def pairs(k, acc):
        last = jnp.minimum(2 * k + 1, per - 1)
        counted = jnp.where(2 * k + 1 < per, 1.0, 0.0)
        values = [
            jnp.concatenate([gat[j, 2 * k], gat[j, last]], axis=0) * 64.0 for j in range(members)
        ]
        signs = [jnp.zeros_like(values[0]) for j in range(members)]
        for a in range(members):
            for b in range(a + 1, members):
                d = jnp.clip(values[a] - values[b], -1.0, 1.0)
                signs[a] = signs[a] + d
                signs[b] = signs[b] - d
        dot = values[0] * signs[0]
        for j in range(1, members):
            dot = dot + values[j] * signs[j]
        for i, part, factor in ((2 * k, slice(0, ROWS), 1.0), (last, slice(ROWS, 2 * ROWS), counted)):
            for j in range(members):
                sums[j, i] = signs[j][part]
            u = m * per + i
            acc = acc + (met_area[lax.rem(u, groups)] * (cw[lax.div(u, groups)] * factor)) * dot[part]
        return acc

    def wait_chunk(chunk):
        first, size = CHUNKS[chunk]

        def one(j, carry):
            arrived(gat.at[j, pl.ds(first, size)], recv1.at[chunk, j])
            return carry

        lax.fori_loop(0, members, one, 0)

    def send_back(chunk):
        first, size = CHUNKS[chunk]
        exchange(
            lambda j: sums.at[j, pl.ds(first, size)],
            lambda i: back.at[pl.ds(i * per + first, size)],
            send2,
            recv2,
            chunk,
        )

    middle = CHUNKS[1][0] // 2

    def chunk_step(chunk, acc):
        @pl.when(chunk == 0)
        def _():
            wait_chunk(0)

        @pl.when(chunk == 1)
        def _():
            send_back(0)
            area_near = collect(box_a1, near_at, send_a1, recv_a1, NEAR)
            box_a2[far_at] = area_near
            share(box_a2, far_at, send_a2, recv_a2, far_peer, far)
            wait_chunk(1)

        return lax.fori_loop(chunk * middle, middle + chunk * ((per + 1) // 2 - middle), pairs, acc)

    spread_sum = lax.fori_loop(0, len(CHUNKS), chunk_step, jnp.zeros((ROWS, BLOCK), jnp.float32))
    mine = skill_sum * (1.0 / count) - spread_sum * (1.0 / (64.0 * count * (count - 1.0)))
    box_l1[near_at] = jnp.sum(mine, axis=0, keepdims=True)
    share(box_l1, near_at, send_l1, recv_l1, near_peer, NEAR)
    send_back(1)

    loss_near = collect(box_l1, near_at, send_l1, recv_l1, NEAR)
    box_l2[z] = loss_near
    share(box_l2, z, send_l2, recv_l2, z_peer, nz)
    loss_z = collect(box_l2, z, send_l2, recv_l2, nz)
    box_l3[y] = loss_z
    share(box_l3, y, send_l3, recv_l3, y_peer, ny)

    area_all = collect(box_a2, far_at, send_a2, recv_a2, far)
    area_total = jnp.sum(area_all, axis=1, keepdims=True)
    points = float(units * ROWS * BLOCK // channels * spaces)
    factor = jnp.broadcast_to(points / area_total, (ROWS, BLOCK))

    def scale_channel(c, carry):
        weight = cw[c]
        for g in range(groups):
            u = c * groups + g
            scale = area[g] * factor * weight
            sgn[u] = sgn[u] * scale
            scl[u] = scale * (1.0 / (count * (count - 1.0)))
        return carry

    lax.fori_loop(0, channels, scale_channel, 0)

    def finish(j, source, first, size):
        part = pl.ds(j * per + first, size)
        result[part] = sgn[part] - scl[part] * source


    for chunk, (first, size) in enumerate(CHUNKS):

        def take_back(j, carry):
            part = back.at[pl.ds(j * per + first, size)]
            arrived(part, recv2.at[chunk, j])
            finish(j, part[...], first, size)
            return carry

        lax.fori_loop(0, members, take_back, 0)

    loss_all = collect(box_l3, y, send_l3, recv_l3, ny)
    loss_total = jnp.sum(loss_all, axis=1, keepdims=True)
    result[units] = jnp.broadcast_to(loss_total / (area_total * float(channels)), (ROWS, BLOCK))

    for chunk, (first, size) in enumerate(CHUNKS):

        def wait_sent(j, carry):
            arrived(gat.at[j, pl.ds(first, size)], send1.at[chunk, j])
            arrived(sums.at[j, pl.ds(first, size)], send2.at[chunk, j])
            return carry

        lax.fori_loop(0, members, wait_sent, 0)
    arrived(box_row.at[0], row_sem.at[0])


def deliver(result, grad, loss, last, sem):
    grad_copy = pltpu.make_async_copy(result.at[pl.ds(0, grad.shape[0])], grad, sem.at[0])
    grad_copy.start()
    last[...] = result[grad.shape[0], 0:1, 0:1]
    loss_copy = pltpu.make_async_copy(last, loss, sem.at[1])
    loss_copy.start()
    loss_copy.wait()
    grad_copy.wait()


def local(members, spaces, ensemble, target, chan_weight, lat_band):
    channels, points = target.shape
    units = channels * points // (ROWS * BLOCK)
    per = units // members
    far = spaces // NEAR
    ny = members // PLANES
    nz = far * PLANES
    f32 = jnp.float32
    dma = pltpu.SemaphoreType.DMA
    vmem = pl.BlockSpec(memory_space=pltpu.VMEM)
    hbm = pl.BlockSpec(memory_space=pltpu.HBM)
    whole = pltpu.VMEM((units, ROWS, BLOCK), f32)
    slabs = pltpu.VMEM((members, per, ROWS, BLOCK), f32)

    def box(n):
        return pltpu.VMEM((n, 1, BLOCK), f32)

    def in_hbm(x):
        return pltpu.with_memory_space_constraint(x, pltpu.HBM)

    def body(*refs):
        kernel(members, spaces, *refs)

    result = pl.pallas_call(
        body,
        out_shape=jax.ShapeDtypeStruct((units + 1, ROWS, BLOCK), f32),
        in_specs=[hbm] * 4,
        out_specs=vmem,
        scratch_shapes=[
            pltpu.SMEM(chan_weight.shape, f32),
            pltpu.VMEM((1, lat_band.shape[0]), lat_band.dtype),
            whole,
            pltpu.VMEM((channels, points), f32),
            whole,
            whole,
            slabs,
            slabs,
            whole,
            pltpu.VMEM((points // (ROWS * BLOCK), ROWS, BLOCK), f32),
            pltpu.VMEM((points // (ROWS * BLOCK), ROWS, BLOCK), f32),
            pltpu.VMEM((2, 1, lat_band.shape[0]), f32),
            box(NEAR),
            box(far),
            box(NEAR),
            box(nz),
            box(ny),
            dma((4,)),
            dma((2,)),
            dma((len(CHUNKS), members)),
            dma((len(CHUNKS), members)),
            dma((len(CHUNKS), members)),
            dma((len(CHUNKS), members)),
            dma((NEAR,)),
            dma((NEAR,)),
            dma((far,)),
            dma((far,)),
            dma((NEAR,)),
            dma((NEAR,)),
            dma((nz,)),
            dma((nz,)),
            dma((ny,)),
            dma((ny,)),
        ],
        compiler_params=pltpu.CompilerParams(
            collective_id=0, has_side_effects=True, vmem_limit_bytes=32 * 1024 * 1024
        ),
    )(
        in_hbm(ensemble.reshape(units, ROWS, BLOCK)),
        in_hbm(target),
        in_hbm(chan_weight),
        in_hbm(lat_band.reshape(1, -1)),
    )
    grad, loss = pl.pallas_call(
        deliver,
        out_shape=(
            jax.ShapeDtypeStruct((units, ROWS, BLOCK), f32),
            jax.ShapeDtypeStruct((1, 1), f32),
        ),
        in_specs=[vmem],
        out_specs=(hbm, hbm),
        scratch_shapes=[pltpu.VMEM((1, 1), f32), dma((2,))],
        compiler_params=pltpu.CompilerParams(vmem_limit_bytes=32 * 1024 * 1024),
    )(result)
    return loss.reshape(()), grad.reshape(1, channels, points)


def solution(mesh):
    members, spaces = mesh.shape["member"], mesh.shape["space"]

    def step(*args):
        return local(members, spaces, *args)

    in_specs = (P("member", None, "space"), P(None, "space"), P(), P("space"))
    out_specs = (P(), P("member", None, "space"))
    return jax.shard_map(step, mesh=mesh, in_specs=in_specs, out_specs=out_specs, check_vma=False)
```

```python
import math

import jax
import jax.numpy as jnp
from jax import lax
from jax.experimental import pallas as pl
from jax.experimental.pallas import tpu as pltpu
from jax.sharding import PartitionSpec as P

BLOCK = 128
BANDS = 720
MESH = pl.DeviceIdType.MESH
ROWS = 4
NEAR = 8
PLANES = 2
CHUNKS = ((0, 6), (6, 7))


def kernel(
    members,
    spaces,
    ens,
    tgt,
    cw_hbm,
    lat_hbm,
    result,
    cw,
    lat,
    own,
    tgt_rows,
    sgn,
    scl,
    gat,
    sums,
    back,
    area,
    met_area,
    box_row,
    box_a1,
    box_a2,
    box_l1,
    box_l2,
    box_l3,
    local_sem,
    row_sem,
    send1,
    recv1,
    send2,
    recv2,
    send_a1,
    recv_a1,
    send_a2,
    recv_a2,
    send_l1,
    recv_l1,
    send_l2,
    recv_l2,
    send_l3,
    recv_l3,
):
    m = lax.axis_index("member")
    s = lax.axis_index("space")
    far = spaces // NEAR
    ny = members // PLANES
    nz = far * PLANES
    near_at = lax.rem(s, NEAR)
    far_at = lax.div(s, NEAR)
    y = lax.div(m, PLANES)
    z = lax.rem(m, PLANES) * far + far_at
    units = ens.shape[0]
    per = units // members
    channels = tgt.shape[0]
    groups = units // channels
    blocks = groups * ROWS

    def member_of(yy, zz):
        return lax.rem(yy + ny, ny) * PLANES + lax.div(lax.rem(zz + nz, nz), far)

    def place(yy, zz):
        return (member_of(yy, zz), lax.rem(lax.rem(zz + nz, nz), far) * NEAR + near_at)

    def near_peer(k):
        return (m, s - near_at + lax.rem(near_at + k, NEAR))

    def far_peer(k):
        return (m, lax.rem(far_at + k, far) * NEAR + near_at)

    def z_peer(k):
        return place(y, z + k)

    def y_peer(k):
        return place(y + k, z)

    quarter = nz // 4

    up, down = place(0, z + quarter), place(0, z - quarter)

    def each_met(visit, start=0, stop=ny // 2):
        def four(pair, carry):
            ahead = lax.rem(y + (ny + ny // 2) - pair, ny) * PLANES
            behind = lax.rem(y + (ny // 2 + 1) + pair, ny) * PLANES
            for along, plane in ((ahead, up), (behind, down), (ahead, down), (behind, up)):
                visit((along + plane[0], plane[1]))
            return carry

        lax.fori_loop(start, stop, four, 0)

    barrier = pltpu.get_barrier_semaphore()

    def greet(peer):
        pl.semaphore_signal(barrier, inc=1, device_id=peer, device_id_type=MESH)

    def greet_all(peer, start, count):
        def one(k, carry):
            greet(peer(k))
            return carry

        lax.fori_loop(start, count, one, 0)

    each_met(greet)
    greet_all(near_peer, 1, NEAR)
    greet_all(z_peer, 1, nz)
    greet_all(y_peer, 1, ny)
    own_copy = pltpu.make_async_copy(ens, own, local_sem.at[0])
    tgt_copy = pltpu.make_async_copy(tgt, tgt_rows, local_sem.at[1])
    cw_copy = pltpu.make_async_copy(cw_hbm, cw, local_sem.at[2])
    lat_copy = pltpu.make_async_copy(lat_hbm, lat, local_sem.at[3])
    lat_copy.start()
    cw_copy.start()
    own_copy.start()
    tgt_copy.start()

    pl.semaphore_wait(barrier, members + (NEAR - 1) + (nz - 1) + (ny - 1))

    def push(src, dst, send, recv, device):
        pltpu.make_async_remote_copy(
            src_ref=src,
            dst_ref=dst,
            send_sem=send,
            recv_sem=recv,
            device_id=device,
            device_id_type=MESH,
        ).start()

    def exchange(source, landing, send, recv, chunk, *span):
        def one(device):
            j = device[0]
            push(source(j), landing(m), send.at[chunk, j], recv.at[chunk, m], device)

        each_met(one, *span)

    def arrived(ref, sem):
        pltpu.make_async_copy(ref, ref, sem).wait()

    def share(box, at, send, recv, peer, count):
        def one(k, carry):
            push(box.at[at], box.at[at], send.at[k], recv.at[at], peer(k))
            return carry

        lax.fori_loop(1, count, one, 0)

    def collect(box, at, send, recv, count):
        def one(k, carry):
            j = lax.rem(at + k, count)
            pltpu.make_async_copy(box.at[j], box.at[j], recv.at[j]).wait()
            pltpu.make_async_copy(box.at[at], box.at[at], send.at[k]).wait()
            return carry

        lax.fori_loop(1, count, one, 0)
        total = box[0]
        for j in range(1, count):
            total = total + box[j]
        return total

    for chunk, (first, size) in enumerate(CHUNKS):
        exchange(
            lambda j: ens.at[pl.ds(j * per + first, size)],
            lambda i: gat.at[i, pl.ds(first, size)],
            send1,
            recv1,
            chunk,
        )

    def along_rows(row):
        square = jnp.broadcast_to(row, (blocks, blocks))
        diagonal = lax.broadcasted_iota(jnp.int32, (blocks, blocks), 0) == lax.broadcasted_iota(
            jnp.int32, (blocks, blocks), 1
        )
        column = jnp.sum(jnp.where(diagonal, square, 0.0), axis=1, keepdims=True)
        return jnp.broadcast_to(column, (blocks, BLOCK))

    lat_copy.wait()
    latitude = ((lat[...].astype(jnp.float32) + 0.5) / BANDS - 0.5) * math.pi
    block_area = jnp.cos(latitude)
    box_row[0] = block_area
    push(box_row.at[0], box_row.at[1], row_sem.at[0], row_sem.at[1], place(y, z + quarter))
    wide = along_rows(block_area)
    for g in range(groups):
        area[g] = wide[g * ROWS : (g + 1) * ROWS]
    box_a1[near_at] = jnp.sum(wide, axis=0, keepdims=True)
    share(box_a1, near_at, send_a1, recv_a1, near_peer, NEAR)

    cw_copy.wait()
    own_copy.wait()
    tgt_copy.wait()

    def skill_rows(first, rows, acc):
        def group(g, acc):
            tiles = [
                tgt_rows[
                    pl.ds(first, rows), pl.ds(pl.multiple_of((g * ROWS + i) * BLOCK, BLOCK), BLOCK)
                ]
                for i in range(ROWS)
            ]
            part = jnp.zeros((ROWS, BLOCK), jnp.float32)
            for r in range(rows):
                u = (first + r) * groups + g
                skill = own[u] - jnp.concatenate([tile[r : r + 1] for tile in tiles], axis=0)
                sgn[u] = jnp.clip(skill * 64.0, -1.0, 1.0) * 0.0625
                part = part + cw[first + r] * jnp.abs(skill)
            return acc + area[g] * part

        return lax.fori_loop(0, groups, group, acc)

    def skill_octet(k, acc):
        return skill_rows(pl.multiple_of(k * 8, 8), 8, acc)

    octets = channels // 8
    skill_sum = lax.fori_loop(0, octets, skill_octet, jnp.zeros((ROWS, BLOCK), jnp.float32))
    if channels % 8:
        skill_sum = skill_rows(octets * 8, channels % 8, skill_sum)

    arrived(box_row.at[1], row_sem.at[1])
    met_wide = along_rows(box_row[1])
    for g in range(groups):
        met_area[g] = met_wide[g * ROWS : (g + 1) * ROWS]
    count = float(members)

    def pairs(k, acc):
        last = jnp.minimum(2 * k + 1, per - 1)
        counted = jnp.where(2 * k + 1 < per, 1.0, 0.0)
        values = [
            jnp.concatenate([gat[j, 2 * k], gat[j, last]], axis=0) * 64.0 for j in range(members)
        ]
        signs = [jnp.zeros_like(values[0]) for j in range(members)]
        for a in range(members):
            for b in range(a + 1, members):
                d = jnp.clip(values[a] - values[b], -1.0, 1.0)
                signs[a] = signs[a] + d
                signs[b] = signs[b] - d
        dot = values[0] * signs[0]
        for j in range(1, members):
            dot = dot + values[j] * signs[j]
        for i, part, factor in ((2 * k, slice(0, ROWS), 1.0), (last, slice(ROWS, 2 * ROWS), counted)):
            for j in range(members):
                sums[j, i] = signs[j][part]
            u = m * per + i
            acc = acc + (met_area[lax.rem(u, groups)] * (cw[lax.div(u, groups)] * factor)) * dot[part]
        return acc

    def wait_chunk(chunk):
        first, size = CHUNKS[chunk]

        def one(j, carry):
            arrived(gat.at[j, pl.ds(first, size)], recv1.at[chunk, j])
            return carry

        lax.fori_loop(0, members, one, 0)

    def send_back(chunk, *span):
        first, size = CHUNKS[chunk]
        exchange(
            lambda j: sums.at[j, pl.ds(first, size)],
            lambda i: back.at[pl.ds(i * per + first, size)],
            send2,
            recv2,
            chunk,
            *span,
        )

    middle = CHUNKS[1][0] // 2

    def chunk_step(chunk, acc):
        @pl.when(chunk == 0)
        def _():
            wait_chunk(0)
            area_near = collect(box_a1, near_at, send_a1, recv_a1, NEAR)
            box_a2[far_at] = area_near
            share(box_a2, far_at, send_a2, recv_a2, far_peer, far)

        @pl.when(chunk == 1)
        def _():
            send_back(0)
            wait_chunk(1)

        return lax.fori_loop(chunk * middle, middle + chunk * ((per + 1) // 2 - middle), pairs, acc)

    spread_sum = lax.fori_loop(0, len(CHUNKS), chunk_step, jnp.zeros((ROWS, BLOCK), jnp.float32))
    send_back(1, 0, ny // 4)
    mine = skill_sum * (1.0 / count) - spread_sum * (1.0 / (64.0 * count * (count - 1.0)))
    box_l1[near_at] = jnp.sum(mine, axis=0, keepdims=True)
    share(box_l1, near_at, send_l1, recv_l1, near_peer, NEAR)
    send_back(1, ny // 4, ny // 2)

    loss_near = collect(box_l1, near_at, send_l1, recv_l1, NEAR)
    box_l2[z] = loss_near
    share(box_l2, z, send_l2, recv_l2, z_peer, nz)
    loss_z = collect(box_l2, z, send_l2, recv_l2, nz)
    box_l3[y] = loss_z
    share(box_l3, y, send_l3, recv_l3, y_peer, ny)

    area_all = collect(box_a2, far_at, send_a2, recv_a2, far)
    area_total = jnp.sum(area_all, axis=1, keepdims=True)
    points = float(units * ROWS * BLOCK // channels * spaces)
    factor = jnp.broadcast_to(points / area_total, (ROWS, BLOCK))

    def scale_channel(c, carry):
        weight = cw[c]
        for g in range(groups):
            u = c * groups + g
            scale = area[g] * factor * weight
            sgn[u] = sgn[u] * scale
            scl[u] = scale * (1.0 / (count * (count - 1.0)))
        return carry

    lax.fori_loop(0, channels, scale_channel, 0)

    def finish(j, source, first, size):
        part = pl.ds(j * per + first, size)
        result[part] = sgn[part] - scl[part] * source


    for chunk, (first, size) in enumerate(CHUNKS):

        def take_back(j, carry):
            part = back.at[pl.ds(j * per + first, size)]
            arrived(part, recv2.at[chunk, j])
            finish(j, part[...], first, size)
            return carry

        lax.fori_loop(0, members, take_back, 0)

    loss_all = collect(box_l3, y, send_l3, recv_l3, ny)
    loss_total = jnp.sum(loss_all, axis=1, keepdims=True)
    result[units] = jnp.broadcast_to(loss_total / (area_total * float(channels)), (ROWS, BLOCK))

    for chunk, (first, size) in enumerate(CHUNKS):

        def wait_sent(j, carry):
            arrived(gat.at[j, pl.ds(first, size)], send1.at[chunk, j])
            arrived(sums.at[j, pl.ds(first, size)], send2.at[chunk, j])
            return carry

        lax.fori_loop(0, members, wait_sent, 0)
    arrived(box_row.at[0], row_sem.at[0])


def deliver(result, grad, loss, last, sem):
    grad_copy = pltpu.make_async_copy(result.at[pl.ds(0, grad.shape[0])], grad, sem.at[0])
    grad_copy.start()
    last[...] = result[grad.shape[0], 0:1, 0:1]
    loss_copy = pltpu.make_async_copy(last, loss, sem.at[1])
    loss_copy.start()
    loss_copy.wait()
    grad_copy.wait()


def local(members, spaces, ensemble, target, chan_weight, lat_band):
    channels, points = target.shape
    units = channels * points // (ROWS * BLOCK)
    per = units // members
    far = spaces // NEAR
    ny = members // PLANES
    nz = far * PLANES
    f32 = jnp.float32
    dma = pltpu.SemaphoreType.DMA
    vmem = pl.BlockSpec(memory_space=pltpu.VMEM)
    hbm = pl.BlockSpec(memory_space=pltpu.HBM)
    whole = pltpu.VMEM((units, ROWS, BLOCK), f32)
    slabs = pltpu.VMEM((members, per, ROWS, BLOCK), f32)

    def box(n):
        return pltpu.VMEM((n, 1, BLOCK), f32)

    def in_hbm(x):
        return pltpu.with_memory_space_constraint(x, pltpu.HBM)

    def body(*refs):
        kernel(members, spaces, *refs)

    result = pl.pallas_call(
        body,
        out_shape=jax.ShapeDtypeStruct((units + 1, ROWS, BLOCK), f32),
        in_specs=[hbm] * 4,
        out_specs=vmem,
        scratch_shapes=[
            pltpu.SMEM(chan_weight.shape, f32),
            pltpu.VMEM((1, lat_band.shape[0]), lat_band.dtype),
            whole,
            pltpu.VMEM((channels, points), f32),
            whole,
            whole,
            slabs,
            slabs,
            whole,
            pltpu.VMEM((points // (ROWS * BLOCK), ROWS, BLOCK), f32),
            pltpu.VMEM((points // (ROWS * BLOCK), ROWS, BLOCK), f32),
            pltpu.VMEM((2, 1, lat_band.shape[0]), f32),
            box(NEAR),
            box(far),
            box(NEAR),
            box(nz),
            box(ny),
            dma((4,)),
            dma((2,)),
            dma((len(CHUNKS), members)),
            dma((len(CHUNKS), members)),
            dma((len(CHUNKS), members)),
            dma((len(CHUNKS), members)),
            dma((NEAR,)),
            dma((NEAR,)),
            dma((far,)),
            dma((far,)),
            dma((NEAR,)),
            dma((NEAR,)),
            dma((nz,)),
            dma((nz,)),
            dma((ny,)),
            dma((ny,)),
        ],
        compiler_params=pltpu.CompilerParams(
            collective_id=0, has_side_effects=True, vmem_limit_bytes=32 * 1024 * 1024
        ),
    )(
        in_hbm(ensemble.reshape(units, ROWS, BLOCK)),
        in_hbm(target),
        in_hbm(chan_weight),
        in_hbm(lat_band.reshape(1, -1)),
    )
    grad, loss = pl.pallas_call(
        deliver,
        out_shape=(
            jax.ShapeDtypeStruct((units, ROWS, BLOCK), f32),
            jax.ShapeDtypeStruct((1, 1), f32),
        ),
        in_specs=[vmem],
        out_specs=(hbm, hbm),
        scratch_shapes=[pltpu.VMEM((1, 1), f32), dma((2,))],
        compiler_params=pltpu.CompilerParams(vmem_limit_bytes=32 * 1024 * 1024),
    )(result)
    return loss.reshape(()), grad.reshape(1, channels, points)


def solution(mesh):
    members, spaces = mesh.shape["member"], mesh.shape["space"]

    def step(*args):
        return local(members, spaces, *args)

    in_specs = (P("member", None, "space"), P(None, "space"), P(), P("space"))
    out_specs = (P(), P("member", None, "space"))
    return jax.shard_map(step, mesh=mesh, in_specs=in_specs, out_specs=out_specs, check_vma=False)
```

```python
import math

import jax
import jax.numpy as jnp
from jax import lax
from jax.experimental import pallas as pl
from jax.experimental.pallas import tpu as pltpu
from jax.sharding import PartitionSpec as P

BLOCK = 128
BANDS = 720
MESH = pl.DeviceIdType.MESH
ROWS = 4
NEAR = 8
PLANES = 2
CHUNKS = ((0, 6), (6, 7))


def kernel(
    members,
    spaces,
    ens,
    tgt,
    cw_hbm,
    lat_hbm,
    result,
    cw,
    lat,
    own,
    tgt_rows,
    sgn,
    scl,
    gat,
    sums,
    back,
    area,
    met_area,
    box_row,
    box_a1,
    box_a2,
    box_l1,
    box_l2,
    box_l3,
    local_sem,
    row_sem,
    send1,
    recv1,
    send2,
    recv2,
    send_a1,
    recv_a1,
    send_a2,
    recv_a2,
    send_l1,
    recv_l1,
    send_l2,
    recv_l2,
    send_l3,
    recv_l3,
):
    m = lax.axis_index("member")
    s = lax.axis_index("space")
    far = spaces // NEAR
    ny = members // PLANES
    nz = far * PLANES
    near_at = lax.rem(s, NEAR)
    far_at = lax.div(s, NEAR)
    y = lax.div(m, PLANES)
    z = lax.rem(m, PLANES) * far + far_at
    units = ens.shape[0]
    per = units // members
    channels = tgt.shape[0]
    groups = units // channels
    blocks = groups * ROWS

    def member_of(yy, zz):
        return lax.rem(yy + ny, ny) * PLANES + lax.div(lax.rem(zz + nz, nz), far)

    def place(yy, zz):
        return (member_of(yy, zz), lax.rem(lax.rem(zz + nz, nz), far) * NEAR + near_at)

    def near_peer(k):
        return (m, s - near_at + lax.rem(near_at + k, NEAR))

    def far_peer(k):
        return (m, lax.rem(far_at + k, far) * NEAR + near_at)

    def z_peer(k):
        return place(y, z + k)

    def y_peer(k):
        return place(y + k, z)

    quarter = nz // 4

    up, down = place(0, z + quarter), place(0, z - quarter)

    def each_met(visit, start=0, stop=ny // 2):
        def four(pair, carry):
            ahead = lax.rem(y + (ny + ny // 2) - pair, ny) * PLANES
            behind = lax.rem(y + (ny // 2 + 1) + pair, ny) * PLANES
            for along, plane in ((ahead, up), (behind, down), (ahead, down), (behind, up)):
                visit((along + plane[0], plane[1]))
            return carry

        lax.fori_loop(start, stop, four, 0)

    barrier = pltpu.get_barrier_semaphore()

    def greet(peer):
        pl.semaphore_signal(barrier, inc=1, device_id=peer, device_id_type=MESH)

    def greet_all(peer, start, count):
        def one(k, carry):
            greet(peer(k))
            return carry

        lax.fori_loop(start, count, one, 0)

    each_met(greet)
    greet_all(near_peer, 1, NEAR)
    greet_all(z_peer, 1, nz)
    greet_all(y_peer, 1, ny)
    own_copy = pltpu.make_async_copy(ens, own, local_sem.at[0])
    tgt_copy = pltpu.make_async_copy(tgt, tgt_rows, local_sem.at[1])
    cw_copy = pltpu.make_async_copy(cw_hbm, cw, local_sem.at[2])
    lat_copy = pltpu.make_async_copy(lat_hbm, lat, local_sem.at[3])
    lat_copy.start()
    cw_copy.start()
    own_copy.start()
    tgt_copy.start()

    pl.semaphore_wait(barrier, members + (NEAR - 1) + (nz - 1) + (ny - 1))

    def push(src, dst, send, recv, device):
        pltpu.make_async_remote_copy(
            src_ref=src,
            dst_ref=dst,
            send_sem=send,
            recv_sem=recv,
            device_id=device,
            device_id_type=MESH,
        ).start()

    def exchange(source, landing, send, recv, chunk, *span):
        def one(device):
            j = device[0]
            push(source(j), landing(m), send.at[chunk, j], recv.at[chunk, m], device)

        each_met(one, *span)

    def arrived(ref, sem):
        pltpu.make_async_copy(ref, ref, sem).wait()

    def share(box, at, send, recv, peer, count):
        def one(k, carry):
            push(box.at[at], box.at[at], send.at[k], recv.at[at], peer(k))
            return carry

        lax.fori_loop(1, count, one, 0)

    def sent(box, send, count):
        def one(k, carry):
            arrived(box.at[0], send.at[k])
            return carry

        lax.fori_loop(1, count, one, 0)

    def collect(box, at, recv, count):
        def one(k, carry):
            j = lax.rem(at + k, count)
            arrived(box.at[j], recv.at[j])
            return carry

        lax.fori_loop(1, count, one, 0)
        total = box[0]
        for j in range(1, count):
            total = total + box[j]
        return total

    for chunk, (first, size) in enumerate(CHUNKS):
        exchange(
            lambda j: ens.at[pl.ds(j * per + first, size)],
            lambda i: gat.at[i, pl.ds(first, size)],
            send1,
            recv1,
            chunk,
        )

    def along_rows(row):
        square = jnp.broadcast_to(row, (blocks, blocks))
        diagonal = lax.broadcasted_iota(jnp.int32, (blocks, blocks), 0) == lax.broadcasted_iota(
            jnp.int32, (blocks, blocks), 1
        )
        column = jnp.sum(jnp.where(diagonal, square, 0.0), axis=1, keepdims=True)
        return jnp.broadcast_to(column, (blocks, BLOCK))

    lat_copy.wait()
    latitude = ((lat[...].astype(jnp.float32) + 0.5) / BANDS - 0.5) * math.pi
    block_area = jnp.cos(latitude)
    box_row[0] = block_area
    push(box_row.at[0], box_row.at[1], row_sem.at[0], row_sem.at[1], place(y, z + quarter))
    wide = along_rows(block_area)
    for g in range(groups):
        area[g] = wide[g * ROWS : (g + 1) * ROWS]
    box_a1[near_at] = jnp.sum(wide, axis=0, keepdims=True)
    share(box_a1, near_at, send_a1, recv_a1, near_peer, NEAR)

    cw_copy.wait()
    own_copy.wait()
    tgt_copy.wait()

    def skill_rows(first, rows, acc):
        def group(g, acc):
            tiles = [
                tgt_rows[
                    pl.ds(first, rows), pl.ds(pl.multiple_of((g * ROWS + i) * BLOCK, BLOCK), BLOCK)
                ]
                for i in range(ROWS)
            ]
            part = jnp.zeros((ROWS, BLOCK), jnp.float32)
            for r in range(rows):
                u = (first + r) * groups + g
                skill = own[u] - jnp.concatenate([tile[r : r + 1] for tile in tiles], axis=0)
                sgn[u] = jnp.clip(skill * 64.0, -1.0, 1.0) * 0.0625
                part = part + cw[first + r] * jnp.abs(skill)
            return acc + area[g] * part

        return lax.fori_loop(0, groups, group, acc)

    def skill_octet(k, acc):
        return skill_rows(pl.multiple_of(k * 8, 8), 8, acc)

    octets = channels // 8
    skill_sum = lax.fori_loop(0, octets, skill_octet, jnp.zeros((ROWS, BLOCK), jnp.float32))
    if channels % 8:
        skill_sum = skill_rows(octets * 8, channels % 8, skill_sum)

    arrived(box_row.at[1], row_sem.at[1])
    met_wide = along_rows(box_row[1])
    for g in range(groups):
        met_area[g] = met_wide[g * ROWS : (g + 1) * ROWS]
    count = float(members)

    def pairs(k, acc):
        last = jnp.minimum(2 * k + 1, per - 1)
        counted = jnp.where(2 * k + 1 < per, 1.0, 0.0)
        values = [
            jnp.concatenate([gat[j, 2 * k], gat[j, last]], axis=0) * 64.0 for j in range(members)
        ]
        signs = [jnp.zeros_like(values[0]) for j in range(members)]
        for a in range(members):
            for b in range(a + 1, members):
                d = jnp.clip(values[a] - values[b], -1.0, 1.0)
                signs[a] = signs[a] + d
                signs[b] = signs[b] - d
        dot = values[0] * signs[0]
        for j in range(1, members):
            dot = dot + values[j] * signs[j]
        for i, part, factor in ((2 * k, slice(0, ROWS), 1.0), (last, slice(ROWS, 2 * ROWS), counted)):
            for j in range(members):
                sums[j, i] = signs[j][part]
            u = m * per + i
            acc = acc + (met_area[lax.rem(u, groups)] * (cw[lax.div(u, groups)] * factor)) * dot[part]
        return acc

    def wait_chunk(chunk):
        first, size = CHUNKS[chunk]

        def one(j, carry):
            arrived(gat.at[j, pl.ds(first, size)], recv1.at[chunk, j])
            return carry

        lax.fori_loop(0, members, one, 0)

    def send_back(chunk, *span):
        first, size = CHUNKS[chunk]
        exchange(
            lambda j: sums.at[j, pl.ds(first, size)],
            lambda i: back.at[pl.ds(i * per + first, size)],
            send2,
            recv2,
            chunk,
            *span,
        )

    middle = CHUNKS[1][0] // 2

    def chunk_step(chunk, acc):
        @pl.when(chunk == 0)
        def _():
            wait_chunk(0)
            area_near = collect(box_a1, near_at, recv_a1, NEAR)
            box_a2[far_at] = area_near
            share(box_a2, far_at, send_a2, recv_a2, far_peer, far)

        @pl.when(chunk == 1)
        def _():
            send_back(0)
            wait_chunk(1)

        return lax.fori_loop(chunk * middle, middle + chunk * ((per + 1) // 2 - middle), pairs, acc)

    spread_sum = lax.fori_loop(0, len(CHUNKS), chunk_step, jnp.zeros((ROWS, BLOCK), jnp.float32))
    send_back(1, 0, ny // 4)
    mine = skill_sum * (1.0 / count) - spread_sum * (1.0 / (64.0 * count * (count - 1.0)))
    box_l1[near_at] = jnp.sum(mine, axis=0, keepdims=True)
    share(box_l1, near_at, send_l1, recv_l1, near_peer, NEAR)
    send_back(1, ny // 4, ny // 2)

    loss_near = collect(box_l1, near_at, recv_l1, NEAR)
    box_l2[z] = loss_near
    share(box_l2, z, send_l2, recv_l2, z_peer, nz)
    loss_z = collect(box_l2, z, recv_l2, nz)
    box_l3[y] = loss_z
    share(box_l3, y, send_l3, recv_l3, y_peer, ny)

    area_all = collect(box_a2, far_at, recv_a2, far)
    area_total = jnp.sum(area_all, axis=1, keepdims=True)
    points = float(units * ROWS * BLOCK // channels * spaces)
    factor = jnp.broadcast_to(points / area_total, (ROWS, BLOCK))

    def scale_channel(c, carry):
        weight = cw[c]
        for g in range(groups):
            u = c * groups + g
            scale = area[g] * factor * weight
            sgn[u] = sgn[u] * scale
            scl[u] = scale * (1.0 / (count * (count - 1.0)))
        return carry

    lax.fori_loop(0, channels, scale_channel, 0)

    def finish(j, source, first, size):
        part = pl.ds(j * per + first, size)
        result[part] = sgn[part] - scl[part] * source


    for chunk, (first, size) in enumerate(CHUNKS):

        def take_back(j, carry):
            part = back.at[pl.ds(j * per + first, size)]
            arrived(part, recv2.at[chunk, j])
            finish(j, part[...], first, size)
            return carry

        lax.fori_loop(0, members, take_back, 0)

    loss_all = collect(box_l3, y, recv_l3, ny)
    loss_total = jnp.sum(loss_all, axis=1, keepdims=True)
    result[units] = jnp.broadcast_to(loss_total / (area_total * float(channels)), (ROWS, BLOCK))

    for chunk, (first, size) in enumerate(CHUNKS):

        def wait_sent(j, carry):
            arrived(gat.at[j, pl.ds(first, size)], send1.at[chunk, j])
            arrived(sums.at[j, pl.ds(first, size)], send2.at[chunk, j])
            return carry

        lax.fori_loop(0, members, wait_sent, 0)
    arrived(box_row.at[0], row_sem.at[0])
    sent(box_a1, send_a1, NEAR)
    sent(box_a2, send_a2, far)
    sent(box_l1, send_l1, NEAR)
    sent(box_l2, send_l2, nz)
    sent(box_l3, send_l3, ny)


def deliver(result, grad, loss, last, sem):
    grad_copy = pltpu.make_async_copy(result.at[pl.ds(0, grad.shape[0])], grad, sem.at[0])
    grad_copy.start()
    last[...] = result[grad.shape[0], 0:1, 0:1]
    loss_copy = pltpu.make_async_copy(last, loss, sem.at[1])
    loss_copy.start()
    loss_copy.wait()
    grad_copy.wait()


def local(members, spaces, ensemble, target, chan_weight, lat_band):
    channels, points = target.shape
    units = channels * points // (ROWS * BLOCK)
    per = units // members
    far = spaces // NEAR
    ny = members // PLANES
    nz = far * PLANES
    f32 = jnp.float32
    dma = pltpu.SemaphoreType.DMA
    vmem = pl.BlockSpec(memory_space=pltpu.VMEM)
    hbm = pl.BlockSpec(memory_space=pltpu.HBM)
    whole = pltpu.VMEM((units, ROWS, BLOCK), f32)
    slabs = pltpu.VMEM((members, per, ROWS, BLOCK), f32)

    def box(n):
        return pltpu.VMEM((n, 1, BLOCK), f32)

    def in_hbm(x):
        return pltpu.with_memory_space_constraint(x, pltpu.HBM)

    def body(*refs):
        kernel(members, spaces, *refs)

    result = pl.pallas_call(
        body,
        out_shape=jax.ShapeDtypeStruct((units + 1, ROWS, BLOCK), f32),
        in_specs=[hbm] * 4,
        out_specs=vmem,
        scratch_shapes=[
            pltpu.SMEM(chan_weight.shape, f32),
            pltpu.VMEM((1, lat_band.shape[0]), lat_band.dtype),
            whole,
            pltpu.VMEM((channels, points), f32),
            whole,
            whole,
            slabs,
            slabs,
            whole,
            pltpu.VMEM((points // (ROWS * BLOCK), ROWS, BLOCK), f32),
            pltpu.VMEM((points // (ROWS * BLOCK), ROWS, BLOCK), f32),
            pltpu.VMEM((2, 1, lat_band.shape[0]), f32),
            box(NEAR),
            box(far),
            box(NEAR),
            box(nz),
            box(ny),
            dma((4,)),
            dma((2,)),
            dma((len(CHUNKS), members)),
            dma((len(CHUNKS), members)),
            dma((len(CHUNKS), members)),
            dma((len(CHUNKS), members)),
            dma((NEAR,)),
            dma((NEAR,)),
            dma((far,)),
            dma((far,)),
            dma((NEAR,)),
            dma((NEAR,)),
            dma((nz,)),
            dma((nz,)),
            dma((ny,)),
            dma((ny,)),
        ],
        compiler_params=pltpu.CompilerParams(
            collective_id=0, has_side_effects=True, vmem_limit_bytes=32 * 1024 * 1024
        ),
    )(
        in_hbm(ensemble.reshape(units, ROWS, BLOCK)),
        in_hbm(target),
        in_hbm(chan_weight),
        in_hbm(lat_band.reshape(1, -1)),
    )
    grad, loss = pl.pallas_call(
        deliver,
        out_shape=(
            jax.ShapeDtypeStruct((units, ROWS, BLOCK), f32),
            jax.ShapeDtypeStruct((1, 1), f32),
        ),
        in_specs=[vmem],
        out_specs=(hbm, hbm),
        scratch_shapes=[pltpu.VMEM((1, 1), f32), dma((2,))],
        compiler_params=pltpu.CompilerParams(vmem_limit_bytes=32 * 1024 * 1024),
    )(result)
    return loss.reshape(()), grad.reshape(1, channels, points)


def solution(mesh):
    members, spaces = mesh.shape["member"], mesh.shape["space"]

    def step(*args):
        return local(members, spaces, *args)

    in_specs = (P("member", None, "space"), P(None, "space"), P(), P("space"))
    out_specs = (P(), P("member", None, "space"))
    return jax.shard_map(step, mesh=mesh, in_specs=in_specs, out_specs=out_specs, check_vma=False)
```
